32 devices in a mesh: ctx: 8 (over y, x, core), fsdp: 4 (over z).
Axes of the slice: x: 2, y: 2, z: 4, core: 2. Of those that a mesh axis runs over, the one named last changes fastest.
Arguments:
- tokens: bfloat16 [2, 2048, 960], P(None, ('ctx', 'fsdp')), may hold values from -6 to 6
- doc_lengths: int32 [2, 4], replicated, may hold values from 1 to 1536, as said below
- block_table: int32 [32], replicated, may hold values from 0 to 31, each once
- attn_gain: bfloat16 [960], P('fsdp'), may hold values from 0.5 to 1.5
- w_query: bfloat16 [960, 960], P('fsdp'), may hold values from -0.1875 to 0.1875
- key_weight: bfloat16 [320, 960], P('fsdp'), may hold values from -0.1875 to 0.1875
- value_weight: bfloat16 [320, 960], P('fsdp'), may hold values from -0.1875 to 0.1875
- w_out: bfloat16 [960, 960], P('fsdp'), may hold values from -1.5 to 1.5
- mlp_gain: bfloat16 [960], P('fsdp'), may hold values from 0.5 to 1.5
- w_gate: bfloat16 [2560, 960], P('fsdp'), may hold values from -0.1875 to 0.1875
- w_up: bfloat16 [2560, 960], P('fsdp'), may hold values from -0.1875 to 0.1875
- w_down: bfloat16 [960, 2560], P('fsdp'), may hold values from -0.125 to 0.125
- out_cotangent: bfloat16 [2, 2048, 960], P(None, ('ctx', 'fsdp')), may hold values from -6 to 6
Outputs:
- layer_out: bfloat16 [2, 2048, 960], P(None, ('ctx', 'fsdp'))
- grad_tokens: bfloat16 [2, 2048, 960], P(None, ('ctx', 'fsdp'))
- grad_attn_gain: float32 [960], P('fsdp')
- grad_query: float32 [960, 960], P('fsdp')
- grad_key: float32 [320, 960], P('fsdp')
- grad_value: float32 [320, 960], P('fsdp')
- grad_out_proj: float32 [960, 960], P('fsdp')
- grad_mlp_gain: float32 [960], P('fsdp')
- grad_gate: float32 [2560, 960], P('fsdp')
- grad_up: float32 [2560, 960], P('fsdp')
- grad_down: float32 [960, 2560], P('fsdp')
The draws below stay inside these ranges and needn't reach their ends.
Inputs may be any that keep to these rules, and one draw needn't show every extreme that they name: Device d holds blocks block_table[d] and 63 - block_table[d] of every sequence; each value appears once. `doc_lengths`: each row sums to 2048; some row begins with a document of 1536 positions.
All inputs are finite; a program needn't handle non-finite values.
Results may differ from the reference program's by a relative error of at most 0.02.
Values may be sent and summed in bfloat16 or wider, within the bound.
No kernel may reach another device: no remote copies, remote signals or barrier semaphores. Data moves between devices by JAX's collectives and lax.ppermute only.
A program may use at most 448 MiB of HBM per device.

```python
import jax
import jax.numpy as jnp
from jax import lax

MODEL_DIMENSION = 960
QUERY_HEADS = 15
KEY_VALUE_HEADS = 5
HEAD_SIZE = 64
FF = 2560
SEQUENCE_COUNT = 2
BLK = 32
PAIRS = 32
SEQUENCE_TOKENS = 2048


def draw_doc_lengths(key, part):
    key = jax.random.fold_in(key, 11)
    subkeys = jax.random.split(key, 5)
    eighth = SEQUENCE_TOKENS // 8
    first_cut = jax.random.randint(subkeys[0], (SEQUENCE_COUNT,), eighth, 3 * eighth)
    second_cut = jax.random.randint(subkeys[1], (SEQUENCE_COUNT,), 3 * eighth, 5 * eighth)
    third_cut = jax.random.randint(subkeys[2], (SEQUENCE_COUNT,), 5 * eighth, 7 * eighth)
    regular = jnp.stack([first_cut, second_cut - first_cut, third_cut - second_cut, SEQUENCE_TOKENS - third_cut], axis=1)
    leading = 3 * SEQUENCE_TOKENS // 4
    middle = leading + jax.random.randint(subkeys[3], (), 1, SEQUENCE_TOKENS - leading - 1)
    special = jnp.stack([jnp.int32(leading), middle - leading, SEQUENCE_TOKENS - 1 - middle, jnp.int32(1)])
    chosen = jax.random.randint(subkeys[4], (), 0, SEQUENCE_COUNT)
    is_chosen = (jnp.arange(SEQUENCE_COUNT) == chosen)[:, None]
    return jnp.where(is_chosen, special[None, :], regular).astype(jnp.int32)


def block_levels(own_key, extent, shards, least, top_value):
    factor_of, own = 1.0, jax.random.fold_in(own_key, 6)
    for dim, blocks in shards:
        heights = jnp.exp(jax.random.uniform(jax.random.fold_in(own, dim), (blocks,), jnp.float32, least / len(shards), top_value / len(shards)))
        factor_of = factor_of * jnp.repeat(heights, extent[dim] // blocks).reshape([-1 if axis == dim else 1 for axis in range(len(extent))])
    return factor_of


def noise(own_key, shape, scale, limit, cuts=(), held_as=jnp.bfloat16):
    drawn = scale * jax.random.normal(own_key, shape, jnp.float32)
    if cuts:
        drawn = drawn * block_levels(own_key, shape, cuts, -0.22, 0.18)
    return jnp.clip(drawn, -limit, limit).astype(held_as)


def setup_inputs(seed: int = 0) -> dict:
    arg_keys = jax.random.split(jax.random.key(seed), 14)
    return {
        "tokens": noise(arg_keys[0], (SEQUENCE_COUNT, SEQUENCE_TOKENS, MODEL_DIMENSION), 1.0, 6.0, ((1, 32),)),
        "doc_lengths": draw_doc_lengths(jax.random.fold_in(arg_keys[13], 71), 0),
        "block_table": jax.random.permutation(arg_keys[2], PAIRS).astype(jnp.int32),
        "attn_gain": jnp.clip(1.0 + 0.1 * jax.random.normal(arg_keys[3], (MODEL_DIMENSION,), jnp.float32), 0.5, 1.5).astype(jnp.bfloat16),
        "w_query": noise(arg_keys[4], (QUERY_HEADS * HEAD_SIZE, MODEL_DIMENSION), MODEL_DIMENSION ** -0.5, 0.1875, ((0, 4),)),
        "key_weight": noise(arg_keys[5], (KEY_VALUE_HEADS * HEAD_SIZE, MODEL_DIMENSION), MODEL_DIMENSION ** -0.5, 0.1875, ((0, 4),)),
        "value_weight": noise(arg_keys[6], (KEY_VALUE_HEADS * HEAD_SIZE, MODEL_DIMENSION), MODEL_DIMENSION ** -0.5, 0.1875, ((0, 4),)),
        "w_out": noise(arg_keys[7], (MODEL_DIMENSION, QUERY_HEADS * HEAD_SIZE), (max(QUERY_HEADS * HEAD_SIZE // 64, 1)) ** -0.5, 1.5, ((0, 4),)),
        "mlp_gain": jnp.clip(1.0 + 0.1 * jax.random.normal(arg_keys[8], (MODEL_DIMENSION,), jnp.float32), 0.5, 1.5).astype(jnp.bfloat16),
        "w_gate": noise(arg_keys[9], (FF, MODEL_DIMENSION), MODEL_DIMENSION ** -0.5, 0.1875, ((0, 4),)),
        "w_up": noise(arg_keys[10], (FF, MODEL_DIMENSION), MODEL_DIMENSION ** -0.5, 0.1875, ((0, 4),)),
        "w_down": noise(arg_keys[11], (MODEL_DIMENSION, FF), FF ** -0.5, 0.125, ((0, 4),)),
        "out_cotangent": noise(arg_keys[12], (SEQUENCE_COUNT, SEQUENCE_TOKENS, MODEL_DIMENSION), 1.0, 6.0, ((1, 32),)),
    }


@jax.custom_vjp
def lower_precision(v):
    return lax.optimization_barrier(v.astype(jnp.bfloat16)).astype(jnp.float32)

@jax.custom_vjp
def lower_precision_back(v):
    return v

def low_keep(v):
    return (lower_precision(v), None)

def low_pass(kept, grad):
    return (grad,)

def back_keep(v):
    return (v, None)

def back_low(kept, grad):
    return (lower_precision(grad),)
lower_precision.defvjp(low_keep, low_pass)
lower_precision_back.defvjp(back_keep, back_low)
PRECISE = lax.Precision.HIGHEST
NEGATIVE = -1e+30
EPSILON = 1e-05
ROPE_BASE = 10000.0

def rope_tables(positions, head_dim):
    half_len = head_dim // 2
    frequency = ROPE_BASE ** (-(2.0 * jnp.arange(half_len, dtype=jnp.float32)) / head_dim)
    angles = positions.astype(jnp.float32)[:, None] * frequency[None, :]
    return (jnp.cos(angles), jnp.sin(angles))

def apply_rotary(value_matrix, cosine_table, sine_table):
    half_len = value_matrix.shape[-1] // 2
    first_half = value_matrix[..., :half_len]
    second_half = value_matrix[..., half_len:]
    cos_wide = cosine_table[None, :, None, :]
    sin_wide = sine_table[None, :, None, :]
    return jnp.concatenate([first_half * cos_wide - second_half * sin_wide, second_half * cos_wide + first_half * sin_wide], axis=-1)

def positions_of(table):
    pair_rows = 2 * BLK
    row_index = jnp.arange(SEQUENCE_TOKENS, dtype=jnp.int32)
    owners = row_index // pair_rows
    within = row_index % pair_rows
    paired = table[owners].astype(jnp.int32)
    blocks = jnp.where(within < BLK, paired, 2 * PAIRS - 1 - paired)
    return (blocks * BLK + within % BLK).astype(jnp.int32)

def apply_projection(inputs, weight):
    return jnp.einsum('sti,oi->sto', inputs, weight, precision=PRECISE)

def attend_block(query_tile_rows, query_pos, query_doc, key_matrix, value_matrix, key_pos, key_doc):
    row_count = query_tile_rows.shape[0]
    grouped_heads = query_tile_rows.reshape(row_count, KEY_VALUE_HEADS, QUERY_HEADS // KEY_VALUE_HEADS, HEAD_SIZE)
    scores = lower_precision_back(jnp.einsum('qgjd,kgd->gjqk', grouped_heads, key_matrix, precision=PRECISE) * HEAD_SIZE ** (-0.5))
    allowed = (key_pos[None, :] <= query_pos[:, None]) & (key_doc[None, :] == query_doc[:, None])
    scores = jnp.where(allowed[None, None], scores, NEGATIVE)
    row_max = lax.optimization_barrier(jnp.max(scores, axis=-1, keepdims=True))
    exp_scores = jnp.exp(scores - row_max)
    weights = lower_precision(exp_scores / lax.optimization_barrier(jnp.sum(exp_scores, axis=-1, keepdims=True)))
    mixed_heads = jnp.einsum('gjqk,kgd->qgjd', weights, value_matrix, precision=PRECISE)
    return mixed_heads.reshape(row_count, QUERY_HEADS, HEAD_SIZE)

def attend(queries, key_matrix, value_matrix, positions, doc_ids):
    block_rows = min(512, SEQUENCE_TOKENS)
    num_blocks = SEQUENCE_TOKENS // block_rows

    def one_sequence(seq_item):
        query_seq, key_seq, value_seq, doc_seq = seq_item

        def one_block(block_item):
            query_tile_rows, pos_block, doc_block = block_item
            return attend_block(query_tile_rows, pos_block, doc_block, key_seq, value_seq, positions, doc_seq)
        pieces = (query_seq.reshape(num_blocks, block_rows, QUERY_HEADS, HEAD_SIZE), positions.reshape(num_blocks, block_rows), doc_seq.reshape(num_blocks, block_rows))
        return lax.map(jax.checkpoint(one_block), pieces).reshape(SEQUENCE_TOKENS, QUERY_HEADS, HEAD_SIZE)
    return lax.map(one_sequence, (queries, key_matrix, value_matrix, doc_ids))

def layer_forward(inputs, gain_attn, w_query, key_weight, value_weight, w_out, gain_mlp, w_gate, w_up, w_down, positions, doc_ids, cosine_table, sine_table):
    normed_attn = inputs * lax.rsqrt(lax.optimization_barrier(jnp.mean(inputs * inputs, axis=-1, keepdims=True)) + EPSILON)
    attention_input = lower_precision(normed_attn * gain_attn)
    queries = lower_precision(apply_rotary(lower_precision_back(apply_projection(attention_input, w_query)).reshape(SEQUENCE_COUNT, SEQUENCE_TOKENS, QUERY_HEADS, HEAD_SIZE), cosine_table, sine_table))
    key_matrix = lower_precision(apply_rotary(lower_precision_back(apply_projection(attention_input, key_weight)).reshape(SEQUENCE_COUNT, SEQUENCE_TOKENS, KEY_VALUE_HEADS, HEAD_SIZE), cosine_table, sine_table))
    value_matrix = lower_precision(lower_precision_back(apply_projection(attention_input, value_weight))).reshape(SEQUENCE_COUNT, SEQUENCE_TOKENS, KEY_VALUE_HEADS, HEAD_SIZE)
    attended = attend(queries, key_matrix, value_matrix, positions, doc_ids).reshape(SEQUENCE_COUNT, SEQUENCE_TOKENS, QUERY_HEADS * HEAD_SIZE)
    mixed = lower_precision(lower_precision_back(attended))
    residual = inputs + lower_precision_back(apply_projection(mixed, w_out))
    normed_mlp = residual * lax.rsqrt(lax.optimization_barrier(jnp.mean(residual * residual, axis=-1, keepdims=True)) + EPSILON)
    mlp_in = lower_precision(normed_mlp * gain_mlp)
    gate_pre = lower_precision_back(apply_projection(mlp_in, w_gate))
    up_pre = lower_precision_back(apply_projection(mlp_in, w_up))
    hidden = lower_precision(gate_pre * jax.nn.sigmoid(gate_pre) * up_pre)
    return residual + lower_precision_back(apply_projection(hidden, w_down))

def reference(tokens, doc_lengths, block_table, attn_gain, w_query, key_weight, value_weight, w_out, mlp_gain, w_gate, w_up, w_down, out_cotangent):
    positions = positions_of(block_table)
    bounds = jnp.cumsum(doc_lengths, axis=1)
    doc_ids = lax.optimization_barrier(jnp.sum((positions[None, :, None] >= bounds[:, None, :-1]).astype(jnp.int32), axis=-1))
    cosine_table, sine_table = rope_tables(positions, HEAD_SIZE)

    def forward(inputs, gain_attn, wq, wk, wv, wo, gain_mlp, wg, wu, wd):
        return layer_forward(inputs, gain_attn, wq, wk, wv, wo, gain_mlp, wg, wu, wd, positions, doc_ids, cosine_table, sine_table)
    inputs = tuple((member.astype(jnp.float32) for member in (tokens, attn_gain, w_query, key_weight, value_weight, w_out, mlp_gain, w_gate, w_up, w_down)))
    result, pull_back = jax.vjp(forward, *inputs)
    gradients = pull_back(out_cotangent.astype(jnp.float32))
    return (result.astype(jnp.bfloat16), gradients[0].astype(jnp.bfloat16), gradients[1], gradients[2], gradients[3], gradients[4], gradients[5], gradients[6], gradients[7], gradients[8], gradients[9])
```

```python
import functools

import jax
import jax.numpy as jnp
from jax import lax
from jax.experimental import pallas as pl
from jax.experimental.pallas import tpu as pltpu
from jax.sharding import PartitionSpec as P

QUERY_HEADS = 15
KEY_VALUE_HEADS = 5
HEAD_SIZE = 64
GROUP = QUERY_HEADS // KEY_VALUE_HEADS
NEGATIVE = -1e30
EPSILON = 1e-05
ROPE_BASE = 10000.0
SCALE = HEAD_SIZE ** (-0.5)
BF16 = jnp.bfloat16
F32 = jnp.float32
VMEM_LIMIT = 56 * 1024 * 1024


def nt(a, b):
    return lax.dot_general(a, b, (((1,), (1,)), ((), ())), preferred_element_type=F32)


def nn(a, b):
    return lax.dot_general(a, b, (((1,), (0,)), ((), ())), preferred_element_type=F32)


def tn(a, b):
    return lax.dot_general(a, b, (((0,), (0,)), ((), ())), preferred_element_type=F32)


def project(x, w):
    return jnp.einsum("sri,oi->sro", x, w, preferred_element_type=F32)


def project_back(g, w):
    return jnp.einsum("sro,oi->sri", g, w, preferred_element_type=F32)


def weight_grad(g, x):
    return jnp.einsum("sro,sri->oi", g, x, preferred_element_type=F32)


def spread(pair, head, half):
    lane = lax.broadcasted_iota(jnp.int32, pair.shape, 1)
    here = (lane // HEAD_SIZE) == (head % 2)
    alone = jnp.where(here, pair, jnp.zeros_like(pair))
    return jnp.where(half == head % 2, alone, pltpu.roll(alone, HEAD_SIZE, 1))


def collect(first, second, half_first, half_second):
    lane = lax.broadcasted_iota(jnp.int32, first.shape, 1)
    low = jnp.where(half_first == 0, first, pltpu.roll(first, HEAD_SIZE, 1))
    high = jnp.where(half_second == 1, second, pltpu.roll(second, HEAD_SIZE, 1))
    return jnp.where(lane < HEAD_SIZE, low, high)


def forward_kernel(
    half_ref, q_ref, k_ref, v_ref, kpos_ref, qpos_ref, qstart_ref, o_ref, lse_ref, q4, bias, m, l, acc
):
    step, steps = pl.program_id(1), pl.num_programs(1)
    rows = q_ref.shape[1]
    heads = q4.shape[0] // rows
    chunk = 128

    @pl.when(step == 0)
    def _():
        for h in range(heads):
            pair = q_ref[0, :, pl.ds((h // 2) * 128, 128)].astype(F32) * SCALE
            q4[pl.ds(h * rows, rows), :] = spread(pair, h, half_ref[h]).astype(BF16)
        m[...] = jnp.full_like(m, NEGATIVE)
        l[...] = jnp.zeros_like(l)
        acc[...] = jnp.zeros_like(acc)

    kpos = kpos_ref[...]
    seen = (kpos <= qpos_ref[...]) & (kpos >= qstart_ref[0])
    bias[...] = jnp.where(seen, 0.0, NEGATIVE)
    keys, values = k_ref[0], v_ref[0]

    def one(i, _):
        at = pl.multiple_of(i * chunk, chunk)
        within = pl.multiple_of(lax.rem(at, rows), chunk)
        s = nt(q4[pl.ds(at, chunk), :], keys) + bias[pl.ds(within, chunk), :]
        old = m[pl.ds(at, chunk), :]
        new = jnp.maximum(old, jnp.max(s, axis=1, keepdims=True))
        p = jnp.exp(s - new)
        factor = jnp.exp(old - new)
        m[pl.ds(at, chunk), :] = new
        l[pl.ds(at, chunk), :] = l[pl.ds(at, chunk), :] * factor + jnp.sum(p, axis=1, keepdims=True)
        acc[pl.ds(at, chunk), :] = acc[pl.ds(at, chunk), :] * factor + nn(p.astype(BF16), values)
        return 0

    lax.fori_loop(0, heads * rows // chunk, one, 0)

    @pl.when(step == steps - 1)
    def _():
        total = l[...]
        lse = m[...] + jnp.log(total)
        for i in range(heads * rows // 128):
            part = jnp.broadcast_to(lse[i * 128 : (i + 1) * 128], (128, 128))
            lse_ref[0, :, pl.ds(i * 128, 128)] = part.T[0:1, :]
        out = acc[...] / total
        for h in range(0, heads, 2):
            both = collect(
                out[h * rows : (h + 1) * rows],
                out[(h + 1) * rows : (h + 2) * rows],
                half_ref[h],
                half_ref[h + 1],
            )
            o_ref[0, :, pl.ds((h // 2) * 128, 128)] = both.astype(BF16)


def backward_kernel(
    half_ref,
    q_ref,
    o_ref,
    do_ref,
    lse_ref,
    k_ref,
    v_ref,
    kpos_ref,
    qpos_ref,
    qstart_ref,
    cos_ref,
    sin_ref,
    dq_ref,
    dk_ref,
    dv_ref,
    q4,
    do4,
    delta,
    dq,
):
    step, steps = pl.program_id(1), pl.num_programs(1)
    rows = q_ref.shape[1]
    heads = q4.shape[0] // rows
    chunk = 256

    @pl.when(step == 0)
    def _():
        for h in range(heads):
            lanes = pl.ds((h // 2) * 128, 128)
            pair = q_ref[0, :, lanes].astype(F32) * SCALE
            q4[pl.ds(h * rows, rows), :] = spread(pair, h, half_ref[h]).astype(BF16)
            grad = do_ref[0, :, lanes].astype(F32)
            wide = spread(grad, h, half_ref[h])
            do4[pl.ds(h * rows, rows), :] = wide.astype(BF16)
            lane = lax.broadcasted_iota(jnp.int32, grad.shape, 1)
            mine = (lane // HEAD_SIZE) == (h % 2)
            both = jnp.where(mine, grad * o_ref[0, :, lanes].astype(F32), 0.0)
            total = jnp.sum(both, axis=1, keepdims=True)
            for i in range(rows // 128):
                part = jnp.broadcast_to(total[i * 128 : (i + 1) * 128], (128, 128))
                delta[:, pl.ds(h * rows + i * 128, 128)] = part.T[0:1, :]
        dq[...] = jnp.zeros_like(dq)

    lse = lse_ref[0]
    row_delta = delta[...]
    qpos, qstart = qpos_ref[...], qstart_ref[0]

    def one(i, _):
        at = pl.multiple_of(i * chunk, chunk)
        keys = k_ref[0, pl.ds(at, chunk), :]
        values = v_ref[0, pl.ds(at, chunk), :]
        kpos = kpos_ref[pl.ds(at, chunk), :]
        seen = (kpos <= qpos) & (kpos >= qstart)
        bias = jnp.where(seen, 0.0, NEGATIVE)
        bias = jnp.concatenate([bias] * heads, axis=1)
        p = jnp.exp(nt(keys, q4[...]) + bias - lse)
        dv_ref[0, pl.ds(at, chunk), :] = nn(p.astype(BF16), do4[...]).astype(dv_ref.dtype)
        ds = (p * (nt(values, do4[...]) - row_delta)).astype(BF16)
        dk_ref[0, pl.ds(at, chunk), :] = nn(ds, q4[...]).astype(dk_ref.dtype)
        dq[...] += tn(ds, keys)
        return 0

    lax.fori_loop(0, k_ref.shape[1] // chunk, one, 0)

    @pl.when(step == steps - 1)
    def _():
        cosine, sine = cos_ref[...], sin_ref[...]
        for h in range(0, heads, 2):
            both = collect(
                dq[pl.ds(h * rows, rows), :],
                dq[pl.ds((h + 1) * rows, rows), :],
                half_ref[h],
                half_ref[h + 1],
            )
            both = both * SCALE
            lane = lax.broadcasted_iota(jnp.int32, both.shape, 1)
            first = (lane % HEAD_SIZE) < HEAD_SIZE // 2
            swapped = jnp.where(
                first, pltpu.roll(both, 128 - HEAD_SIZE // 2, 1), pltpu.roll(both, HEAD_SIZE // 2, 1)
            )
            back = both * cosine - swapped * sine
            dq_ref[0, :, pl.ds((h // 2) * 128, 128)] = back.astype(BF16)


def key_step(count):
    return 2048 if count % 2048 == 0 else count


def attention_forward(half, queries, keys, values, key_pos, own_pos, own_start):
    seqs, rows, width = queries.shape
    count = keys.shape[1]
    step = key_step(count)
    heads = width // HEAD_SIZE
    smem = pl.BlockSpec(memory_space=pltpu.SMEM)
    return pl.pallas_call(
        forward_kernel,
        grid=(seqs, count // step),
        in_specs=[
            smem,
            pl.BlockSpec((1, rows, width), lambda s, b: (s, 0, 0)),
            pl.BlockSpec((1, step, 128), lambda s, b: (s, b, 0)),
            pl.BlockSpec((1, step, 128), lambda s, b: (s, b, 0)),
            pl.BlockSpec((1, step), lambda s, b: (0, b)),
            pl.BlockSpec((rows, 1), lambda s, b: (0, 0)),
            pl.BlockSpec((1, rows, 1), lambda s, b: (s, 0, 0)),
        ],
        out_specs=[
            pl.BlockSpec((1, rows, width), lambda s, b: (s, 0, 0)),
            pl.BlockSpec((1, 1, heads * rows), lambda s, b: (s, 0, 0)),
        ],
        out_shape=[
            jax.ShapeDtypeStruct((seqs, rows, width), BF16),
            jax.ShapeDtypeStruct((seqs, 1, heads * rows), F32),
        ],
        scratch_shapes=[
            pltpu.VMEM((heads * rows, 128), BF16),
            pltpu.VMEM((rows, step), F32),
            pltpu.VMEM((heads * rows, 1), F32),
            pltpu.VMEM((heads * rows, 1), F32),
            pltpu.VMEM((heads * rows, 128), F32),
        ],
        compiler_params=pltpu.CompilerParams(
            dimension_semantics=("arbitrary", "arbitrary"), vmem_limit_bytes=VMEM_LIMIT
        ),
        cost_estimate=pl.CostEstimate(
            flops=4 * seqs * heads * rows * count * 128,
            bytes_accessed=seqs * count * 512,
            transcendentals=seqs * heads * rows * count,
        ),
        name="attention_forward",
    )(half, queries, keys, values, key_pos[None, :], own_pos[:, None], own_start[:, :, None])


def attention_backward(
    half, queries, mixed, grads, lse, keys, values, key_pos, own_pos, own_start, cosine, sine
):
    seqs, rows, width = queries.shape
    count = keys.shape[1]
    step = key_step(count)
    heads = width // HEAD_SIZE
    smem = pl.BlockSpec(memory_space=pltpu.SMEM)
    own = pl.BlockSpec((1, rows, width), lambda s, b: (s, 0, 0))
    others = pl.BlockSpec((1, step, 128), lambda s, b: (s, b, 0))
    table = pl.BlockSpec((rows, 128), lambda s, b: (0, 0))
    return pl.pallas_call(
        backward_kernel,
        grid=(seqs, count // step),
        in_specs=[
            smem,
            own,
            own,
            own,
            pl.BlockSpec((1, 1, heads * rows), lambda s, b: (s, 0, 0)),
            others,
            others,
            pl.BlockSpec((step, 1), lambda s, b: (b, 0)),
            pl.BlockSpec((1, rows), lambda s, b: (0, 0)),
            pl.BlockSpec((1, 1, rows), lambda s, b: (s, 0, 0)),
            table,
            table,
        ],
        out_specs=[own, others, others],
        out_shape=[
            jax.ShapeDtypeStruct((seqs, rows, width), BF16),
            jax.ShapeDtypeStruct((seqs, count, 128), BF16),
            jax.ShapeDtypeStruct((seqs, count, 128), BF16),
        ],
        scratch_shapes=[
            pltpu.VMEM((heads * rows, 128), BF16),
            pltpu.VMEM((heads * rows, 128), BF16),
            pltpu.VMEM((1, heads * rows), F32),
            pltpu.VMEM((heads * rows, 128), F32),
        ],
        compiler_params=pltpu.CompilerParams(
            dimension_semantics=("arbitrary", "arbitrary"), vmem_limit_bytes=VMEM_LIMIT
        ),
        cost_estimate=pl.CostEstimate(
            flops=10 * seqs * heads * rows * count * 128,
            bytes_accessed=seqs * count * 1024,
            transcendentals=seqs * heads * rows * count,
        ),
        name="attention_backward",
    )(
        half,
        queries,
        mixed,
        grads,
        lse,
        keys,
        values,
        key_pos[:, None],
        own_pos[None, :],
        own_start[:, None, :],
        cosine,
        sine,
    )


def swap_halves(w):
    parts = w.reshape(-1, 2, HEAD_SIZE // 2, w.shape[-1])
    return jnp.concatenate([parts[:, 1:], parts[:, :1]], axis=1).reshape(w.shape)


def rows_from(arrays, start, count):
    return lax.dynamic_slice_in_dim(jnp.concatenate(arrays, axis=0), start, count, 0)


def local(
    tokens,
    doc_lengths,
    block_table,
    attn_gain,
    w_query,
    key_weight,
    value_weight,
    w_out,
    mlp_gain,
    w_gate,
    w_up,
    w_down,
    out_cotangent,
):
    nf, nc = lax.axis_size("fsdp"), lax.axis_size("ctx")
    z, c = lax.axis_index("fsdp"), lax.axis_index("ctx")
    seqs, piece, width = tokens.shape
    rows = nf * piece
    half_len = HEAD_SIZE // 2
    up = [(i, i + 1) for i in range(nf - 1)]
    down = [(i + 1, i) for i in range(nf - 1)]

    heads = -(-QUERY_HEADS // nf)
    q_rows, k_rows = w_query.shape[0], key_weight.shape[0]
    q_width, k_width = heads * HEAD_SIZE, 2 * HEAD_SIZE
    q_shift = q_width - q_rows
    k_shift = k_rows - HEAD_SIZE
    q_edge, k_edge = q_shift * (nf - 1), k_shift * (nf - 1)
    head_index = jnp.arange(heads, dtype=jnp.int32)
    half = jnp.minimum((z * heads + head_index) // GROUP - z, 1).astype(jnp.int32)

    x = lax.all_gather(tokens, "fsdp", axis=1, tiled=True).astype(F32)
    attn_gain_all = lax.all_gather(attn_gain, "fsdp", axis=0, tiled=True).astype(F32)
    mlp_gain_all = lax.all_gather(mlp_gain, "fsdp", axis=0, tiled=True).astype(F32)
    from_next = lax.ppermute(
        jnp.concatenate([w_query[:q_edge], key_weight[:k_edge], value_weight[:k_edge]], axis=0),
        "fsdp",
        down,
    )
    from_prev = lax.ppermute(
        jnp.concatenate([key_weight[k_rows - k_edge :], value_weight[k_rows - k_edge :]], axis=0),
        "fsdp",
        up,
    )
    zero_rows = jnp.zeros((q_width + q_edge - q_rows - q_edge, width), BF16)
    wq = rows_from([w_query, from_next[:q_edge], zero_rows], q_shift * z, q_width)
    k_start = k_edge - k_shift * z
    wk = rows_from(
        [from_prev[:k_edge], key_weight, from_next[q_edge : q_edge + k_edge]], k_start, k_width
    )
    wv = rows_from(
        [from_prev[k_edge:], value_weight, from_next[q_edge + k_edge :]], k_start, k_width
    )
    w_out_all = lax.all_gather(w_out, "fsdp", axis=0, tiled=True)
    cotangent = lax.all_gather(out_cotangent, "fsdp", axis=1, tiled=True)

    units = w_gate.shape[0]
    own_down = lax.dynamic_slice_in_dim(w_down, z * units, units, 1)
    pieces = [own_down]
    for shift in range(1, nf):
        piece_out = lax.dynamic_slice_in_dim(w_down, lax.rem(z + shift, nf) * units, units, 1)
        pieces.append(lax.ppermute(piece_out, "fsdp", [(i, (i + shift) % nf) for i in range(nf)]))
    stacked = jnp.stack(pieces)
    order = lax.rem(z - jnp.arange(nf, dtype=jnp.int32) + nf, nf)
    w_down_units = jnp.take(stacked, order, axis=0).reshape(width, units)

    table = block_table.astype(jnp.int32)
    block = piece // 2
    paired = jnp.stack([table, 2 * table.shape[0] - 1 - table], axis=1)
    positions = (paired[:, :, None] * block + jnp.arange(block, dtype=jnp.int32)).reshape(-1)
    key_pos = positions
    own_pos = lax.dynamic_slice_in_dim(positions, c * rows, rows, 0)
    bounds = jnp.cumsum(doc_lengths, axis=1)
    reached = own_pos[None, :, None] >= bounds[:, None, :-1]
    own_start = jnp.max(jnp.where(reached, bounds[:, None, :-1], 0), axis=-1)

    frequency = ROPE_BASE ** (-(2.0 * jnp.arange(half_len, dtype=F32)) / HEAD_SIZE)
    angles = own_pos.astype(F32)[:, None] * frequency[None, :]
    cos, sin = jnp.cos(angles), jnp.sin(angles)
    cosine = jnp.tile(jnp.concatenate([cos, cos], axis=1), (1, 2))
    sine = jnp.tile(jnp.concatenate([-sin, sin], axis=1), (1, 2))

    inv_attn = lax.rsqrt(jnp.mean(x * x, axis=-1, keepdims=True) + EPSILON)
    normed_attn = x * inv_attn
    attn_in = (normed_attn * attn_gain_all).astype(BF16)
    qk_width = q_width + k_width
    w_in = jnp.concatenate([wq, wk, wv, swap_halves(wq), swap_halves(wk)], axis=0)
    projected = project(attn_in, w_in)
    repeat = qk_width // 128
    turned = (
        projected[..., :qk_width] * jnp.tile(cosine, (1, repeat))
        + projected[..., qk_width + k_width :] * jnp.tile(sine, (1, repeat))
    ).astype(BF16)
    queries = turned[..., :q_width]
    own_kv = jnp.concatenate(
        [turned[..., q_width:], projected[..., qk_width : qk_width + k_width].astype(BF16)], axis=-1
    )
    all_kv = lax.all_gather(own_kv, "ctx", axis=1, tiled=True)
    keys, values = all_kv[..., :k_width], all_kv[..., k_width:]
    mixed_own, lse = attention_forward(half, queries, keys, values, key_pos, own_pos, own_start)
    mixed = lax.all_gather(mixed_own, "fsdp", axis=2, tiled=True)[..., : QUERY_HEADS * HEAD_SIZE]

    residual = x + project(mixed, w_out_all)
    inv_mlp = lax.rsqrt(jnp.mean(residual * residual, axis=-1, keepdims=True) + EPSILON)
    normed_mlp = residual * inv_mlp
    mlp_in = (normed_mlp * mlp_gain_all).astype(BF16)
    gate_pre = project(mlp_in, w_gate)
    up_pre = project(mlp_in, w_up)
    sigmoid_gate = jax.nn.sigmoid(gate_pre)
    silu_gate = gate_pre * sigmoid_gate
    hidden = (silu_gate * up_pre).astype(BF16)
    grad_hidden = project_back(cotangent, w_down_units)
    grad_gate_pre = (
        grad_hidden * up_pre * (sigmoid_gate + gate_pre * sigmoid_gate * (1.0 - sigmoid_gate))
    ).astype(BF16)
    grad_up_pre = (grad_hidden * silu_gate).astype(BF16)
    grad_mlp_part = project_back(grad_gate_pre, w_gate) + project_back(grad_up_pre, w_up)

    def own_rows(array):
        return lax.dynamic_slice_in_dim(array, z * piece, piece, 1)

    def exchange(part):
        cut = jnp.stack([part[:, i * piece : (i + 1) * piece] for i in range(nf)]).astype(BF16)
        swapped = lax.all_to_all(cut, "fsdp", 0, 0, tiled=True)
        return jnp.sum(swapped.astype(F32), axis=0)

    grad_mlp_in = exchange(grad_mlp_part)
    own_normed, own_inv = own_rows(normed_mlp), own_rows(inv_mlp)
    scaled = grad_mlp_in * mlp_gain_all
    grad_gain_mlp = jnp.sum(grad_mlp_in * own_normed, axis=(0, 1))
    grad_residual = out_cotangent.astype(F32) + own_inv * (
        scaled - own_normed * jnp.mean(scaled * own_normed, axis=-1, keepdims=True)
    )
    grad_attn_branch = lax.all_gather(grad_residual.astype(BF16), "fsdp", axis=1, tiled=True)

    w_out_pad = jnp.pad(w_out_all, ((0, 0), (0, nf * q_width - QUERY_HEADS * HEAD_SIZE)))
    w_out_heads = lax.dynamic_slice_in_dim(w_out_pad, z * q_width, q_width, 1)
    grad_mixed = project_back(grad_attn_branch, w_out_heads).astype(BF16)
    grad_query_pre, dk, dv = attention_backward(
        half, queries, mixed_own, grad_mixed, lse, keys, values, key_pos, own_pos, own_start, cosine, sine
    )

    down_part = project(hidden, w_down_units)
    layer_out = (
        own_rows(residual)
        + lax.psum_scatter(down_part.astype(BF16), "fsdp", scatter_dimension=1, tiled=True).astype(F32)
    ).astype(BF16)
    hidden_all = lax.all_gather(hidden, "fsdp", axis=2, tiled=True)
    out_rows = w_out.shape[0]
    grad_branch_own = lax.dynamic_slice_in_dim(cotangent, z * out_rows, out_rows, 2)
    grad_attn_own = lax.dynamic_slice_in_dim(grad_attn_branch, z * out_rows, out_rows, 2)
    grad_down_w = weight_grad(grad_branch_own, hidden_all).astype(BF16)
    grad_gate_w = weight_grad(grad_gate_pre, mlp_in).astype(BF16)
    grad_up_w = weight_grad(grad_up_pre, mlp_in).astype(BF16)
    grad_down_w, grad_gate_w, grad_up_w = lax.psum((grad_down_w, grad_gate_w, grad_up_w), "ctx")
    grad_out_w = weight_grad(grad_attn_own, mixed).astype(BF16)

    grad_kv = lax.all_to_all(
        jnp.concatenate([dk, dv], axis=-1).reshape(seqs, nc, rows, 2 * k_width), "ctx", 1, 1, tiled=True
    )
    grad_kv = jnp.sum(grad_kv.astype(F32), axis=1)
    grad_key_rot = grad_kv[..., :k_width]
    parts = grad_key_rot.reshape(seqs, rows, 2, 2, half_len)
    swapped = jnp.concatenate([parts[:, :, :, 1:], parts[:, :, :, :1]], axis=3)
    grad_key_pre = (
        grad_key_rot * cosine - swapped.reshape(seqs, rows, k_width) * sine
    ).astype(BF16)
    grad_value_pre = grad_kv[..., k_width:].astype(BF16)

    grad_pre = jnp.concatenate([grad_query_pre, grad_key_pre, grad_value_pre], axis=-1)
    grad_attn_part = project_back(grad_pre, jnp.concatenate([wq, wk, wv], axis=0))
    grad_in_w = weight_grad(grad_pre, attn_in).astype(BF16)
    grad_attn_in = exchange(grad_attn_part)
    own_normed, own_inv = own_rows(normed_attn), own_rows(inv_attn)
    scaled = grad_attn_in * attn_gain_all
    grad_gain_attn = jnp.sum(grad_attn_in * own_normed, axis=(0, 1))
    grad_tokens = (
        grad_residual
        + own_inv * (scaled - own_normed * jnp.mean(scaled * own_normed, axis=-1, keepdims=True))
    ).astype(BF16)

    gains = lax.psum(jnp.stack([grad_gain_attn, grad_gain_mlp]), ("ctx", "fsdp"))
    gains = lax.dynamic_slice_in_dim(gains, z * attn_gain.shape[0], attn_gain.shape[0], 1)

    gq, gk, gv = (
        grad_in_w[:q_width],
        grad_in_w[q_width : q_width + k_width],
        grad_in_w[q_width + k_width :],
    )
    prev = lax.ppermute(
        jnp.concatenate([gq[q_width - q_edge :], gk[k_width - k_edge :], gv[k_width - k_edge :]], axis=0),
        "fsdp",
        up,
    )
    following = lax.ppermute(jnp.concatenate([gk[:k_edge], gv[:k_edge]], axis=0), "fsdp", down)
    grad_query_w = rows_from([prev[:q_edge], gq], q_edge - q_shift * z, q_rows)

    def shard_of(own, before, after):
        early = jnp.concatenate([before, jnp.zeros((k_rows, width), BF16)], axis=0)
        early = lax.dynamic_slice_in_dim(
            jnp.concatenate([jnp.zeros((k_shift, width), BF16), early], axis=0), k_shift * z, k_rows, 0
        )
        late = rows_from(
            [jnp.zeros((HEAD_SIZE, width), BF16), after, jnp.zeros((k_rows, width), BF16)],
            k_shift * z,
            k_rows,
        )
        mine = lax.dynamic_slice_in_dim(own, k_shift * z, k_rows, 0)
        return (mine.astype(F32) + early.astype(F32) + late.astype(F32)).astype(BF16)

    grad_key_w = shard_of(gk, prev[q_edge : q_edge + k_edge], following[:k_edge])
    grad_value_w = shard_of(gv, prev[q_edge + k_edge :], following[k_edge:])
    grad_query_w, grad_key_w, grad_value_w, grad_out_w = lax.psum(
        (grad_query_w, grad_key_w, grad_value_w, grad_out_w), "ctx"
    )
    return (
        layer_out,
        grad_tokens,
        gains[0],
        grad_query_w.astype(F32),
        grad_key_w.astype(F32),
        grad_value_w.astype(F32),
        grad_out_w.astype(F32),
        gains[1],
        grad_gate_w.astype(F32),
        grad_up_w.astype(F32),
        grad_down_w.astype(F32),
    )


def solution(mesh):
    rows = P(None, ("ctx", "fsdp"), None)
    gain, weight = P("fsdp"), P("fsdp", None)
    return jax.shard_map(
        local,
        mesh=mesh,
        in_specs=(rows, P(), P(), gain, weight, weight, weight, weight, gain, weight, weight, weight, rows),
        out_specs=(rows, rows, gain, weight, weight, weight, weight, gain, weight, weight, weight),
        check_vma=False,
    )
```

```python
import functools

import jax
import jax.numpy as jnp
from jax import lax
from jax.experimental import pallas as pl
from jax.experimental.pallas import tpu as pltpu
from jax.sharding import PartitionSpec as P

QUERY_HEADS = 15
KEY_VALUE_HEADS = 5
HEAD_SIZE = 64
GROUP = QUERY_HEADS // KEY_VALUE_HEADS
NEGATIVE = -1e30
EPSILON = 1e-05
ROPE_BASE = 10000.0
SCALE = HEAD_SIZE ** (-0.5)
BF16 = jnp.bfloat16
F32 = jnp.float32
VMEM_LIMIT = 56 * 1024 * 1024
CTX = ("pair", "core")


def nt(a, b):
    return lax.dot_general(a, b, (((1,), (1,)), ((), ())), preferred_element_type=F32)


def nn(a, b):
    return lax.dot_general(a, b, (((1,), (0,)), ((), ())), preferred_element_type=F32)


def tn(a, b):
    return lax.dot_general(a, b, (((0,), (0,)), ((), ())), preferred_element_type=F32)


def spread(pair, head, half):
    lane = lax.broadcasted_iota(jnp.int32, pair.shape, 1)
    here = (lane // HEAD_SIZE) == (head % 2)
    alone = jnp.where(here, pair, jnp.zeros_like(pair))
    return jnp.where(half == head % 2, alone, pltpu.roll(alone, HEAD_SIZE, 1))


def collect(first, second, half_first, half_second):
    lane = lax.broadcasted_iota(jnp.int32, first.shape, 1)
    low = jnp.where(half_first == 0, first, pltpu.roll(first, HEAD_SIZE, 1))
    high = jnp.where(half_second == 1, second, pltpu.roll(second, HEAD_SIZE, 1))
    return jnp.where(lane < HEAD_SIZE, low, high)


def swap_lanes(x):
    lane = lax.broadcasted_iota(jnp.int32, x.shape, 1)
    half_len = HEAD_SIZE // 2
    first = (lane % HEAD_SIZE) < half_len
    return jnp.where(first, pltpu.roll(x, x.shape[1] - half_len, 1), pltpu.roll(x, half_len, 1))


def input_kernel(
    place_ref,
    gathered_ref,
    gain_ref,
    q_ref,
    k_ref,
    v_ref,
    next_ref,
    prev_ref,
    cos_ref,
    sin_ref,
    attn_out,
    turned_out,
    kv_out,
    weight_out,
    q_rows,
    k_rows,
):
    z = place_ref[0]
    members, piece = attn_out.shape[0], attn_out.shape[1]
    q_width, k_width = turned_out.shape[2], kv_out.shape[2] // 2
    q_own, k_own = q_ref.shape[0], k_ref.shape[0]
    k_edge = prev_ref.shape[0] // 2
    q_edge = next_ref.shape[0] - 2 * k_edge
    q_shift, k_shift = q_edge // (members - 1), k_edge // (members - 1)

    q_rows[pl.ds(0, q_own), :] = q_ref[...]
    q_rows[pl.ds(q_own, q_edge), :] = next_ref[pl.ds(0, q_edge), :]
    rest = q_rows.shape[0] - q_own - q_edge
    q_rows[pl.ds(q_own + q_edge, rest), :] = jnp.zeros((rest, q_rows.shape[1]), BF16)
    start = pl.multiple_of(z * q_shift, 16)
    weight_out[pl.ds(0, q_width), :] = q_rows[pl.ds(start, q_width), :]
    for i, own in enumerate((k_ref, v_ref)):
        k_rows[pl.ds(0, k_edge), :] = prev_ref[pl.ds(i * k_edge, k_edge), :]
        k_rows[pl.ds(k_edge, k_own), :] = own[...]
        k_rows[pl.ds(k_edge + k_own, k_edge), :] = next_ref[pl.ds(q_edge + i * k_edge, k_edge), :]
        start = pl.multiple_of(k_edge - z * k_shift, 16)
        weight_out[pl.ds(q_width + i * k_width, k_width), :] = k_rows[pl.ds(start, k_width), :]

    gain = gain_ref[...]
    cosine, sine = cos_ref[...], sin_ref[...]
    for j in range(members):
        x = gathered_ref[j, pl.ds(0, piece), :].astype(F32)
        inverse = lax.rsqrt(jnp.mean(x * x, axis=1, keepdims=True) + EPSILON)
        attn_out[j] = (x * inverse * gain).astype(BF16)
        made = nt(attn_out[j], weight_out[...])
        for i in range((q_width + k_width) // 128):
            part = made[:, i * 128 : (i + 1) * 128]
            part = (part * cosine[j] + swap_lanes(part) * sine[j]).astype(BF16)
            if i < q_width // 128:
                turned_out[j, :, pl.ds(i * 128, 128)] = part
            else:
                kv_out[j, :, pl.ds(i * 128 - q_width, 128)] = part
        kv_out[j, :, pl.ds(k_width, k_width)] = made[:, q_width + k_width :].astype(BF16)


def project_inputs(z, gathered, gain, w_query, key_weight, value_weight, from_next, from_prev, cosine, sine, heads):
    members, width = gathered.shape[0], gathered.shape[2]
    piece = cosine.shape[1]
    q_width, k_width = heads * HEAD_SIZE, 2 * HEAD_SIZE
    k_edge = from_prev.shape[0] // 2
    whole = pl.BlockSpec(memory_space=pltpu.VMEM)
    return pl.pallas_call(
        input_kernel,
        in_specs=[pl.BlockSpec(memory_space=pltpu.SMEM)] + [whole] * 9,
        out_specs=[whole] * 4,
        out_shape=[
            jax.ShapeDtypeStruct((members, piece, width), BF16),
            jax.ShapeDtypeStruct((members, piece, q_width), BF16),
            jax.ShapeDtypeStruct((members, piece, 2 * k_width), BF16),
            jax.ShapeDtypeStruct((q_width + 2 * k_width, width), BF16),
        ],
        scratch_shapes=[
            pltpu.VMEM((q_width + from_next.shape[0] - 2 * k_edge, width), BF16),
            pltpu.VMEM((key_weight.shape[0] + 2 * k_edge, width), BF16),
        ],
        compiler_params=pltpu.CompilerParams(vmem_limit_bytes=VMEM_LIMIT),
        cost_estimate=pl.CostEstimate(
            flops=2 * members * piece * width * (q_width + 2 * k_width), bytes_accessed=6000000, transcendentals=0
        ),
        name="project_inputs",
    )(
        jnp.reshape(z, (1,)).astype(jnp.int32),
        gathered,
        gain,
        w_query,
        key_weight,
        value_weight,
        from_next,
        from_prev,
        cosine,
        sine,
    )


def flat(x):
    return x.reshape(-1, x.shape[-1])


def forward_kernel(
    half_ref, q_ref, k_ref, v_ref, k2_ref, v2_ref, kpos_ref, kpos2_ref, qpos_ref, qstart_ref,
    o_ref, lse_ref, q4, bias, m, l, acc,
):
    step, steps = pl.program_id(1), pl.num_programs(1)
    rows = q_ref.shape[0] * q_ref.shape[2]
    heads = q4.shape[0] // rows
    chunk = 256

    @pl.when(step == 0)
    def _():
        for h in range(heads):
            pair = flat(q_ref[:, 0, :, pl.ds((h // 2) * 128, 128)]).astype(F32) * SCALE
            q4[pl.ds(h * rows, rows), :] = spread(pair, h, half_ref[h]).astype(BF16)
        m[...] = jnp.full_like(m, NEGATIVE)
        l[...] = jnp.zeros_like(l)
        acc[...] = jnp.zeros_like(acc)

    kpos = jnp.concatenate([kpos_ref[...], kpos2_ref[...]], axis=1)
    seen = (kpos <= qpos_ref[...]) & (kpos >= qstart_ref[0])
    bias[...] = jnp.where(seen, 0.0, NEGATIVE)
    keys = jnp.concatenate([flat(k_ref[:, 0]), flat(k2_ref[:, 0])], axis=0)
    values = jnp.concatenate([flat(v_ref[:, 0]), flat(v2_ref[:, 0])], axis=0)

    def one(i, _):
        at = pl.multiple_of(i * chunk, chunk)
        within = pl.multiple_of(lax.rem(at, rows), chunk)
        s = nt(q4[pl.ds(at, chunk), :], keys) + bias[pl.ds(within, chunk), :]
        old = m[pl.ds(at, chunk), :]
        new = jnp.maximum(old, jnp.max(s, axis=1, keepdims=True))
        p = jnp.exp(s - new)
        factor = jnp.exp(old - new)
        m[pl.ds(at, chunk), :] = new
        l[pl.ds(at, chunk), :] = l[pl.ds(at, chunk), :] * factor + jnp.sum(p, axis=1, keepdims=True)
        acc[pl.ds(at, chunk), :] = acc[pl.ds(at, chunk), :] * factor + nn(p.astype(BF16), values)
        return 0

    lax.fori_loop(0, heads * rows // chunk, one, 0)

    @pl.when(step == steps - 1)
    def _():
        total = l[...]
        lse = m[...] + jnp.log(total)
        for i in range(heads * rows // 128):
            part = jnp.broadcast_to(lse[i * 128 : (i + 1) * 128], (128, 128))
            lse_ref[0, :, pl.ds(i * 128, 128)] = part.T[0:1, :]
        out = acc[...] / total
        for h in range(0, heads, 2):
            both = collect(
                out[h * rows : (h + 1) * rows],
                out[(h + 1) * rows : (h + 2) * rows],
                half_ref[h],
                half_ref[h + 1],
            )
            both = both.astype(BF16).reshape(o_ref.shape[0], o_ref.shape[2], 128)
            o_ref[:, 0, :, pl.ds((h // 2) * 128, 128)] = both


def backward_kernel(
    half_ref,
    q_ref,
    o_ref,
    do_ref,
    lse_ref,
    k_ref,
    v_ref,
    k2_ref,
    v2_ref,
    kpos_ref,
    kpos2_ref,
    qpos_ref,
    qstart_ref,
    cos_ref,
    sin_ref,
    dq_ref,
    dkv_ref,
    dkv2_ref,
    q4,
    do4,
    delta,
    dq,
):
    step, steps = pl.program_id(1), pl.num_programs(1)
    rows = q_ref.shape[0] * q_ref.shape[2]
    piece = k_ref.shape[2]
    heads = q4.shape[0] // rows
    blocks = min(4, k_ref.shape[0])
    chunk = blocks * piece

    @pl.when(step == 0)
    def _():
        for h in range(heads):
            lanes = pl.ds((h // 2) * 128, 128)
            pair = flat(q_ref[:, 0, :, lanes]).astype(F32) * SCALE
            q4[pl.ds(h * rows, rows), :] = spread(pair, h, half_ref[h]).astype(BF16)
            grad = flat(do_ref[:, 0, :, lanes]).astype(F32)
            wide = spread(grad, h, half_ref[h])
            do4[pl.ds(h * rows, rows), :] = wide.astype(BF16)
            lane = lax.broadcasted_iota(jnp.int32, grad.shape, 1)
            mine = (lane // HEAD_SIZE) == (h % 2)
            both = jnp.where(mine, grad * flat(o_ref[:, 0, :, lanes]).astype(F32), 0.0)
            total = jnp.sum(both, axis=1, keepdims=True)
            for i in range(rows // 128):
                part = jnp.broadcast_to(total[i * 128 : (i + 1) * 128], (128, 128))
                delta[:, pl.ds(h * rows + i * 128, 128)] = part.T[0:1, :]
        dq[...] = jnp.zeros_like(dq)

    lse = lse_ref[0]
    row_delta = delta[...]
    qpos, qstart = qpos_ref[...], qstart_ref[0]

    def one(k, v, positions, out, i):
        at = pl.multiple_of(i * chunk, chunk)
        keys = flat(k[pl.ds(i * blocks, blocks), 0])
        values = flat(v[pl.ds(i * blocks, blocks), 0])
        kpos = positions[pl.ds(at, chunk), :]
        seen = (kpos <= qpos) & (kpos >= qstart)
        bias = jnp.where(seen, 0.0, NEGATIVE)
        bias = jnp.concatenate([bias] * heads, axis=1)
        p = jnp.exp(nt(keys, q4[...]) + bias - lse)
        dv = nn(p.astype(BF16), do4[...]).astype(BF16)
        ds = (p * (nt(values, do4[...]) - row_delta)).astype(BF16)
        dk = nn(ds, q4[...]).astype(BF16)
        out[pl.ds(i * blocks, blocks), 0, :, pl.ds(0, 128)] = dk.reshape(blocks, piece, 128)
        out[pl.ds(i * blocks, blocks), 0, :, pl.ds(128, 128)] = dv.reshape(blocks, piece, 128)
        dq[...] += tn(ds, keys)

    def both(i, _):
        one(k_ref, v_ref, kpos_ref, dkv_ref, i)
        one(k2_ref, v2_ref, kpos2_ref, dkv2_ref, i)
        return 0

    lax.fori_loop(0, k_ref.shape[0] // blocks, both, 0)

    @pl.when(step == steps - 1)
    def _():
        cosine, sine = flat(cos_ref[...]), flat(sin_ref[...])
        for h in range(0, heads, 2):
            both = collect(
                dq[pl.ds(h * rows, rows), :],
                dq[pl.ds((h + 1) * rows, rows), :],
                half_ref[h],
                half_ref[h + 1],
            )
            both = both * SCALE
            back = (both * cosine - swap_lanes(both) * sine).astype(BF16)
            dq_ref[:, 0, :, pl.ds((h // 2) * 128, 128)] = back.reshape(dq_ref.shape[0], dq_ref.shape[2], 128)


def key_step(owners, piece):
    most = max(1, 1024 // piece)
    return most if owners % most == 0 else owners


def attention_forward(half, queries, kv, key_pos, own_pos, own_start):
    members, seqs, piece, width = queries.shape
    owners = kv[0].shape[0]
    rows, count = members * piece, 2 * owners * piece
    step = key_step(owners, piece)
    heads = width // HEAD_SIZE
    own = pl.BlockSpec((members, 1, piece, width), lambda s, b: (0, s, 0, 0))
    keys = pl.BlockSpec((step, 1, piece, 128), lambda s, b: (b, s, 0, 0))
    values = pl.BlockSpec((step, 1, piece, 128), lambda s, b: (b, s, 0, 1))
    places = pl.BlockSpec((1, step * piece), lambda s, b: (0, b))
    return pl.pallas_call(
        forward_kernel,
        grid=(seqs, owners // step),
        in_specs=[
            pl.BlockSpec(memory_space=pltpu.SMEM),
            own,
            keys,
            values,
            keys,
            values,
            places,
            places,
            pl.BlockSpec((rows, 1), lambda s, b: (0, 0)),
            pl.BlockSpec((1, rows, 1), lambda s, b: (s, 0, 0)),
        ],
        out_specs=[own, pl.BlockSpec((1, 1, heads * rows), lambda s, b: (s, 0, 0))],
        out_shape=[
            jax.ShapeDtypeStruct(queries.shape, BF16),
            jax.ShapeDtypeStruct((seqs, 1, heads * rows), F32),
        ],
        scratch_shapes=[
            pltpu.VMEM((heads * rows, 128), BF16),
            pltpu.VMEM((rows, 2 * step * piece), F32),
            pltpu.VMEM((heads * rows, 1), F32),
            pltpu.VMEM((heads * rows, 1), F32),
            pltpu.VMEM((heads * rows, 128), F32),
        ],
        compiler_params=pltpu.CompilerParams(
            dimension_semantics=("arbitrary", "arbitrary"), vmem_limit_bytes=VMEM_LIMIT
        ),
        cost_estimate=pl.CostEstimate(
            flops=4 * seqs * heads * rows * count * 128,
            bytes_accessed=seqs * count * 512,
            transcendentals=seqs * heads * rows * count,
        ),
        name="attention_forward",
    )(
        half,
        queries,
        kv[0],
        kv[0],
        kv[1],
        kv[1],
        key_pos[0][None, :],
        key_pos[1][None, :],
        own_pos[:, None],
        own_start[:, :, None],
    )


def attention_backward(half, queries, mixed, grads, lse, kv, key_pos, own_pos, own_start, cosine, sine):
    members, seqs, piece, width = queries.shape
    owners = kv[0].shape[0]
    rows, count = members * piece, 2 * owners * piece
    step = key_step(owners, piece)
    heads = width // HEAD_SIZE
    own = pl.BlockSpec((members, 1, piece, width), lambda s, b: (0, s, 0, 0))
    table = pl.BlockSpec((members, piece, 128), lambda s, b: (0, 0, 0))
    keys = pl.BlockSpec((step, 1, piece, 128), lambda s, b: (b, s, 0, 0))
    values = pl.BlockSpec((step, 1, piece, 128), lambda s, b: (b, s, 0, 1))
    places = pl.BlockSpec((step * piece, 1), lambda s, b: (b, 0))
    made = pl.BlockSpec((step, 1, piece, 256), lambda s, b: (b, s, 0, 0))
    return pl.pallas_call(
        backward_kernel,
        grid=(seqs, owners // step),
        in_specs=[
            pl.BlockSpec(memory_space=pltpu.SMEM),
            own,
            own,
            own,
            pl.BlockSpec((1, 1, heads * rows), lambda s, b: (s, 0, 0)),
            keys,
            values,
            keys,
            values,
            places,
            places,
            pl.BlockSpec((1, rows), lambda s, b: (0, 0)),
            pl.BlockSpec((1, 1, rows), lambda s, b: (s, 0, 0)),
            table,
            table,
        ],
        out_specs=[own, made, made],
        out_shape=[
            jax.ShapeDtypeStruct(queries.shape, BF16),
            jax.ShapeDtypeStruct(kv[0].shape, BF16),
            jax.ShapeDtypeStruct(kv[1].shape, BF16),
        ],
        scratch_shapes=[
            pltpu.VMEM((heads * rows, 128), BF16),
            pltpu.VMEM((heads * rows, 128), BF16),
            pltpu.VMEM((1, heads * rows), F32),
            pltpu.VMEM((heads * rows, 128), F32),
        ],
        compiler_params=pltpu.CompilerParams(
            dimension_semantics=("arbitrary", "arbitrary"), vmem_limit_bytes=VMEM_LIMIT
        ),
        cost_estimate=pl.CostEstimate(
            flops=10 * seqs * heads * rows * count * 128,
            bytes_accessed=seqs * count * 1024,
            transcendentals=seqs * heads * rows * count,
        ),
        name="attention_backward",
    )(
        half,
        queries,
        mixed,
        grads,
        lse,
        kv[0],
        kv[0],
        kv[1],
        kv[1],
        key_pos[0][:, None],
        key_pos[1][:, None],
        own_pos[None, :],
        own_start[:, None, :],
        cosine,
        sine,
    )


def feed_forward_kernel(
    place_ref,
    main_ref,
    side_ref,
    tokens_ref,
    parts_ref,
    parts_mate_ref,
    gain_ref,
    gate_ref,
    up_ref,
    *refs,
):
    members, chips = parts_ref.shape[1], parts_ref.shape[0]
    cotangent_refs, refs = refs[:members], refs[members:]
    residual_out, mixed_out, heads_out, mlp_out, hidden_out, gate_out, up_out, part_out, layer_out, cotangent = refs[:10]
    w_out, w_down, residual = refs[10:]
    z, parity, chip = place_ref[0], place_ref[1], place_ref[2]
    own, width, units = cotangent_refs[0].shape[0], w_out.shape[0], w_down.shape[1]
    out_rows, wide = width // members, w_out.shape[1]
    lanes = wide // members
    some = parts_ref.shape[2]
    for shift in range(members):
        source = lax.rem(z - shift + members, members)
        cotangent[pl.ds(pl.multiple_of(source * own, 16), own), :] = cotangent_refs[shift][...]
        first = source * out_rows
        for q in range(chips):
            for who, parts in enumerate((parts_ref, parts_mate_ref)):
                index = 2 * (chip ^ q) + (parity ^ who)
                at = pl.multiple_of(first + jnp.minimum(index * some, out_rows - some), 16)
                w_out[pl.ds(at, some), :] = parts[q, shift, :, pl.ds(0, wide)]
                w_down[pl.ds(at, some), :] = parts[q, shift, :, pl.ds(wide, units)]
    count = main_ref.shape[1]
    for j in range(members):
        mixed_out[pl.ds(0, count), pl.ds(j * lanes, lanes)] = main_ref[j]
        shift = lax.rem(z - j + members, members)
        mixed_out[pl.ds(count, side_ref.shape[1]), pl.ds(j * lanes, lanes)] = side_ref[shift]
    heads_out[...] = w_out[:, pl.ds(pl.multiple_of(z * lanes, lanes), lanes)]

    x = jnp.concatenate([tokens_ref[j, pl.ds(0, own), :] for j in range(members)], axis=0)
    residual[...] = x.astype(F32) + nt(mixed_out[...], w_out[...])
    residual_out[...] = residual[pl.ds(pl.multiple_of(z * own, own), own), :]
    here = residual[...]
    inverse = lax.rsqrt(jnp.mean(here * here, axis=1, keepdims=True) + EPSILON)
    mlp_out[...] = (here * inverse * gain_ref[...]).astype(BF16)
    mlp_in = mlp_out[...]
    gate_pre = nn(mlp_in, gate_ref[...])
    up_pre = nn(mlp_in, up_ref[...])
    sigmoid_gate = jax.nn.sigmoid(gate_pre)
    silu_gate = gate_pre * sigmoid_gate
    hidden_out[...] = (silu_gate * up_pre).astype(BF16)
    grad_hidden = nn(cotangent[...], w_down[...])
    slope = sigmoid_gate + silu_gate * (1.0 - sigmoid_gate)
    gate_out[...] = (grad_hidden * up_pre * slope).astype(BF16)
    up_out[...] = (grad_hidden * silu_gate).astype(BF16)
    part = nt(gate_out[...], gate_ref[...]) + nt(up_out[...], up_ref[...])
    part_out[:, :, pl.ds(0, width)] = part.astype(BF16).reshape(members, own, width)
    part_out[:, :, pl.ds(width, wide - width)] = jnp.zeros((members, own, wide - width), BF16)
    layer = nt(hidden_out[...], w_down[...])
    layer_out[:, :, pl.ds(0, width)] = layer.astype(BF16).reshape(members, own, width)
    layer_out[:, :, pl.ds(width, wide - width)] = jnp.zeros((members, own, wide - width), BF16)


def feed_forward(place, main, side, tokens, parts, parts_mate, gain, gate_turned, up_turned, cotangents):
    members, lanes = main.shape[0], main.shape[2]
    own, width = cotangents[0].shape
    rows, units, wide = members * own, gate_turned.shape[1], members * lanes
    whole = pl.BlockSpec(memory_space=pltpu.VMEM)
    return pl.pallas_call(
        feed_forward_kernel,
        in_specs=[pl.BlockSpec(memory_space=pltpu.SMEM)] + [whole] * (8 + members),
        out_specs=[whole] * 10,
        out_shape=[
            jax.ShapeDtypeStruct((own, width), F32),
            jax.ShapeDtypeStruct((rows, wide), BF16),
            jax.ShapeDtypeStruct((width, lanes), BF16),
            jax.ShapeDtypeStruct((rows, width), BF16),
            jax.ShapeDtypeStruct((rows, units), BF16),
            jax.ShapeDtypeStruct((rows, units), BF16),
            jax.ShapeDtypeStruct((rows, units), BF16),
            jax.ShapeDtypeStruct((members, own, wide), BF16),
            jax.ShapeDtypeStruct((members, own, wide), BF16),
            jax.ShapeDtypeStruct((rows, width), BF16),
        ],
        scratch_shapes=[
            pltpu.VMEM((width, wide), BF16),
            pltpu.VMEM((width, units), BF16),
            pltpu.VMEM((rows, width), F32),
        ],
        compiler_params=pltpu.CompilerParams(vmem_limit_bytes=VMEM_LIMIT),
        cost_estimate=pl.CostEstimate(
            flops=2 * rows * width * (6 * units + width), bytes_accessed=12000000, transcendentals=rows * units
        ),
        name="feed_forward",
    )(place, main, side, tokens, parts, parts_mate, gain, gate_turned, up_turned, *cotangents)


def feed_forward_grads_kernel(mlp_ref, gate_ref, up_ref, cotangent_ref, hidden_ref, out_ref):
    half_rows = out_ref.shape[2]
    for i, (x, g) in enumerate(((mlp_ref, gate_ref), (mlp_ref, up_ref), (cotangent_ref, hidden_ref))):
        made = tn(x[...], g[...]).astype(BF16)
        out_ref[0, i] = made[:half_rows]
        out_ref[1, i] = made[half_rows:]


def feed_forward_grads(mlp_in, grad_gate_pre, grad_up_pre, cotangent, hidden):
    rows, width = mlp_in.shape
    units = hidden.shape[1]
    whole = pl.BlockSpec(memory_space=pltpu.VMEM)
    return pl.pallas_call(
        feed_forward_grads_kernel,
        in_specs=[whole] * 5,
        out_specs=whole,
        out_shape=jax.ShapeDtypeStruct((2, 3, width // 2, units), BF16),
        compiler_params=pltpu.CompilerParams(vmem_limit_bytes=VMEM_LIMIT),
        cost_estimate=pl.CostEstimate(flops=6 * rows * width * units, bytes_accessed=8000000, transcendentals=0),
        name="feed_forward_grads",
    )(mlp_in, grad_gate_pre, grad_up_pre, cotangent, hidden)


def output_kernel(
    dq_ref, pair_ref, cos_ref, sin_ref, attn_ref, weight_ref, tokens_ref, *refs
):
    others, (grad_weight_out, part_out, gain_out, pre) = refs[:-4], refs[-4:]
    members, piece, width = attn_ref.shape
    q_width = dq_ref.shape[2]
    gain = jnp.zeros((1, attn_ref.shape[2]), F32)
    for j in range(members):
        total = pair_ref[j]
        for other in others:
            total = total + other[j].astype(F32)
        keys = total[:, :128]
        pre[j, :, pl.ds(0, q_width)] = dq_ref[j]
        pre[j, :, pl.ds(q_width, 128)] = (keys * cos_ref[j] - swap_lanes(keys) * sin_ref[j]).astype(BF16)
        pre[j, :, pl.ds(q_width + 128, 128)] = total[:, 128:].astype(BF16)
        part = nn(pre[j], weight_ref[...])
        part_out[j, :, pl.ds(0, width)] = part.astype(BF16)
        part_out[j, :, pl.ds(width, part_out.shape[2] - width)] = jnp.zeros((piece, part_out.shape[2] - width), BF16)
        x = tokens_ref[j, pl.ds(0, piece), :].astype(F32)
        inverse = lax.rsqrt(jnp.mean(x * x, axis=1, keepdims=True) + EPSILON)
        gain = gain + jnp.sum(part * (x * inverse), axis=0, keepdims=True)
    gain_out[...] = jnp.broadcast_to(gain, gain_out.shape)
    grad_weight_out[...] = tn(flat(pre[...]), flat(attn_ref[...])).astype(BF16)


def project_outputs(dq, pair, others, cosine, sine, attn_in, w_in, tokens):
    members, piece, width = attn_in.shape
    whole = pl.BlockSpec(memory_space=pltpu.VMEM)
    return pl.pallas_call(
        output_kernel,
        in_specs=[whole] * (7 + len(others)),
        out_specs=[whole] * 3,
        out_shape=[
            jax.ShapeDtypeStruct(w_in.shape, BF16),
            jax.ShapeDtypeStruct((members, piece, -(-width // 128) * 128), BF16),
            jax.ShapeDtypeStruct((8, width), F32),
        ],
        scratch_shapes=[pltpu.VMEM((members, piece, w_in.shape[0]), BF16)],
        compiler_params=pltpu.CompilerParams(vmem_limit_bytes=VMEM_LIMIT),
        cost_estimate=pl.CostEstimate(
            flops=4 * members * piece * width * w_in.shape[0], bytes_accessed=8000000, transcendentals=0
        ),
        name="project_outputs",
    )(dq, pair, cosine, sine, attn_in, w_in, tokens, *others)


def shard_kernel(place_ref, own_ref, prev_ref, next_ref, out_ref, gains_ref, keep_out, give_out, sent_out, q_rows, early, late):
    z = place_ref[0]
    width = own_ref.shape[1]
    k_edge = next_ref.shape[0] // 2
    q_edge = prev_ref.shape[0] - 2 * k_edge
    q_width = q_rows.shape[0] - q_edge
    k_width = (own_ref.shape[0] - q_width) // 2
    k_own = early.shape[0] // 2
    k_shift = k_own - HEAD_SIZE
    q_shift = q_edge * k_shift // k_edge
    q_own = q_width - q_shift
    q_rows[pl.ds(0, q_edge), :] = prev_ref[pl.ds(0, q_edge), :]
    q_rows[pl.ds(q_edge, q_width), :] = own_ref[pl.ds(0, q_width), :]
    start = pl.multiple_of(q_edge - z * q_shift, 16)
    sent_out[...] = jnp.zeros_like(sent_out)
    middle = sent_out.shape[0] // 2
    out_rows = out_ref.shape[0]
    lanes = pl.ds(0, width)
    sent_out[pl.ds(0, q_own), lanes] = q_rows[pl.ds(start, q_own), :]
    sent_out[pl.ds(middle, out_rows), lanes] = out_ref[...]
    early[...] = jnp.zeros_like(early)
    late[...] = jnp.zeros_like(late)
    start = pl.multiple_of(z * k_shift, 16)
    for i, at in enumerate((q_own, middle + out_rows)):
        early[pl.ds(k_shift, k_edge), :] = prev_ref[pl.ds(q_edge + i * k_edge, k_edge), :]
        late[pl.ds(HEAD_SIZE, k_edge), :] = next_ref[pl.ds(i * k_edge, k_edge), :]
        first = pl.multiple_of(q_width + i * k_width + start, 16)
        total = own_ref[pl.ds(first, k_own), :].astype(F32)
        total = total + early[pl.ds(start, k_own), :].astype(F32) + late[pl.ds(start, k_own), :].astype(F32)
        sent_out[pl.ds(at, k_own), lanes] = total.astype(BF16)
    sent_out[pl.ds(middle + out_rows + k_own, 16), lanes] = gains_ref[...]
    parity = place_ref[1]
    keep_out[...] = sent_out[pl.ds(pl.multiple_of(parity * middle, 16), middle), :]
    give_out[...] = sent_out[pl.ds(pl.multiple_of((1 - parity) * middle, 16), middle), :]


def shard_rows(place, own, prev, following, grad_out, gains, q_width, k_rows, total_rows):
    width = own.shape[1]
    k_edge = following.shape[0] // 2
    q_edge = prev.shape[0] - 2 * k_edge
    whole = pl.BlockSpec(memory_space=pltpu.VMEM)
    return pl.pallas_call(
        shard_kernel,
        in_specs=[pl.BlockSpec(memory_space=pltpu.SMEM)] + [whole] * 5,
        out_specs=[whole] * 2,
        out_shape=[jax.ShapeDtypeStruct((total_rows // 2, -(-width // 128) * 128), BF16)] * 2,
        scratch_shapes=[
            pltpu.VMEM((total_rows, -(-width // 128) * 128), BF16),
            pltpu.VMEM((q_width + q_edge, width), BF16),
            pltpu.VMEM((2 * k_rows, width), BF16),
            pltpu.VMEM((HEAD_SIZE + 2 * k_rows, width), BF16),
        ],
        compiler_params=pltpu.CompilerParams(vmem_limit_bytes=VMEM_LIMIT),
        cost_estimate=pl.CostEstimate(flops=0, bytes_accessed=4000000, transcendentals=0),
        name="shard_rows",
    )(place, own, prev, following, grad_out, gains)


def mate(x):
    return lax.ppermute(x, "core", [(0, 1), (1, 0)])


def across(x, by):
    return lax.ppermute(x, "pair", [(i, i ^ by) for i in range(lax.axis_size("pair"))])


def everywhere(x):
    return [x] + [across(x, by) for by in range(1, lax.axis_size("pair"))]


def pick(x, index, axis=0):
    return lax.dynamic_index_in_dim(x, index, axis, keepdims=False)


def pair_sum(x, parity):
    return (pick(x, parity).astype(F32) + mate(pick(x, 1 - parity)).astype(F32)).astype(BF16)


def add_up(pieces):
    total = pieces[0].astype(F32)
    for one in pieces[1:]:
        total = total + one.astype(F32)
    return total


def rotate(x, shift):
    nf = lax.axis_size("fsdp")
    return lax.ppermute(x, "fsdp", [(i, (i + shift) % nf) for i in range(nf)])


def after(x, *others):
    return lax.optimization_barrier((x, *others))[0]


def local(
    tokens,
    doc_lengths,
    block_table,
    attn_gain,
    w_query,
    key_weight,
    value_weight,
    w_out,
    mlp_gain,
    w_gate,
    w_up,
    w_down,
    out_cotangent,
):
    nf, chips, nc = lax.axis_size("fsdp"), lax.axis_size("pair"), lax.axis_size(CTX)
    z, parity, chip = lax.axis_index("fsdp"), lax.axis_index("core"), lax.axis_index("pair")
    c = 2 * chip + parity
    seqs, piece, width = tokens.shape
    rows = nf * piece
    half_len = HEAD_SIZE // 2
    up = [(i, i + 1) for i in range(nf - 1)]
    down = [(i + 1, i) for i in range(nf - 1)]

    heads = -(-QUERY_HEADS // nf)
    q_rows, k_rows = w_query.shape[0], key_weight.shape[0]
    q_width, k_width = heads * HEAD_SIZE, 2 * HEAD_SIZE
    q_shift = q_width - q_rows
    k_shift = k_rows - HEAD_SIZE
    q_edge, k_edge = q_shift * (nf - 1), k_shift * (nf - 1)
    head_index = jnp.arange(heads, dtype=jnp.int32)
    half = jnp.minimum((z * heads + head_index) // GROUP - z, 1).astype(jnp.int32)

    block = piece // 2
    pairs = block_table.shape[0]
    within = jnp.arange(block, dtype=jnp.int32)

    def positions_of(table):
        paired = jnp.stack([table, 2 * pairs - 1 - table], axis=1)
        return (paired[:, :, None] * block + within).reshape(-1)

    group_pos = positions_of(lax.dynamic_slice_in_dim(block_table.astype(jnp.int32), c * nf, nf, 0))
    frequency = ROPE_BASE ** (-(2.0 * jnp.arange(half_len, dtype=F32)) / HEAD_SIZE)
    angles = group_pos.astype(F32)[:, None] * frequency[None, :]
    cos, sin = jnp.cos(angles), jnp.sin(angles)
    cosine = jnp.concatenate([cos, cos, cos, cos], axis=1).reshape(nf, piece, 128)
    sine = jnp.concatenate([-sin, sin, -sin, sin], axis=1).reshape(nf, piece, 128)
    cosine_all, sine_all = jnp.concatenate([cosine] * seqs, axis=1), jnp.concatenate([sine] * seqs, axis=1)

    own_tokens = seqs * piece
    group_tokens = nf * own_tokens
    own_cotangent = out_cotangent.reshape(own_tokens, width)
    from_next = lax.ppermute(
        jnp.concatenate([w_query[:q_edge], key_weight[:k_edge], value_weight[:k_edge]], axis=0),
        "fsdp",
        down,
    )
    from_prev = lax.ppermute(
        jnp.concatenate([key_weight[k_rows - k_edge :], value_weight[k_rows - k_edge :]], axis=0),
        "fsdp",
        up,
    )

    gain_rows = jnp.pad(jnp.stack([attn_gain, mlp_gain]), ((0, 6), (0, width - attn_gain.shape[0])))
    own_payload = jnp.concatenate([tokens.reshape(own_tokens, width), gain_rows], axis=0)
    own_payload, from_next, from_prev = lax.optimization_barrier((own_payload, from_next, from_prev))
    gathered = lax.all_gather(own_payload, "fsdp", axis=0)
    gains_all = gathered[:, own_tokens : own_tokens + 2, : attn_gain.shape[0]]
    gains_all = jnp.transpose(gains_all, (1, 0, 2)).reshape(2, width).astype(F32)

    attn_in, queries, own_kv, w_in = project_inputs(
        z, gathered, gains_all[:1], w_query, key_weight, value_weight, from_next, from_prev,
        cosine_all, sine_all, heads,
    )
    same_core = jnp.concatenate(everywhere(own_kv), axis=0)
    kv = [half_kv.reshape(-1, seqs, piece, 2 * k_width) for half_kv in (same_core, mate(same_core))]
    queries = queries.reshape(nf, seqs, piece, q_width)
    late_table, late_lengths = after((block_table, doc_lengths), own_kv)
    positions = positions_of(late_table.astype(jnp.int32)).reshape(nc, rows)
    even = 2 * jnp.arange(chips, dtype=jnp.int32)
    key_pos = [jnp.take(positions, c ^ (even + i), axis=0).reshape(-1) for i in range(2)]
    own_pos = key_pos[0][:rows]
    bounds = jnp.cumsum(late_lengths, axis=1)
    reached = own_pos[None, :, None] >= bounds[:, None, :-1]
    own_start = jnp.max(jnp.where(reached, bounds[:, None, :-1], 0), axis=-1)

    out_rows, units = w_out.shape[0], w_gate.shape[0]
    some = -(-out_rows // (16 * nc)) * 16
    from_row = jnp.minimum(c * some, out_rows - some)
    wide = nf * q_width
    some_out = jnp.pad(lax.dynamic_slice_in_dim(w_out, from_row, some, 0), ((0, 0), (0, wide - width)))
    some_down = lax.dynamic_slice_in_dim(w_down, from_row, some, 0)
    some_out, some_down, late_cotangent = lax.optimization_barrier((some_out, some_down, own_cotangent, own_kv))[:3]
    pieces = []
    for shift in range(nf):
        columns = lax.dynamic_slice_in_dim(some_down, lax.rem(z + shift, nf) * units, units, 1)
        piece_out = jnp.concatenate([some_out, columns], axis=1)
        pieces.append(rotate(piece_out, shift) if shift else piece_out)
    cotangents = [own_cotangent] + [rotate(late_cotangent, shift) for shift in range(1, nf)]
    parts = everywhere(after(jnp.stack(pieces), same_core))
    gate_turned, up_turned = w_gate.T, w_up.T

    mixed_own, lse = attention_forward(half, queries, kv, key_pos, own_pos, own_start)
    parts = jnp.stack(after(parts, mixed_own))
    parts_mate = mate(parts)
    mixed_rows = after(mixed_own.reshape(group_tokens, q_width), parts, *cotangents)
    main_rows = group_tokens - 16
    side = jnp.stack([mixed_rows[main_rows:]] + [rotate(mixed_rows[main_rows:], shift) for shift in range(1, nf)])
    main = lax.all_gather(mixed_rows[:main_rows], "fsdp", axis=0)

    place = jnp.stack([z, parity, chip]).astype(jnp.int32)
    (
        residual, mixed, w_out_heads, mlp_in, hidden, grad_gate_pre, grad_up_pre, grad_mlp_part, layer_part, cotangent,
    ) = feed_forward(
        place, main, side, gathered, parts, parts_mate, gains_all[1:], gate_turned, up_turned, cotangents
    )
    mixed = mixed[:, : QUERY_HEADS * HEAD_SIZE]

    def exchange(part):
        swapped = lax.all_to_all(part, "fsdp", 0, 0, tiled=True)
        return jnp.sum(swapped.astype(F32), axis=0)[:, :width]

    grad_mlp_in = exchange(grad_mlp_part)
    inv_mlp = lax.rsqrt(jnp.mean(residual * residual, axis=-1, keepdims=True) + EPSILON)
    normed_mlp = residual * inv_mlp
    scaled = grad_mlp_in * gains_all[1]
    grad_gain_mlp = jnp.sum(grad_mlp_in * normed_mlp, axis=0)
    grad_residual = own_cotangent.astype(F32) + inv_mlp * (
        scaled - normed_mlp * jnp.mean(scaled * normed_mlp, axis=-1, keepdims=True)
    )
    made = feed_forward_grads(mlp_in, grad_gate_pre, grad_up_pre, cotangent, hidden)
    made_pair = pair_sum(made, parity).reshape(3, chips, -1, units)
    made_pieces = [pick(made_pair, chip, 1)] + [across(pick(made_pair, chip ^ by, 1), by) for by in range(1, chips)]
    branch_own, made_pair = lax.optimization_barrier((grad_residual.astype(BF16), made_pair))
    grad_attn_branch = lax.all_gather(branch_own, "fsdp", axis=0, tiled=True)

    grad_attn_branch, made_pieces = lax.optimization_barrier((grad_attn_branch, made_pieces))
    grad_mixed = nn(grad_attn_branch, w_out_heads).astype(BF16).reshape(queries.shape)
    grad_query_pre, *grad_kv = attention_backward(
        half, queries, mixed_own, grad_mixed, lse, kv, key_pos, own_pos, own_start, cosine, sine
    )
    layer_part = exchange(after(layer_part, grad_attn_branch))

    pair = (grad_kv[0].astype(F32) + mate(grad_kv[1]).astype(F32)).reshape(chips, nf, own_tokens, 2 * k_width)
    pair_low = pair.astype(BF16)
    others = [across(pair_low[by], by) for by in range(1, chips)]
    made_total = add_up(after(made_pieces, pair_low)).astype(BF16)
    made_found = everywhere(made_total)
    grad_in_w, grad_attn_part, grad_gain_attn = project_outputs(
        grad_query_pre.reshape(nf, own_tokens, q_width), pair[0], others, cosine_all, sine_all, attn_in, w_in, gathered
    )

    k_from = q_width + k_width
    prev = lax.ppermute(
        jnp.concatenate(
            [grad_in_w[q_width - q_edge : q_width], grad_in_w[k_from - k_edge : k_from], grad_in_w[-k_edge:]], axis=0
        ),
        "fsdp",
        up,
    )
    following = lax.ppermute(
        jnp.concatenate([grad_in_w[q_width : q_width + k_edge], grad_in_w[k_from : k_from + k_edge]], axis=0),
        "fsdp",
        down,
    )
    gain_width = attn_gain.shape[0]
    gains = jnp.stack([grad_gain_attn[0], grad_gain_mlp]).reshape(2, nf, gain_width)
    gains = add_up(
        [pick(gains, z, 1)] + [rotate(pick(gains, lax.rem(z + shift, nf), 1), shift) for shift in range(1, nf)]
    )
    gain_rows = jnp.pad(gains.reshape(1, 2 * gain_width), ((0, 15), (0, width - 2 * gain_width))).astype(BF16)
    gain_rows, made_found = lax.optimization_barrier((gain_rows, made_found))
    grad_attn_own = lax.dynamic_slice_in_dim(grad_attn_branch, z * out_rows, out_rows, 1)
    grad_out_w = tn(grad_attn_own, mixed).astype(BF16)
    half_rows = max(q_rows + k_rows, out_rows + k_rows + 16)
    half_rows = -(-half_rows // (16 * chips)) * 16 * chips
    keep, give = shard_rows(place, grad_in_w, prev, following, grad_out_w, gain_rows, q_width, k_rows, 2 * half_rows)
    sent_pair = (keep.astype(F32) + mate(give).astype(F32)).astype(BF16)
    swapped = lax.all_to_all(sent_pair.reshape(chips, half_rows // chips, -1), "pair", 0, 0, tiled=True)
    sent_total = jnp.sum(swapped.astype(F32), axis=0).astype(BF16)
    mine = lax.all_gather(sent_total, "pair", axis=0, tiled=True)
    other = mate(mine)
    low = jnp.where(parity == 0, mine, other)[:, :width].astype(F32)
    high = jnp.where(parity == 0, other, mine)[:, :width].astype(F32)
    gains = high[out_rows + k_rows, : 2 * gain_width]

    grad_attn_in = exchange(after(grad_attn_part, prev, following))
    own_x = tokens.reshape(own_tokens, width).astype(F32)
    inv_attn = lax.rsqrt(jnp.mean(own_x * own_x, axis=-1, keepdims=True) + EPSILON)
    normed_attn = own_x * inv_attn
    scaled = grad_attn_in * gains_all[0]
    grad_tokens = (
        grad_residual
        + inv_attn * (scaled - normed_attn * jnp.mean(scaled * normed_attn, axis=-1, keepdims=True))
    ).astype(BF16)

    layer_part = after(layer_part, sent_pair)
    layer_out = (residual + layer_part).astype(BF16)
    order = chip ^ jnp.arange(chips, dtype=jnp.int32)
    made_half = jnp.transpose(jnp.take(jnp.stack(made_found), order, axis=0), (1, 0, 2, 3)).reshape(3, width // 2, units)
    made_other = mate(made_half[:2])
    first = jnp.where(parity == 0, made_half[:2], made_other)
    second = jnp.where(parity == 0, made_other, made_half[:2])
    grad_gate_up = jnp.concatenate([first, second], axis=1).astype(F32)

    blocks = nf // 2
    down_own = made_half[2].reshape(blocks, out_rows, units)
    down_found = [pick(down_own, lax.rem(z, blocks))]
    for shift in range(1, nf):
        sent_block = pick(down_own, lax.rem(z + shift, nf) - blocks * parity)
        links = [
            (p * nf + i, p * nf + (i + shift) % nf) for p in range(2) for i in range(nf) if (i + shift) % nf // blocks == p
        ]
        down_found.append(lax.ppermute(sent_block, ("core", "fsdp"), links))
    sources = lax.rem(z - jnp.arange(nf, dtype=jnp.int32) + nf, nf)
    down_found = jnp.take(jnp.stack(down_found), sources, axis=0)
    down_found = jnp.where(z // blocks == parity, down_found, mate(down_found))
    grad_down_w = jnp.transpose(down_found, (1, 0, 2)).reshape(out_rows, nf * units)
    return (
        layer_out.reshape(tokens.shape),
        grad_tokens.reshape(tokens.shape),
        gains[:gain_width],
        low[:q_rows],
        low[q_rows : q_rows + k_rows],
        high[out_rows : out_rows + k_rows],
        high[:out_rows],
        gains[gain_width:],
        grad_gate_up[0].T,
        grad_gate_up[1].T,
        grad_down_w.astype(F32),
    )


def solution(mesh):
    count, members = mesh.shape["ctx"], mesh.shape["fsdp"]
    paired = jax.sharding.Mesh(mesh.devices.reshape(count // 2, 2, members), ("pair", "core", "fsdp"))
    rows = P(None, ("pair", "core", "fsdp"), None)
    gain, weight = P("fsdp"), P("fsdp", None)
    return jax.shard_map(
        local,
        mesh=paired,
        in_specs=(rows, P(), P(), gain, weight, weight, weight, weight, gain, weight, weight, weight, rows),
        out_specs=(rows, rows, gain, weight, weight, weight, weight, gain, weight, weight, weight),
        check_vma=False,
    )
```

```python
import functools

import jax
import jax.numpy as jnp
from jax import lax
from jax.experimental import pallas as pl
from jax.experimental.pallas import tpu as pltpu
from jax.sharding import PartitionSpec as P

QUERY_HEADS = 15
KEY_VALUE_HEADS = 5
HEAD_SIZE = 64
GROUP = QUERY_HEADS // KEY_VALUE_HEADS
NEGATIVE = -1e30
EPSILON = 1e-05
ROPE_BASE = 10000.0
SCALE = HEAD_SIZE ** (-0.5)
BF16 = jnp.bfloat16
F32 = jnp.float32
VMEM_LIMIT = 56 * 1024 * 1024
SHORT = pl.CostEstimate(flops=1000000, bytes_accessed=1000000, transcendentals=0)
CTX = ("pair", "core")


def nt(a, b):
    return lax.dot_general(a, b, (((1,), (1,)), ((), ())), preferred_element_type=F32)


def nn(a, b):
    return lax.dot_general(a, b, (((1,), (0,)), ((), ())), preferred_element_type=F32)


def tn(a, b):
    return lax.dot_general(a, b, (((0,), (0,)), ((), ())), preferred_element_type=F32)


def spread(pair, head, half):
    lane = lax.broadcasted_iota(jnp.int32, pair.shape, 1)
    here = (lane // HEAD_SIZE) == (head % 2)
    alone = jnp.where(here, pair, jnp.zeros_like(pair))
    return jnp.where(half == head % 2, alone, pltpu.roll(alone, HEAD_SIZE, 1))


def collect(first, second, half_first, half_second):
    lane = lax.broadcasted_iota(jnp.int32, first.shape, 1)
    low = jnp.where(half_first == 0, first, pltpu.roll(first, HEAD_SIZE, 1))
    high = jnp.where(half_second == 1, second, pltpu.roll(second, HEAD_SIZE, 1))
    return jnp.where(lane < HEAD_SIZE, low, high)


def swap_lanes(x):
    lane = lax.broadcasted_iota(jnp.int32, x.shape, 1)
    half_len = HEAD_SIZE // 2
    first = (lane % HEAD_SIZE) < half_len
    return jnp.where(first, pltpu.roll(x, x.shape[1] - half_len, 1), pltpu.roll(x, half_len, 1))


def input_kernel(
    place_ref,
    gathered_ref,
    gain_ref,
    q_ref,
    k_ref,
    v_ref,
    next_ref,
    prev_ref,
    cos_ref,
    sin_ref,
    attn_out,
    turned_out,
    kv_out,
    weight_out,
    q_rows,
    k_rows,
):
    z = place_ref[0]
    members, piece = attn_out.shape[0], attn_out.shape[1]
    q_width, k_width = turned_out.shape[2], kv_out.shape[2] // 2
    q_own, k_own = q_ref.shape[0], k_ref.shape[0]
    k_edge = prev_ref.shape[0] // 2
    q_edge = next_ref.shape[0] - 2 * k_edge
    q_shift, k_shift = q_edge // (members - 1), k_edge // (members - 1)

    q_rows[pl.ds(0, q_own), :] = q_ref[...]
    q_rows[pl.ds(q_own, q_edge), :] = next_ref[pl.ds(0, q_edge), :]
    rest = q_rows.shape[0] - q_own - q_edge
    q_rows[pl.ds(q_own + q_edge, rest), :] = jnp.zeros((rest, q_rows.shape[1]), BF16)
    start = pl.multiple_of(z * q_shift, 16)
    weight_out[pl.ds(0, q_width), :] = q_rows[pl.ds(start, q_width), :]
    for i, own in enumerate((k_ref, v_ref)):
        k_rows[pl.ds(0, k_edge), :] = prev_ref[pl.ds(i * k_edge, k_edge), :]
        k_rows[pl.ds(k_edge, k_own), :] = own[...]
        k_rows[pl.ds(k_edge + k_own, k_edge), :] = next_ref[pl.ds(q_edge + i * k_edge, k_edge), :]
        start = pl.multiple_of(k_edge - z * k_shift, 16)
        weight_out[pl.ds(q_width + i * k_width, k_width), :] = k_rows[pl.ds(start, k_width), :]

    gain = gain_ref[...]
    cosine, sine = cos_ref[...], sin_ref[...]
    for j in range(members):
        x = gathered_ref[j, pl.ds(0, piece), :].astype(F32)
        inverse = lax.rsqrt(jnp.mean(x * x, axis=1, keepdims=True) + EPSILON)
        attn_out[j] = (x * inverse * gain).astype(BF16)
        made = nt(attn_out[j], weight_out[...])
        for i in range((q_width + k_width) // 128):
            part = made[:, i * 128 : (i + 1) * 128]
            part = (part * cosine[j] + swap_lanes(part) * sine[j]).astype(BF16)
            if i < q_width // 128:
                turned_out[j, :, pl.ds(i * 128, 128)] = part
            else:
                kv_out[j, :, pl.ds(i * 128 - q_width, 128)] = part
        kv_out[j, :, pl.ds(k_width, k_width)] = made[:, q_width + k_width :].astype(BF16)


def project_inputs(z, gathered, gain, w_query, key_weight, value_weight, from_next, from_prev, cosine, sine, heads):
    members, width = gathered.shape[0], gathered.shape[2]
    piece = cosine.shape[1]
    q_width, k_width = heads * HEAD_SIZE, 2 * HEAD_SIZE
    k_edge = from_prev.shape[0] // 2
    whole = pl.BlockSpec(memory_space=pltpu.VMEM)
    return pl.pallas_call(
        input_kernel,
        in_specs=[pl.BlockSpec(memory_space=pltpu.SMEM)] + [whole] * 9,
        out_specs=[whole] * 4,
        out_shape=[
            jax.ShapeDtypeStruct((members, piece, width), BF16),
            jax.ShapeDtypeStruct((members, piece, q_width), BF16),
            jax.ShapeDtypeStruct((members, piece, 2 * k_width), BF16),
            jax.ShapeDtypeStruct((q_width + 2 * k_width, width), BF16),
        ],
        scratch_shapes=[
            pltpu.VMEM((q_width + from_next.shape[0] - 2 * k_edge, width), BF16),
            pltpu.VMEM((key_weight.shape[0] + 2 * k_edge, width), BF16),
        ],
        compiler_params=pltpu.CompilerParams(vmem_limit_bytes=VMEM_LIMIT),
        cost_estimate=pl.CostEstimate(
            flops=2 * members * piece * width * (q_width + 2 * k_width), bytes_accessed=6000000, transcendentals=0
        ),
        name="project_inputs",
    )(
        jnp.reshape(z, (1,)).astype(jnp.int32),
        gathered,
        gain,
        w_query,
        key_weight,
        value_weight,
        from_next,
        from_prev,
        cosine,
        sine,
    )


def flat(x):
    return x.reshape(-1, x.shape[-1])


def forward_kernel(
    half_ref, q_ref, k_ref, v_ref, k2_ref, v2_ref, kpos_ref, kpos2_ref, qpos_ref, qstart_ref,
    o_ref, lse_ref, q4, bias, m, l, acc,
):
    step, steps = pl.program_id(1), pl.num_programs(1)
    rows = q_ref.shape[0] * q_ref.shape[2]
    heads = q4.shape[0] // rows
    chunk = 256

    @pl.when(step == 0)
    def _():
        for h in range(heads):
            pair = flat(q_ref[:, 0, :, pl.ds((h // 2) * 128, 128)]).astype(F32) * SCALE
            q4[pl.ds(h * rows, rows), :] = spread(pair, h, half_ref[h]).astype(BF16)
        m[...] = jnp.full_like(m, NEGATIVE)
        l[...] = jnp.zeros_like(l)
        acc[...] = jnp.zeros_like(acc)

    kpos = jnp.concatenate([kpos_ref[...], kpos2_ref[...]], axis=1)
    seen = (kpos <= qpos_ref[...]) & (kpos >= qstart_ref[0])
    bias[...] = jnp.where(seen, 0.0, NEGATIVE)
    keys = jnp.concatenate([flat(k_ref[:, 0]), flat(k2_ref[:, 0])], axis=0)
    values = jnp.concatenate([flat(v_ref[:, 0]), flat(v2_ref[:, 0])], axis=0)

    def one(i, _):
        at = pl.multiple_of(i * chunk, chunk)
        within = pl.multiple_of(lax.rem(at, rows), chunk)
        s = nt(q4[pl.ds(at, chunk), :], keys) + bias[pl.ds(within, chunk), :]
        old = m[pl.ds(at, chunk), :]
        new = jnp.maximum(old, jnp.max(s, axis=1, keepdims=True))
        p = jnp.exp(s - new)
        factor = jnp.exp(old - new)
        m[pl.ds(at, chunk), :] = new
        l[pl.ds(at, chunk), :] = l[pl.ds(at, chunk), :] * factor + jnp.sum(p, axis=1, keepdims=True)
        acc[pl.ds(at, chunk), :] = acc[pl.ds(at, chunk), :] * factor + nn(p.astype(BF16), values)
        return 0

    lax.fori_loop(0, heads * rows // chunk, one, 0)

    @pl.when(step == steps - 1)
    def _():
        total = l[...]
        lse = m[...] + jnp.log(total)
        for i in range(heads * rows // 128):
            part = jnp.broadcast_to(lse[i * 128 : (i + 1) * 128], (128, 128))
            lse_ref[0, :, pl.ds(i * 128, 128)] = part.T[0:1, :]
        out = acc[...] / total
        for h in range(0, heads, 2):
            both = collect(
                out[h * rows : (h + 1) * rows],
                out[(h + 1) * rows : (h + 2) * rows],
                half_ref[h],
                half_ref[h + 1],
            )
            both = both.astype(BF16).reshape(o_ref.shape[0], o_ref.shape[2], 128)
            o_ref[:, 0, :, pl.ds((h // 2) * 128, 128)] = both


def backward_kernel(
    half_ref,
    q_ref,
    o_ref,
    do_ref,
    lse_ref,
    k_ref,
    v_ref,
    k2_ref,
    v2_ref,
    kpos_ref,
    kpos2_ref,
    qpos_ref,
    qstart_ref,
    cos_ref,
    sin_ref,
    dq_ref,
    dkv_ref,
    dkv2_ref,
    q4,
    do4,
    delta,
    dq,
):
    step, steps = pl.program_id(1), pl.num_programs(1)
    rows = q_ref.shape[0] * q_ref.shape[2]
    piece = k_ref.shape[2]
    heads = q4.shape[0] // rows
    blocks = min(4, k_ref.shape[0])
    chunk = blocks * piece

    @pl.when(step == 0)
    def _():
        for h in range(heads):
            lanes = pl.ds((h // 2) * 128, 128)
            pair = flat(q_ref[:, 0, :, lanes]).astype(F32) * SCALE
            q4[pl.ds(h * rows, rows), :] = spread(pair, h, half_ref[h]).astype(BF16)
            grad = flat(do_ref[:, 0, :, lanes]).astype(F32)
            wide = spread(grad, h, half_ref[h])
            do4[pl.ds(h * rows, rows), :] = wide.astype(BF16)
            lane = lax.broadcasted_iota(jnp.int32, grad.shape, 1)
            mine = (lane // HEAD_SIZE) == (h % 2)
            both = jnp.where(mine, grad * flat(o_ref[:, 0, :, lanes]).astype(F32), 0.0)
            total = jnp.sum(both, axis=1, keepdims=True)
            for i in range(rows // 128):
                part = jnp.broadcast_to(total[i * 128 : (i + 1) * 128], (128, 128))
                delta[:, pl.ds(h * rows + i * 128, 128)] = part.T[0:1, :]
        dq[...] = jnp.zeros_like(dq)

    lse = lse_ref[0]
    row_delta = delta[...]
    qpos, qstart = qpos_ref[...], qstart_ref[0]

    def one(k, v, positions, out, i):
        at = pl.multiple_of(i * chunk, chunk)
        keys = flat(k[pl.ds(i * blocks, blocks), 0])
        values = flat(v[pl.ds(i * blocks, blocks), 0])
        kpos = jnp.broadcast_to(positions[:, pl.ds(at, chunk)].astype(F32), (128, chunk)).T[:, :1].astype(jnp.int32)
        seen = (kpos <= qpos) & (kpos >= qstart)
        bias = jnp.where(seen, 0.0, NEGATIVE)
        bias = jnp.concatenate([bias] * heads, axis=1)
        p = jnp.exp(nt(keys, q4[...]) + bias - lse)
        dv = nn(p.astype(BF16), do4[...]).astype(BF16)
        ds = (p * (nt(values, do4[...]) - row_delta)).astype(BF16)
        dk = nn(ds, q4[...]).astype(BF16)
        out[pl.ds(i * blocks, blocks), 0, :, pl.ds(0, 128)] = dk.reshape(blocks, piece, 128)
        out[pl.ds(i * blocks, blocks), 0, :, pl.ds(128, 128)] = dv.reshape(blocks, piece, 128)
        dq[...] += tn(ds, keys)

    def both(i, _):
        one(k_ref, v_ref, kpos_ref, dkv_ref, i)
        one(k2_ref, v2_ref, kpos2_ref, dkv2_ref, i)
        return 0

    lax.fori_loop(0, k_ref.shape[0] // blocks, both, 0)

    @pl.when(step == steps - 1)
    def _():
        cosine, sine = flat(cos_ref[...]), flat(sin_ref[...])
        for h in range(0, heads, 2):
            both = collect(
                dq[pl.ds(h * rows, rows), :],
                dq[pl.ds((h + 1) * rows, rows), :],
                half_ref[h],
                half_ref[h + 1],
            )
            both = both * SCALE
            back = (both * cosine - swap_lanes(both) * sine).astype(BF16)
            dq_ref[:, 0, :, pl.ds((h // 2) * 128, 128)] = back.reshape(dq_ref.shape[0], dq_ref.shape[2], 128)


def key_step(owners, piece):
    most = max(1, 1024 // piece)
    return most if owners % most == 0 else owners


def attention_forward(half, queries, kv, key_pos, own_pos, own_start):
    members, seqs, piece, width = queries.shape
    owners = kv[0].shape[0]
    rows, count = members * piece, 2 * owners * piece
    step = key_step(owners, piece)
    heads = width // HEAD_SIZE
    own = pl.BlockSpec((members, 1, piece, width), lambda s, b: (0, s, 0, 0))
    keys = pl.BlockSpec((step, 1, piece, 128), lambda s, b: (b, s, 0, 0))
    values = pl.BlockSpec((step, 1, piece, 128), lambda s, b: (b, s, 0, 1))
    places = pl.BlockSpec((1, step * piece), lambda s, b: (0, b))
    return pl.pallas_call(
        forward_kernel,
        grid=(seqs, owners // step),
        in_specs=[
            pl.BlockSpec(memory_space=pltpu.SMEM),
            own,
            keys,
            values,
            keys,
            values,
            places,
            places,
            pl.BlockSpec((rows, 1), lambda s, b: (0, 0)),
            pl.BlockSpec((1, rows, 1), lambda s, b: (s, 0, 0)),
        ],
        out_specs=[own, pl.BlockSpec((1, 1, heads * rows), lambda s, b: (s, 0, 0))],
        out_shape=[
            jax.ShapeDtypeStruct(queries.shape, BF16),
            jax.ShapeDtypeStruct((seqs, 1, heads * rows), F32),
        ],
        scratch_shapes=[
            pltpu.VMEM((heads * rows, 128), BF16),
            pltpu.VMEM((rows, 2 * step * piece), F32),
            pltpu.VMEM((heads * rows, 1), F32),
            pltpu.VMEM((heads * rows, 1), F32),
            pltpu.VMEM((heads * rows, 128), F32),
        ],
        compiler_params=pltpu.CompilerParams(
            dimension_semantics=("arbitrary", "arbitrary"), vmem_limit_bytes=VMEM_LIMIT
        ),
        cost_estimate=SHORT,
        name="attention_forward",
    )(
        half,
        queries,
        kv[0],
        kv[0],
        kv[1],
        kv[1],
        key_pos[0][None, :],
        key_pos[1][None, :],
        own_pos[:, None],
        own_start[:, :, None],
    )


def attention_backward(half, queries, mixed, grads, lse, kv, key_pos, own_pos, own_start, cosine, sine):
    members, seqs, piece, width = queries.shape
    owners = kv[0].shape[0]
    rows, count = members * piece, 2 * owners * piece
    step = key_step(owners, piece)
    heads = width // HEAD_SIZE
    own = pl.BlockSpec((members, 1, piece, width), lambda s, b: (0, s, 0, 0))
    table = pl.BlockSpec((members, piece, 128), lambda s, b: (0, 0, 0))
    keys = pl.BlockSpec((step, 1, piece, 128), lambda s, b: (b, s, 0, 0))
    values = pl.BlockSpec((step, 1, piece, 128), lambda s, b: (b, s, 0, 1))
    places = pl.BlockSpec((1, step * piece), lambda s, b: (0, b))
    made = pl.BlockSpec((step, 1, piece, 256), lambda s, b: (b, s, 0, 0))
    return pl.pallas_call(
        backward_kernel,
        grid=(seqs, owners // step),
        in_specs=[
            pl.BlockSpec(memory_space=pltpu.SMEM),
            own,
            own,
            own,
            pl.BlockSpec((1, 1, heads * rows), lambda s, b: (s, 0, 0)),
            keys,
            values,
            keys,
            values,
            places,
            places,
            pl.BlockSpec((1, rows), lambda s, b: (0, 0)),
            pl.BlockSpec((1, 1, rows), lambda s, b: (s, 0, 0)),
            table,
            table,
        ],
        out_specs=[own, made, made],
        out_shape=[
            jax.ShapeDtypeStruct(queries.shape, BF16),
            jax.ShapeDtypeStruct(kv[0].shape, BF16),
            jax.ShapeDtypeStruct(kv[1].shape, BF16),
        ],
        scratch_shapes=[
            pltpu.VMEM((heads * rows, 128), BF16),
            pltpu.VMEM((heads * rows, 128), BF16),
            pltpu.VMEM((1, heads * rows), F32),
            pltpu.VMEM((heads * rows, 128), F32),
        ],
        compiler_params=pltpu.CompilerParams(
            dimension_semantics=("arbitrary", "arbitrary"), vmem_limit_bytes=VMEM_LIMIT
        ),
        cost_estimate=SHORT,
        name="attention_backward",
    )(
        half,
        queries,
        mixed,
        grads,
        lse,
        kv[0],
        kv[0],
        kv[1],
        kv[1],
        key_pos[0][None, :],
        key_pos[1][None, :],
        own_pos[None, :],
        own_start[:, None, :],
        cosine,
        sine,
    )


def feed_forward_kernel(
    place_ref,
    main_ref,
    side_ref,
    tokens_ref,
    parts_ref,
    parts_mate_ref,
    gain_ref,
    gate_ref,
    up_ref,
    cotangent_ref,
    residual_out,
    mixed_out,
    heads_out,
    mlp_out,
    hidden_out,
    gate_out,
    up_out,
    part_out,
    layer_out,
    w_out,
    w_down,
    residual,
):
    members, chips = parts_ref.shape[1], parts_ref.shape[0]
    z, parity, chip = place_ref[0], place_ref[1], place_ref[2]
    own, width, units = residual_out.shape[0], w_out.shape[0], w_down.shape[1]
    out_rows, wide = width // members, w_out.shape[1]
    lanes = wide // members
    some = parts_ref.shape[2]
    for shift in range(members):
        source = lax.rem(z - shift + members, members)
        first = source * out_rows
        for q in range(chips):
            for who, parts in enumerate((parts_ref, parts_mate_ref)):
                index = 2 * (chip ^ q) + (parity ^ who)
                at = pl.multiple_of(first + jnp.minimum(index * some, out_rows - some), 16)
                w_out[pl.ds(at, some), :] = parts[q, shift, :, pl.ds(0, wide)]
                w_down[pl.ds(at, some), :] = parts[q, shift, :, pl.ds(wide, units)]
    count = main_ref.shape[1]
    for j in range(members):
        mixed_out[pl.ds(0, count), pl.ds(j * lanes, lanes)] = main_ref[j]
        shift = lax.rem(z - j + members, members)
        mixed_out[pl.ds(count, side_ref.shape[1]), pl.ds(j * lanes, lanes)] = side_ref[shift]
    heads_out[...] = w_out[:, pl.ds(pl.multiple_of(z * lanes, lanes), lanes)]

    x = jnp.concatenate([tokens_ref[j, pl.ds(0, own), :] for j in range(members)], axis=0)
    residual[...] = x.astype(F32) + nt(mixed_out[...], w_out[...])
    residual_out[...] = residual[pl.ds(pl.multiple_of(z * own, own), own), :]
    here = residual[...]
    inverse = lax.rsqrt(jnp.mean(here * here, axis=1, keepdims=True) + EPSILON)
    mlp_out[...] = (here * inverse * gain_ref[...]).astype(BF16)
    mlp_in = mlp_out[...]
    gate_pre = nn(mlp_in, gate_ref[...])
    up_pre = nn(mlp_in, up_ref[...])
    sigmoid_gate = jax.nn.sigmoid(gate_pre)
    silu_gate = gate_pre * sigmoid_gate
    hidden_out[...] = (silu_gate * up_pre).astype(BF16)
    grad_hidden = nn(flat(cotangent_ref[...]), w_down[...])
    slope = sigmoid_gate + silu_gate * (1.0 - sigmoid_gate)
    gate_out[...] = (grad_hidden * up_pre * slope).astype(BF16)
    up_out[...] = (grad_hidden * silu_gate).astype(BF16)
    part = nt(gate_out[...], gate_ref[...]) + nt(up_out[...], up_ref[...])
    part_out[:, :, pl.ds(0, width)] = part.astype(BF16).reshape(members, own, width)
    part_out[:, :, pl.ds(width, wide - width)] = jnp.zeros((members, own, wide - width), BF16)
    layer = nt(hidden_out[...], w_down[...])
    layer_out[:, :, pl.ds(0, width)] = layer.astype(BF16).reshape(members, own, width)
    layer_out[:, :, pl.ds(width, wide - width)] = jnp.zeros((members, own, wide - width), BF16)


def feed_forward(place, main, side, tokens, parts, parts_mate, gain, gate_turned, up_turned, cotangent):
    members, lanes = main.shape[0], main.shape[2]
    own, width = cotangent.shape[1:]
    rows, units, wide = members * own, gate_turned.shape[1], members * lanes
    whole = pl.BlockSpec(memory_space=pltpu.VMEM)
    return pl.pallas_call(
        feed_forward_kernel,
        in_specs=[pl.BlockSpec(memory_space=pltpu.SMEM)] + [whole] * 9,
        out_specs=[whole] * 9,
        out_shape=[
            jax.ShapeDtypeStruct((own, width), F32),
            jax.ShapeDtypeStruct((rows, wide), BF16),
            jax.ShapeDtypeStruct((width, lanes), BF16),
            jax.ShapeDtypeStruct((rows, width), BF16),
            jax.ShapeDtypeStruct((rows, units), BF16),
            jax.ShapeDtypeStruct((rows, units), BF16),
            jax.ShapeDtypeStruct((rows, units), BF16),
            jax.ShapeDtypeStruct((members, own, wide), BF16),
            jax.ShapeDtypeStruct((members, own, wide), BF16),
        ],
        scratch_shapes=[
            pltpu.VMEM((width, wide), BF16),
            pltpu.VMEM((width, units), BF16),
            pltpu.VMEM((rows, width), F32),
        ],
        compiler_params=pltpu.CompilerParams(vmem_limit_bytes=VMEM_LIMIT),
        cost_estimate=SHORT,
        name="feed_forward",
    )(place, main, side, tokens, parts, parts_mate, gain, gate_turned, up_turned, cotangent)


def feed_forward_grads_kernel(place_ref, mlp_ref, gate_ref, up_ref, cotangent_ref, hidden_ref, keep_out, give_out):
    parity = place_ref[1]
    count = mlp_ref.shape[1] // 2
    rest = keep_out.shape[1] - count
    for i, (x, g) in enumerate(((mlp_ref, gate_ref), (mlp_ref, up_ref), (cotangent_ref, hidden_ref))):
        made = tn(x[...], g[...]).astype(BF16)
        low, high = made[:count], made[count:]
        keep_out[i, pl.ds(0, count), :] = jnp.where(parity == 0, low, high)
        give_out[i, pl.ds(0, count), :] = jnp.where(parity == 0, high, low)
        for out in (keep_out, give_out):
            out[i, pl.ds(count, rest), :] = jnp.zeros((rest, made.shape[1]), BF16)


def feed_forward_grads(place, mlp_in, grad_gate_pre, grad_up_pre, cotangent, hidden, half_rows):
    rows, width = mlp_in.shape
    units = hidden.shape[1]
    whole = pl.BlockSpec(memory_space=pltpu.VMEM)
    return pl.pallas_call(
        feed_forward_grads_kernel,
        in_specs=[pl.BlockSpec(memory_space=pltpu.SMEM)] + [whole] * 5,
        out_specs=[whole] * 2,
        out_shape=[jax.ShapeDtypeStruct((3, half_rows, units), BF16)] * 2,
        compiler_params=pltpu.CompilerParams(vmem_limit_bytes=VMEM_LIMIT),
        cost_estimate=pl.CostEstimate(flops=6 * rows * width * units, bytes_accessed=8000000, transcendentals=0),
        name="feed_forward_grads",
    )(place, mlp_in, grad_gate_pre, grad_up_pre, cotangent, hidden)


def finish_kernel(place_ref, *refs):
    chips = (len(refs) - 3) // 2
    parts, outs = refs[:-3], refs[-3:]
    parity, chip = place_ref[1], place_ref[2]
    part = parts[0].shape[1]
    count = outs[2].shape[0]
    tail = count % part
    for who in range(2):
        first = (parity ^ who) * count
        for q in range(chips):
            at = (chip ^ q) * part
            for i in range(3 - who):
                block = parts[who * chips + q][i].astype(outs[i].dtype)
                base = at if i == 2 else first + at

                @pl.when(at + part <= count)
                def _():
                    outs[i][pl.ds(pl.multiple_of(base, 16), part), :] = block

                if tail:

                    @pl.when(at + tail == count)
                    def _():
                        outs[i][pl.ds(pl.multiple_of(base, 16), tail), :] = block[:tail]


def finish(place, found, found_mate, width):
    units = found[0].shape[2]
    whole = pl.BlockSpec(memory_space=pltpu.VMEM)
    parts = [*found, *found_mate]
    return pl.pallas_call(
        finish_kernel,
        in_specs=[pl.BlockSpec(memory_space=pltpu.SMEM)] + [whole] * len(parts),
        out_specs=[whole] * 3,
        out_shape=[jax.ShapeDtypeStruct((width, units), F32)] * 2 + [jax.ShapeDtypeStruct((width // 2, units), BF16)],
        compiler_params=pltpu.CompilerParams(vmem_limit_bytes=VMEM_LIMIT),
        cost_estimate=pl.CostEstimate(flops=0, bytes_accessed=9000000, transcendentals=0),
        name="finish",
    )(place, *parts)


def down_kernel(place_ref, *refs):
    parts, out = refs[:-1], refs[-1]
    members = len(parts) // 2
    z, parity = place_ref[0], place_ref[1]
    units = parts[0].shape[1]
    mine = z // (members // 2) == parity
    for shift in range(members):
        source = lax.rem(z - shift + members, members)
        block = jnp.where(mine, parts[shift][...], parts[members + shift][...])
        out[:, pl.ds(pl.multiple_of(source * units, 128), units)] = block.astype(F32)


def finish_down(place, found, found_mate):
    rows, units = found[0].shape
    whole = pl.BlockSpec(memory_space=pltpu.VMEM)
    return pl.pallas_call(
        down_kernel,
        in_specs=[pl.BlockSpec(memory_space=pltpu.SMEM)] + [whole] * 2 * len(found),
        out_specs=whole,
        out_shape=jax.ShapeDtypeStruct((rows, len(found) * units), F32),
        compiler_params=pltpu.CompilerParams(vmem_limit_bytes=VMEM_LIMIT),
        cost_estimate=pl.CostEstimate(flops=0, bytes_accessed=6000000, transcendentals=0),
        name="finish_down",
    )(place, *found, *found_mate)


def output_kernel(
    place_ref, dq_ref, pair_ref, cos_ref, sin_ref, attn_ref, weight_ref, tokens_ref, grad_out_ref, mlp_gain_ref, *refs
):
    others, (keep_out, give_out, part_out, pre, sent) = refs[:-5], refs[-5:]
    members, piece, width = attn_ref.shape
    q_width = dq_ref.shape[2]
    gain = jnp.zeros((1, width), F32)
    for j in range(members):
        total = pair_ref[j]
        for other in others:
            total = total + other[j].astype(F32)
        keys = total[:, :128]
        pre[j, :, pl.ds(0, q_width)] = dq_ref[j]
        pre[j, :, pl.ds(q_width, 128)] = (keys * cos_ref[j] - swap_lanes(keys) * sin_ref[j]).astype(BF16)
        pre[j, :, pl.ds(q_width + 128, 128)] = total[:, 128:].astype(BF16)
        part = nn(pre[j], weight_ref[...])
        part_out[j, :, pl.ds(0, width)] = part.astype(BF16)
        part_out[j, :, pl.ds(width, part_out.shape[2] - width)] = jnp.zeros((piece, part_out.shape[2] - width), BF16)
        x = tokens_ref[j, pl.ds(0, piece), :].astype(F32)
        inverse = lax.rsqrt(jnp.mean(x * x, axis=1, keepdims=True) + EPSILON)
        gain = gain + jnp.sum(part * (x * inverse), axis=0, keepdims=True)
    half_rows = keep_out.shape[0]
    low = q_width + 128
    out_rows = grad_out_ref.shape[0]
    lanes = pl.ds(0, width)
    sent[...] = jnp.zeros_like(sent)
    made = tn(flat(pre[...]), flat(attn_ref[...])).astype(BF16)
    sent[pl.ds(0, low), lanes] = made[:low]
    sent[pl.ds(half_rows, 128), lanes] = made[low:]
    sent[pl.ds(half_rows + 128, out_rows), lanes] = grad_out_ref[...]
    row = lax.broadcasted_iota(jnp.int32, (16, width), 0)
    gains = jnp.where(row == 0, gain, jnp.where(row == 1, mlp_gain_ref[...], 0.0))
    sent[pl.ds(half_rows + 128 + out_rows, 16), lanes] = gains.astype(BF16)
    parity = place_ref[1]
    keep_out[...] = sent[pl.ds(pl.multiple_of(parity * half_rows, 16), half_rows), :]
    give_out[...] = sent[pl.ds(pl.multiple_of((1 - parity) * half_rows, 16), half_rows), :]


def project_outputs(place, dq, pair, others, cosine, sine, attn_in, w_in, tokens, grad_out, gain_mlp, half_rows):
    members, piece, width = attn_in.shape
    wide = -(-width // 128) * 128
    whole = pl.BlockSpec(memory_space=pltpu.VMEM)
    return pl.pallas_call(
        output_kernel,
        in_specs=[pl.BlockSpec(memory_space=pltpu.SMEM)] + [whole] * (9 + len(others)),
        out_specs=[whole] * 3,
        out_shape=[
            jax.ShapeDtypeStruct((half_rows, wide), BF16),
            jax.ShapeDtypeStruct((half_rows, wide), BF16),
            jax.ShapeDtypeStruct((members, piece, wide), BF16),
        ],
        scratch_shapes=[
            pltpu.VMEM((members, piece, w_in.shape[0]), BF16),
            pltpu.VMEM((2 * half_rows, wide), BF16),
        ],
        compiler_params=pltpu.CompilerParams(vmem_limit_bytes=VMEM_LIMIT),
        cost_estimate=SHORT,
        name="project_outputs",
    )(place, dq, pair, cosine, sine, attn_in, w_in, tokens, grad_out, gain_mlp, *others)


def shard_kernel(
    place_ref, mine_ref, other_ref, up_ref, up_mate_ref, down_ref, down_mate_ref, q_out, k_out, v_out, o_out, q_rows, early, late
):
    z, parity = place_ref[0], place_ref[1]
    width = q_out.shape[1]
    k_edge = down_ref.shape[0]
    q_edge = up_ref.shape[0] - k_edge
    q_width = q_rows.shape[0] - q_edge
    k_own, q_own = k_out.shape[0], q_out.shape[0]
    k_shift, q_shift = k_own - HEAD_SIZE, q_width - q_own

    def ordered(mine, other, rows):
        a, b = mine[rows, pl.ds(0, width)], other[rows, pl.ds(0, width)]
        return jnp.where(parity == 0, a, b), jnp.where(parity == 0, b, a)

    q_rows[pl.ds(0, q_edge), :] = ordered(up_ref, up_mate_ref, pl.ds(0, q_edge))[0]
    q_rows[pl.ds(q_edge, q_width), :] = ordered(mine_ref, other_ref, pl.ds(0, q_width))[0]
    start = pl.multiple_of(q_edge - z * q_shift, 16)
    q_out[...] = q_rows[pl.ds(start, q_own), :].astype(F32)
    o_out[...] = ordered(mine_ref, other_ref, pl.ds(128, o_out.shape[0]))[1].astype(F32)
    early[...] = jnp.zeros_like(early)
    late[...] = jnp.zeros_like(late)
    start = pl.multiple_of(z * k_shift, 16)
    for which, first, edge_at, out in ((0, q_width, q_edge, k_out), (1, 0, 0, v_out)):
        early[pl.ds(k_shift, k_edge), :] = ordered(up_ref, up_mate_ref, pl.ds(edge_at, k_edge))[which]
        late[pl.ds(HEAD_SIZE, k_edge), :] = ordered(down_ref, down_mate_ref, pl.ds(0, k_edge))[which]
        rows = pl.ds(pl.multiple_of(first + start, 16), k_own)
        total = ordered(mine_ref, other_ref, rows)[which].astype(F32)
        out[...] = total + early[pl.ds(start, k_own), :].astype(F32) + late[pl.ds(start, k_own), :].astype(F32)


def shard_rows(place, mine, other, up, up_mate, down, down_mate, q_width, q_rows, k_rows, out_rows, width):
    k_edge = down.shape[0]
    q_edge = up.shape[0] - k_edge
    whole = pl.BlockSpec(memory_space=pltpu.VMEM)
    return pl.pallas_call(
        shard_kernel,
        in_specs=[pl.BlockSpec(memory_space=pltpu.SMEM)] + [whole] * 6,
        out_specs=[whole] * 4,
        out_shape=[jax.ShapeDtypeStruct((rows, width), F32) for rows in (q_rows, k_rows, k_rows, out_rows)],
        scratch_shapes=[
            pltpu.VMEM((q_width + q_edge, width), BF16),
            pltpu.VMEM((2 * k_rows, width), BF16),
            pltpu.VMEM((HEAD_SIZE + 2 * k_rows, width), BF16),
        ],
        compiler_params=pltpu.CompilerParams(vmem_limit_bytes=VMEM_LIMIT),
        cost_estimate=SHORT,
        name="shard_rows",
    )(place, mine, other, up, up_mate, down, down_mate)


def mate(x):
    return lax.ppermute(x, "core", [(0, 1), (1, 0)])


def across(x, by):
    return lax.ppermute(x, "pair", [(i, i ^ by) for i in range(lax.axis_size("pair"))])


def everywhere(x):
    return [x] + [across(x, by) for by in range(1, lax.axis_size("pair"))]


def pick(x, index, axis=0):
    return lax.dynamic_index_in_dim(x, index, axis, keepdims=False)


def pair_sum(x, parity):
    return (pick(x, parity).astype(F32) + mate(pick(x, 1 - parity)).astype(F32)).astype(BF16)


def add_up(pieces):
    total = pieces[0].astype(F32)
    for one in pieces[1:]:
        total = total + one.astype(F32)
    return total


def rotate(x, shift):
    nf = lax.axis_size("fsdp")
    return lax.ppermute(x, "fsdp", [(i, (i + shift) % nf) for i in range(nf)])


def after(x, *others):
    return lax.optimization_barrier((x, *others))[0]


def local(
    tokens,
    doc_lengths,
    block_table,
    attn_gain,
    w_query,
    key_weight,
    value_weight,
    w_out,
    mlp_gain,
    w_gate,
    w_up,
    w_down,
    out_cotangent,
):
    nf, chips, nc = lax.axis_size("fsdp"), lax.axis_size("pair"), lax.axis_size(CTX)
    z, parity, chip = lax.axis_index("fsdp"), lax.axis_index("core"), lax.axis_index("pair")
    c = 2 * chip + parity
    seqs, piece, width = tokens.shape
    rows = nf * piece
    half_len = HEAD_SIZE // 2
    up = [(i, i + 1) for i in range(nf - 1)]
    down = [(i + 1, i) for i in range(nf - 1)]

    heads = -(-QUERY_HEADS // nf)
    q_rows, k_rows = w_query.shape[0], key_weight.shape[0]
    q_width, k_width = heads * HEAD_SIZE, 2 * HEAD_SIZE
    q_shift = q_width - q_rows
    k_shift = k_rows - HEAD_SIZE
    q_edge, k_edge = q_shift * (nf - 1), k_shift * (nf - 1)
    head_index = jnp.arange(heads, dtype=jnp.int32)
    half = jnp.minimum((z * heads + head_index) // GROUP - z, 1).astype(jnp.int32)

    block = piece // 2
    pairs = block_table.shape[0]
    within = jnp.arange(block, dtype=jnp.int32)

    def positions_of(table):
        paired = jnp.stack([table, 2 * pairs - 1 - table], axis=1)
        return (paired[:, :, None] * block + within).reshape(-1)

    group_pos = positions_of(lax.dynamic_slice_in_dim(block_table.astype(jnp.int32), c * nf, nf, 0))
    frequency = ROPE_BASE ** (-(2.0 * jnp.arange(half_len, dtype=F32)) / HEAD_SIZE)
    angles = group_pos.astype(F32)[:, None] * frequency[None, :]
    cos, sin = jnp.cos(angles), jnp.sin(angles)
    cosine = jnp.concatenate([cos, cos, cos, cos], axis=1).reshape(nf, piece, 128)
    sine = jnp.concatenate([-sin, sin, -sin, sin], axis=1).reshape(nf, piece, 128)
    cosine_all, sine_all = jnp.concatenate([cosine] * seqs, axis=1), jnp.concatenate([sine] * seqs, axis=1)

    own_tokens = seqs * piece
    group_tokens = nf * own_tokens
    own_cotangent = out_cotangent.reshape(own_tokens, width)
    from_next = lax.ppermute(
        jnp.concatenate([w_query[:q_edge], key_weight[:k_edge], value_weight[:k_edge]], axis=0),
        "fsdp",
        down,
    )
    from_prev = lax.ppermute(
        jnp.concatenate([key_weight[k_rows - k_edge :], value_weight[k_rows - k_edge :]], axis=0),
        "fsdp",
        up,
    )

    gain_rows = jnp.pad(jnp.stack([attn_gain, mlp_gain]), ((0, 6), (0, width - attn_gain.shape[0])))
    own_payload = jnp.concatenate([tokens.reshape(own_tokens, width), gain_rows], axis=0)
    own_payload, from_next, from_prev = lax.optimization_barrier((own_payload, from_next, from_prev))
    gathered = lax.all_gather(own_payload, "fsdp", axis=0)
    gains_all = gathered[:, own_tokens : own_tokens + 2, : attn_gain.shape[0]]
    gains_all = jnp.transpose(gains_all, (1, 0, 2)).reshape(2, width).astype(F32)

    attn_in, queries, own_kv, w_in = project_inputs(
        z, gathered, gains_all[:1], w_query, key_weight, value_weight, from_next, from_prev,
        cosine_all, sine_all, heads,
    )
    cotangent = lax.all_gather(after(own_cotangent, own_kv), "fsdp", axis=0)
    same_core, cotangent = lax.optimization_barrier((everywhere(own_kv), cotangent))
    same_core = jnp.concatenate(same_core, axis=0)
    kv = [half_kv.reshape(-1, seqs, piece, 2 * k_width) for half_kv in (same_core, mate(same_core))]
    queries = queries.reshape(nf, seqs, piece, q_width)
    late_table, late_lengths = after((block_table, doc_lengths), own_kv)
    positions = positions_of(late_table.astype(jnp.int32)).reshape(nc, rows)
    even = 2 * jnp.arange(chips, dtype=jnp.int32)
    key_pos = [jnp.take(positions, c ^ (even + i), axis=0).reshape(-1) for i in range(2)]
    own_pos = key_pos[0][:rows]
    bounds = jnp.cumsum(late_lengths, axis=1)
    reached = own_pos[None, :, None] >= bounds[:, None, :-1]
    own_start = jnp.max(jnp.where(reached, bounds[:, None, :-1], 0), axis=-1)

    out_rows, units = w_out.shape[0], w_gate.shape[0]
    some = -(-out_rows // (16 * nc)) * 16
    from_row = jnp.minimum(c * some, out_rows - some)
    wide = nf * q_width
    some_out = jnp.pad(lax.dynamic_slice_in_dim(w_out, from_row, some, 0), ((0, 0), (0, wide - width)))
    some_down = lax.dynamic_slice_in_dim(w_down, from_row, some, 0)
    some_out, some_down = lax.optimization_barrier((some_out, some_down, gathered))[:2]
    pieces = []
    for shift in range(nf):
        columns = lax.dynamic_slice_in_dim(some_down, lax.rem(z + shift, nf) * units, units, 1)
        piece_out = jnp.concatenate([some_out, columns], axis=1)
        pieces.append(rotate(piece_out, shift) if shift else piece_out)
    parts = everywhere(jnp.stack(pieces))
    gate_turned, up_turned = w_gate.T, w_up.T

    mixed_own, lse = attention_forward(half, queries, kv, key_pos, own_pos, own_start)
    parts = jnp.stack(after(parts, mixed_own))
    parts_mate = mate(parts)
    mixed_rows = after(mixed_own.reshape(group_tokens, q_width), parts)
    main_rows = group_tokens - 16
    side = jnp.stack([mixed_rows[main_rows:]] + [rotate(mixed_rows[main_rows:], shift) for shift in range(1, nf)])
    main = lax.all_gather(mixed_rows[:main_rows], "fsdp", axis=0)

    place = jnp.stack([z, parity, chip]).astype(jnp.int32)
    (
        residual, mixed, w_out_heads, mlp_in, hidden, grad_gate_pre, grad_up_pre, grad_mlp_part, layer_part,
    ) = feed_forward(
        place, main, side, gathered, parts, parts_mate, gains_all[1:], gate_turned, up_turned, cotangent
    )
    mixed = mixed[:, : QUERY_HEADS * HEAD_SIZE]

    def exchange(part):
        swapped = lax.all_to_all(part, "fsdp", 0, 0, tiled=True)
        return jnp.sum(swapped.astype(F32), axis=0)[:, :width]

    grad_mlp_in = exchange(grad_mlp_part)
    inv_mlp = lax.rsqrt(jnp.mean(residual * residual, axis=-1, keepdims=True) + EPSILON)
    normed_mlp = residual * inv_mlp
    scaled = grad_mlp_in * gains_all[1]
    grad_gain_mlp = jnp.sum(grad_mlp_in * normed_mlp, axis=0)
    grad_residual = own_cotangent.astype(F32) + inv_mlp * (
        scaled - normed_mlp * jnp.mean(scaled * normed_mlp, axis=-1, keepdims=True)
    )
    part_rows = -(-(width // 2) // (16 * chips)) * 16
    keep, give = feed_forward_grads(
        place, mlp_in, grad_gate_pre, grad_up_pre, cotangent.reshape(group_tokens, width), hidden, part_rows * chips
    )
    made_pair = (keep.astype(F32) + mate(give).astype(F32)).astype(BF16).reshape(3, chips, part_rows, units)
    made_pieces = [pick(made_pair, chip, 1)] + [across(pick(made_pair, chip ^ by, 1), by) for by in range(1, chips)]
    branch_own, _ = lax.optimization_barrier((grad_residual.astype(BF16), made_pair))
    grad_attn_branch = lax.all_gather(branch_own, "fsdp", axis=0, tiled=True)

    made_total = add_up(made_pieces).astype(BF16)
    grad_attn_branch, made_total = lax.optimization_barrier((grad_attn_branch, made_total))
    made_found = everywhere(made_total)
    grad_mixed = nn(grad_attn_branch, w_out_heads).astype(BF16).reshape(queries.shape)
    grad_query_pre, *grad_kv = attention_backward(
        half, queries, mixed_own, grad_mixed, lse, kv, key_pos, own_pos, own_start, cosine_all, sine_all
    )
    layer_part = lax.all_to_all(after(layer_part, grad_attn_branch), "fsdp", 0, 0, tiled=True)

    grad_kv, made_found, layer_part = lax.optimization_barrier((grad_kv, made_found, layer_part))
    taken = [own.reshape(chips, nf, own_tokens, 2 * k_width) for own in (grad_kv[0], mate(grad_kv[1]))]
    pair = taken[0][0].astype(F32) + taken[1][0].astype(F32)
    pair_low = [(taken[0][by].astype(F32) + taken[1][by].astype(F32)).astype(BF16) for by in range(1, chips)]
    others = [across(pair_low[by - 1], by) for by in range(1, chips)]
    grad_attn_own = lax.dynamic_slice_in_dim(grad_attn_branch, z * out_rows, out_rows, 1)
    grad_out_w = tn(grad_attn_own, mixed).astype(BF16)
    made_found = after(made_found, pair_low)
    grad_gate_w, grad_up_w, down_own = finish(place, made_found, [mate(found) for found in made_found], width)
    others, grad_gate_w, grad_up_w, down_own = lax.optimization_barrier((others, grad_gate_w, grad_up_w, down_own))
    half_rows = max(q_width + k_width, k_width + out_rows + 16)
    half_rows = -(-half_rows // (16 * chips)) * 16 * chips
    keep, give, grad_attn_part = project_outputs(
        place, grad_query_pre.reshape(nf, own_tokens, q_width), pair, others, cosine_all, sine_all, attn_in, w_in, gathered,
        grad_out_w, grad_gain_mlp[None], half_rows,
    )

    sent_pair = (keep.astype(F32) + mate(give).astype(F32)).astype(BF16)
    sent_pair = sent_pair.reshape(chips, half_rows // chips, -1)
    sent_pieces = [pick(sent_pair, chip)] + [across(pick(sent_pair, chip ^ by), by) for by in range(1, chips)]
    swapped = lax.all_to_all(grad_attn_part, "fsdp", 0, 0, tiled=True)

    blocks = nf // 2
    down_own = after(down_own, sent_pair).reshape(blocks, out_rows, units)
    down_found = [pick(down_own, lax.rem(z, blocks))]
    for shift in range(1, nf):
        sent_block = pick(down_own, lax.rem(z + shift, nf) - blocks * parity)
        links = [
            (p * nf + i, p * nf + (i + shift) % nf) for p in range(2) for i in range(nf) if (i + shift) % nf // blocks == p
        ]
        down_found.append(lax.ppermute(sent_block, ("core", "fsdp"), links))
    sent_total = add_up(sent_pieces).astype(BF16)
    mine = lax.all_gather(sent_total, "pair", axis=0, tiled=True)
    other = mate(mine)

    edge_rows = jnp.zeros((q_edge, mine.shape[1]), BF16)
    upward = jnp.where(
        parity == 0,
        jnp.concatenate([mine[q_width - q_edge : q_width], mine[q_width + k_width - k_edge : q_width + k_width]]),
        jnp.concatenate([mine[k_width - k_edge : k_width], edge_rows]),
    )
    downward = jnp.where(parity == 0, mine[q_width : q_width + k_edge], mine[:k_edge])
    upward, downward = lax.ppermute(upward, "fsdp", up), lax.ppermute(downward, "fsdp", down)
    grad_query_w, grad_key_w, grad_value_w, grad_out_w = shard_rows(
        place, mine, other, upward, mate(upward), downward, mate(downward), q_width, q_rows, k_rows, out_rows, width
    )
    gain_width = attn_gain.shape[0]
    gain_row = k_width + out_rows
    gains = jnp.where(parity == 0, other[gain_row : gain_row + 2, :width], mine[gain_row : gain_row + 2, :width])
    gains = gains.astype(F32).reshape(2, nf, gain_width)
    gains = add_up(
        [pick(gains, z, 1)] + [rotate(pick(gains, lax.rem(z + shift, nf), 1), shift) for shift in range(1, nf)]
    )

    swapped = after(swapped, sent_total)
    grad_attn_in = add_up([pick(swapped, i) for i in range(nf)])[:, :width]
    own_x = tokens.reshape(own_tokens, width).astype(F32)
    inv_attn = lax.rsqrt(jnp.mean(own_x * own_x, axis=-1, keepdims=True) + EPSILON)
    normed_attn = own_x * inv_attn
    scaled = grad_attn_in * gains_all[0]
    grad_tokens = (
        grad_residual
        + inv_attn * (scaled - normed_attn * jnp.mean(scaled * normed_attn, axis=-1, keepdims=True))
    ).astype(BF16)

    layer_part = after(layer_part, sent_pair)
    layer_out = (residual + jnp.sum(layer_part.astype(F32), axis=0)[:, :width]).astype(BF16)
    down_found = after(down_found, mine)
    grad_down_w = finish_down(place, down_found, [mate(found) for found in down_found])
    return (
        layer_out.reshape(tokens.shape),
        grad_tokens.reshape(tokens.shape),
        gains[0],
        grad_query_w,
        grad_key_w,
        grad_value_w,
        grad_out_w,
        gains[1],
        grad_gate_w.T,
        grad_up_w.T,
        grad_down_w,
    )


def solution(mesh):
    count, members = mesh.shape["ctx"], mesh.shape["fsdp"]
    paired = jax.sharding.Mesh(mesh.devices.reshape(count // 2, 2, members), ("pair", "core", "fsdp"))
    rows = P(None, ("pair", "core", "fsdp"), None)
    gain, weight = P("fsdp"), P("fsdp", None)
    return jax.shard_map(
        local,
        mesh=paired,
        in_specs=(rows, P(), P(), gain, weight, weight, weight, weight, gain, weight, weight, weight, rows),
        out_specs=(rows, rows, gain, weight, weight, weight, weight, gain, weight, weight, weight),
        check_vma=False,
    )
```

```python
import functools

import jax
import jax.numpy as jnp
from jax import lax
from jax.experimental import pallas as pl
from jax.experimental.pallas import tpu as pltpu
from jax.sharding import PartitionSpec as P

QUERY_HEADS = 15
KEY_VALUE_HEADS = 5
HEAD_SIZE = 64
GROUP = QUERY_HEADS // KEY_VALUE_HEADS
NEGATIVE = -1e30
EPSILON = 1e-05
ROPE_BASE = 10000.0
SCALE = HEAD_SIZE ** (-0.5)
BF16 = jnp.bfloat16
F32 = jnp.float32
VMEM_LIMIT = 56 * 1024 * 1024
SHORT = pl.CostEstimate(flops=1000000, bytes_accessed=1000000, transcendentals=0)
CTX = ("pair", "core")
FORWARD_ROWS, FORWARD_UNROLL = 512, 2
BACKWARD_BLOCKS, BACKWARD_UNROLL = 8, 2


def nt(a, b):
    return lax.dot_general(a, b, (((1,), (1,)), ((), ())), preferred_element_type=F32)


def nn(a, b):
    return lax.dot_general(a, b, (((1,), (0,)), ((), ())), preferred_element_type=F32)


def tn(a, b):
    return lax.dot_general(a, b, (((0,), (0,)), ((), ())), preferred_element_type=F32)


def spread(pair, head, half):
    lane = lax.broadcasted_iota(jnp.int32, pair.shape, 1)
    here = (lane // HEAD_SIZE) == (head % 2)
    alone = jnp.where(here, pair, jnp.zeros_like(pair))
    return jnp.where(half == head % 2, alone, pltpu.roll(alone, HEAD_SIZE, 1))


def collect(first, second, half_first, half_second):
    lane = lax.broadcasted_iota(jnp.int32, first.shape, 1)
    low = jnp.where(half_first == 0, first, pltpu.roll(first, HEAD_SIZE, 1))
    high = jnp.where(half_second == 1, second, pltpu.roll(second, HEAD_SIZE, 1))
    return jnp.where(lane < HEAD_SIZE, low, high)


def swap_lanes(x):
    lane = lax.broadcasted_iota(jnp.int32, x.shape, 1)
    half_len = HEAD_SIZE // 2
    first = (lane % HEAD_SIZE) < half_len
    return jnp.where(first, pltpu.roll(x, x.shape[1] - half_len, 1), pltpu.roll(x, half_len, 1))


def input_kernel(
    place_ref,
    gathered_ref,
    gain_ref,
    q_ref,
    k_ref,
    v_ref,
    next_ref,
    prev_ref,
    cos_ref,
    sin_ref,
    attn_out,
    turned_out,
    kv_out,
    weight_out,
    q_rows,
    k_rows,
):
    z = place_ref[0]
    members, piece = attn_out.shape[0], attn_out.shape[1]
    q_width, k_width = turned_out.shape[2], kv_out.shape[2] // 2
    q_own, k_own = q_ref.shape[0], k_ref.shape[0]
    k_edge = prev_ref.shape[0] // 2
    q_edge = next_ref.shape[0] - 2 * k_edge
    q_shift, k_shift = q_edge // (members - 1), k_edge // (members - 1)

    q_rows[pl.ds(0, q_own), :] = q_ref[...]
    q_rows[pl.ds(q_own, q_edge), :] = next_ref[pl.ds(0, q_edge), :]
    rest = q_rows.shape[0] - q_own - q_edge
    q_rows[pl.ds(q_own + q_edge, rest), :] = jnp.zeros((rest, q_rows.shape[1]), BF16)
    start = pl.multiple_of(z * q_shift, 16)
    weight_out[pl.ds(0, q_width), :] = q_rows[pl.ds(start, q_width), :]
    for i, own in enumerate((k_ref, v_ref)):
        k_rows[pl.ds(0, k_edge), :] = prev_ref[pl.ds(i * k_edge, k_edge), :]
        k_rows[pl.ds(k_edge, k_own), :] = own[...]
        k_rows[pl.ds(k_edge + k_own, k_edge), :] = next_ref[pl.ds(q_edge + i * k_edge, k_edge), :]
        start = pl.multiple_of(k_edge - z * k_shift, 16)
        weight_out[pl.ds(q_width + i * k_width, k_width), :] = k_rows[pl.ds(start, k_width), :]

    gain = gain_ref[...]
    cosine, sine = cos_ref[...], sin_ref[...]
    for j in range(members):
        x = gathered_ref[j, pl.ds(0, piece), :].astype(F32)
        inverse = lax.rsqrt(jnp.mean(x * x, axis=1, keepdims=True) + EPSILON)
        attn_out[j] = (x * inverse * gain).astype(BF16)
        made = nt(attn_out[j], weight_out[...])
        for i in range((q_width + k_width) // 128):
            part = made[:, i * 128 : (i + 1) * 128]
            part = (part * cosine[j] + swap_lanes(part) * sine[j]).astype(BF16)
            if i < q_width // 128:
                turned_out[j, :, pl.ds(i * 128, 128)] = part
            else:
                kv_out[j, :, pl.ds(i * 128 - q_width, 128)] = part
        kv_out[j, :, pl.ds(k_width, k_width)] = made[:, q_width + k_width :].astype(BF16)


def project_inputs(z, gathered, gain, w_query, key_weight, value_weight, from_next, from_prev, cosine, sine, heads):
    members, width = gathered.shape[0], gathered.shape[2]
    piece = cosine.shape[1]
    q_width, k_width = heads * HEAD_SIZE, 2 * HEAD_SIZE
    k_edge = from_prev.shape[0] // 2
    whole = pl.BlockSpec(memory_space=pltpu.VMEM)
    return pl.pallas_call(
        input_kernel,
        in_specs=[pl.BlockSpec(memory_space=pltpu.SMEM)] + [whole] * 9,
        out_specs=[whole] * 4,
        out_shape=[
            jax.ShapeDtypeStruct((members, piece, width), BF16),
            jax.ShapeDtypeStruct((members, piece, q_width), BF16),
            jax.ShapeDtypeStruct((members, piece, 2 * k_width), BF16),
            jax.ShapeDtypeStruct((q_width + 2 * k_width, width), BF16),
        ],
        scratch_shapes=[
            pltpu.VMEM((q_width + from_next.shape[0] - 2 * k_edge, width), BF16),
            pltpu.VMEM((key_weight.shape[0] + 2 * k_edge, width), BF16),
        ],
        compiler_params=pltpu.CompilerParams(vmem_limit_bytes=VMEM_LIMIT),
        cost_estimate=pl.CostEstimate(
            flops=2 * members * piece * width * (q_width + 2 * k_width), bytes_accessed=6000000, transcendentals=0
        ),
        name="project_inputs",
    )(
        jnp.reshape(z, (1,)).astype(jnp.int32),
        gathered,
        gain,
        w_query,
        key_weight,
        value_weight,
        from_next,
        from_prev,
        cosine,
        sine,
    )


def flat(x):
    return x.reshape(-1, x.shape[-1])


def forward_kernel(
    half_ref, q_ref, k_ref, v_ref, k2_ref, v2_ref, kpos_ref, kpos2_ref, qpos_ref, qstart_ref,
    o_ref, lse_ref, q4, bias, m, l, acc,
):
    step, steps = pl.program_id(1), pl.num_programs(1)
    rows = q_ref.shape[0] * q_ref.shape[2]
    heads = q4.shape[0] // rows
    chunk = max(rows, min(FORWARD_ROWS, heads * rows))

    @pl.when(step == 0)
    def _():
        for h in range(heads):
            pair = flat(q_ref[:, 0, :, pl.ds((h // 2) * 128, 128)]).astype(F32) * SCALE
            q4[pl.ds(h * rows, rows), :] = spread(pair, h, half_ref[h]).astype(BF16)
        m[...] = jnp.full_like(m, NEGATIVE)
        l[...] = jnp.zeros_like(l)
        acc[...] = jnp.zeros_like(acc)

    kpos = jnp.concatenate([kpos_ref[...], kpos2_ref[...]], axis=1)
    seen = (kpos <= qpos_ref[...]) & (kpos >= qstart_ref[0])
    bias[...] = jnp.where(seen, 0.0, NEGATIVE)
    keys = jnp.concatenate([flat(k_ref[:, 0]), flat(k2_ref[:, 0])], axis=0)
    values = jnp.concatenate([flat(v_ref[:, 0]), flat(v2_ref[:, 0])], axis=0)

    def one(i, _):
        at = pl.multiple_of(i * chunk, chunk)
        s = nt(q4[pl.ds(at, chunk), :], keys) + jnp.concatenate([bias[...]] * (chunk // rows), axis=0)
        old = m[pl.ds(at, chunk), :]
        new = jnp.maximum(old, jnp.max(s, axis=1, keepdims=True))
        p = jnp.exp(s - new)
        factor = jnp.exp(old - new)
        m[pl.ds(at, chunk), :] = new
        l[pl.ds(at, chunk), :] = l[pl.ds(at, chunk), :] * factor + jnp.sum(p, axis=1, keepdims=True)
        acc[pl.ds(at, chunk), :] = acc[pl.ds(at, chunk), :] * factor + nn(p.astype(BF16), values)
        return 0

    lax.fori_loop(0, heads * rows // chunk, one, 0, unroll=FORWARD_UNROLL)

    @pl.when(step == steps - 1)
    def _():
        total = l[...]
        lse = m[...] + jnp.log(total)
        for i in range(heads * rows // 128):
            part = jnp.broadcast_to(lse[i * 128 : (i + 1) * 128], (128, 128))
            lse_ref[0, :, pl.ds(i * 128, 128)] = part.T[0:1, :]
        out = acc[...] / total
        for h in range(0, heads, 2):
            both = collect(
                out[h * rows : (h + 1) * rows],
                out[(h + 1) * rows : (h + 2) * rows],
                half_ref[h],
                half_ref[h + 1],
            )
            both = both.astype(BF16).reshape(o_ref.shape[0], o_ref.shape[2], 128)
            o_ref[:, 0, :, pl.ds((h // 2) * 128, 128)] = both


def backward_kernel(
    half_ref,
    q_ref,
    o_ref,
    branch_ref,
    w_ref,
    lse_ref,
    k_ref,
    v_ref,
    k2_ref,
    v2_ref,
    kpos_ref,
    kpos2_ref,
    qpos_ref,
    qstart_ref,
    cos_ref,
    sin_ref,
    dq_ref,
    dkv_ref,
    dkv2_ref,
    q4,
    do4,
    delta,
    dq,
):
    step, steps = pl.program_id(1), pl.num_programs(1)
    rows = q_ref.shape[0] * q_ref.shape[2]
    piece = k_ref.shape[2]
    heads = q4.shape[0] // rows
    blocks = min(BACKWARD_BLOCKS, k_ref.shape[0])
    chunk = blocks * piece

    @pl.when(step == 0)
    def _():
        grad_mixed = nn(flat(branch_ref[:, 0]), w_ref[...]).astype(BF16).astype(F32)
        for h in range(heads):
            lanes = pl.ds((h // 2) * 128, 128)
            pair = flat(q_ref[:, 0, :, lanes]).astype(F32) * SCALE
            q4[pl.ds(h * rows, rows), :] = spread(pair, h, half_ref[h]).astype(BF16)
            grad = grad_mixed[:, (h // 2) * 128 : (h // 2 + 1) * 128]
            wide = spread(grad, h, half_ref[h])
            do4[pl.ds(h * rows, rows), :] = wide.astype(BF16)
            lane = lax.broadcasted_iota(jnp.int32, grad.shape, 1)
            mine = (lane // HEAD_SIZE) == (h % 2)
            both = jnp.where(mine, grad * flat(o_ref[:, 0, :, lanes]).astype(F32), 0.0)
            total = jnp.sum(both, axis=1, keepdims=True)
            for i in range(rows // 128):
                part = jnp.broadcast_to(total[i * 128 : (i + 1) * 128], (128, 128))
                delta[:, pl.ds(h * rows + i * 128, 128)] = part.T[0:1, :]
        dq[...] = jnp.zeros_like(dq)

    lse = lse_ref[0]
    row_delta = delta[...]
    qpos, qstart = qpos_ref[...], qstart_ref[0]

    def one(k, v, positions, out, i):
        at = pl.multiple_of(i * chunk, chunk)
        keys = flat(k[pl.ds(i * blocks, blocks), 0])
        values = flat(v[pl.ds(i * blocks, blocks), 0])
        kpos = jnp.broadcast_to(positions[:, pl.ds(at, chunk)].astype(F32), (128, chunk)).T[:, :1].astype(jnp.int32)
        seen = (kpos <= qpos) & (kpos >= qstart)
        bias = jnp.where(seen, 0.0, NEGATIVE)
        bias = jnp.concatenate([bias] * heads, axis=1)
        p = jnp.exp(nt(keys, q4[...]) + bias - lse)
        dv = nn(p.astype(BF16), do4[...]).astype(BF16)
        ds = (p * (nt(values, do4[...]) - row_delta)).astype(BF16)
        dk = nn(ds, q4[...]).astype(BF16)
        out[pl.ds(i * blocks, blocks), 0, :, pl.ds(0, 128)] = dk.reshape(blocks, piece, 128)
        out[pl.ds(i * blocks, blocks), 0, :, pl.ds(128, 128)] = dv.reshape(blocks, piece, 128)
        dq[...] += tn(ds, keys)

    def both(i, _):
        one(k_ref, v_ref, kpos_ref, dkv_ref, i)
        one(k2_ref, v2_ref, kpos2_ref, dkv2_ref, i)
        return 0

    lax.fori_loop(0, k_ref.shape[0] // blocks, both, 0, unroll=BACKWARD_UNROLL)

    @pl.when(step == steps - 1)
    def _():
        cosine, sine = flat(cos_ref[...]), flat(sin_ref[...])
        for h in range(0, heads, 2):
            both = collect(
                dq[pl.ds(h * rows, rows), :],
                dq[pl.ds((h + 1) * rows, rows), :],
                half_ref[h],
                half_ref[h + 1],
            )
            both = both * SCALE
            back = (both * cosine - swap_lanes(both) * sine).astype(BF16)
            dq_ref[:, 0, :, pl.ds((h // 2) * 128, 128)] = back.reshape(dq_ref.shape[0], dq_ref.shape[2], 128)


def key_step(owners, piece):
    most = max(1, 1024 // piece)
    return most if owners % most == 0 else owners


def attention_forward(half, queries, kv, own_pos, own_start, key_pos, key_pos2):
    members, seqs, piece, width = queries.shape
    owners = kv[0].shape[0]
    rows, count = members * piece, 2 * owners * piece
    step = key_step(owners, piece)
    heads = width // HEAD_SIZE
    own = pl.BlockSpec((members, 1, piece, width), lambda s, b: (0, s, 0, 0))
    keys = pl.BlockSpec((step, 1, piece, 128), lambda s, b: (b, s, 0, 0))
    values = pl.BlockSpec((step, 1, piece, 128), lambda s, b: (b, s, 0, 1))
    places = pl.BlockSpec((1, step * piece), lambda s, b: (0, b))
    return pl.pallas_call(
        forward_kernel,
        grid=(seqs, owners // step),
        in_specs=[
            pl.BlockSpec(memory_space=pltpu.SMEM),
            own,
            keys,
            values,
            keys,
            values,
            places,
            places,
            pl.BlockSpec((rows, 1), lambda s, b: (0, 0)),
            pl.BlockSpec((1, rows, 1), lambda s, b: (s, 0, 0)),
        ],
        out_specs=[own, pl.BlockSpec((1, 1, heads * rows), lambda s, b: (s, 0, 0))],
        out_shape=[
            jax.ShapeDtypeStruct(queries.shape, BF16),
            jax.ShapeDtypeStruct((seqs, 1, heads * rows), F32),
        ],
        scratch_shapes=[
            pltpu.VMEM((heads * rows, 128), BF16),
            pltpu.VMEM((rows, 2 * step * piece), F32),
            pltpu.VMEM((heads * rows, 1), F32),
            pltpu.VMEM((heads * rows, 1), F32),
            pltpu.VMEM((heads * rows, 128), F32),
        ],
        compiler_params=pltpu.CompilerParams(
            dimension_semantics=("arbitrary", "arbitrary"), vmem_limit_bytes=VMEM_LIMIT
        ),
        cost_estimate=SHORT,
        name="attention_forward",
    )(
        half,
        queries,
        kv[0],
        kv[0],
        kv[1],
        kv[1],
        key_pos,
        key_pos2,
        own_pos,
        own_start,
    )


def attention_backward(half, queries, mixed, branch, w_heads, lse, kv, key_pos, own_pos, own_start, cosine, sine):
    members, seqs, piece, width = queries.shape
    owners = kv[0].shape[0]
    rows, count = members * piece, 2 * owners * piece
    step = key_step(owners, piece)
    heads = width // HEAD_SIZE
    own = pl.BlockSpec((members, 1, piece, width), lambda s, b: (0, s, 0, 0))
    table = pl.BlockSpec((members, piece, 128), lambda s, b: (0, 0, 0))
    keys = pl.BlockSpec((step, 1, piece, 128), lambda s, b: (b, s, 0, 0))
    values = pl.BlockSpec((step, 1, piece, 128), lambda s, b: (b, s, 0, 1))
    places = pl.BlockSpec((1, step * piece), lambda s, b: (0, b))
    made = pl.BlockSpec((step, 1, piece, 256), lambda s, b: (b, s, 0, 0))
    return pl.pallas_call(
        backward_kernel,
        grid=(seqs, owners // step),
        in_specs=[
            pl.BlockSpec(memory_space=pltpu.SMEM),
            own,
            own,
            pl.BlockSpec((members, 1, piece, branch.shape[3]), lambda s, b: (0, s, 0, 0)),
            pl.BlockSpec(w_heads.shape, lambda s, b: (0, 0)),
            pl.BlockSpec((1, 1, heads * rows), lambda s, b: (s, 0, 0)),
            keys,
            values,
            keys,
            values,
            places,
            places,
            pl.BlockSpec((1, rows), lambda s, b: (0, 0)),
            pl.BlockSpec((1, 1, rows), lambda s, b: (s, 0, 0)),
            table,
            table,
        ],
        out_specs=[own, made, made],
        out_shape=[
            jax.ShapeDtypeStruct(queries.shape, BF16),
            jax.ShapeDtypeStruct(kv[0].shape, BF16),
            jax.ShapeDtypeStruct(kv[1].shape, BF16),
        ],
        scratch_shapes=[
            pltpu.VMEM((heads * rows, 128), BF16),
            pltpu.VMEM((heads * rows, 128), BF16),
            pltpu.VMEM((1, heads * rows), F32),
            pltpu.VMEM((heads * rows, 128), F32),
        ],
        compiler_params=pltpu.CompilerParams(
            dimension_semantics=("arbitrary", "arbitrary"), vmem_limit_bytes=VMEM_LIMIT
        ),
        cost_estimate=SHORT,
        name="attention_backward",
    )(
        half,
        queries,
        mixed,
        branch,
        w_heads,
        lse,
        kv[0],
        kv[0],
        kv[1],
        kv[1],
        *key_pos,
        own_pos[None, :],
        own_start[:, None, :],
        cosine,
        sine,
    )


def feed_forward_kernel(
    place_ref,
    main_ref,
    side_ref,
    tokens_ref,
    gain_ref,
    gate_ref,
    up_ref,
    cotangent_ref,
    *refs,
):
    parts, refs = refs[:-12], refs[-12:]
    residual_out, mixed_out, heads_out, mlp_out, hidden_out, gate_out, up_out, part_out, layer_out = refs[:9]
    w_out, w_down, residual = refs[9:]
    members, chips = main_ref.shape[0], len(parts) // 2
    z, parity, chip = place_ref[0], place_ref[1], place_ref[2]
    own, width, units = residual_out.shape[0], w_out.shape[0], w_down.shape[1]
    out_rows, wide = width // members, w_out.shape[1]
    lanes = wide // members
    some = parts[0].shape[1]
    for shift in range(members):
        source = lax.rem(z - shift + members, members)
        first = source * out_rows
        for q in range(chips):
            for who in range(2):
                part = parts[who * chips + q]
                index = 2 * (chip ^ q) + (parity ^ who)
                at = pl.multiple_of(first + jnp.minimum(index * some, out_rows - some), 16)
                w_out[pl.ds(at, some), :] = part[shift, :, pl.ds(0, wide)]
                w_down[pl.ds(at, some), :] = part[shift, :, pl.ds(wide, units)]
    count = main_ref.shape[1]
    for j in range(members):
        mixed_out[pl.ds(0, count), pl.ds(j * lanes, lanes)] = main_ref[j]
        shift = lax.rem(z - j + members, members)
        mixed_out[pl.ds(count, side_ref.shape[1]), pl.ds(j * lanes, lanes)] = side_ref[shift]
    heads_out[...] = w_out[:, pl.ds(pl.multiple_of(z * lanes, lanes), lanes)]

    x = jnp.concatenate([tokens_ref[j, pl.ds(0, own), :] for j in range(members)], axis=0)
    residual[...] = x.astype(F32) + nt(mixed_out[...], w_out[...])
    residual_out[...] = residual[pl.ds(pl.multiple_of(z * own, own), own), :]
    here = residual[...]
    inverse = lax.rsqrt(jnp.mean(here * here, axis=1, keepdims=True) + EPSILON)
    mlp_out[...] = (here * inverse * gain_ref[...]).astype(BF16)
    mlp_in = mlp_out[...]
    gate_pre = nn(mlp_in, gate_ref[...])
    up_pre = nn(mlp_in, up_ref[...])
    sigmoid_gate = jax.nn.sigmoid(gate_pre)
    silu_gate = gate_pre * sigmoid_gate
    hidden_out[...] = (silu_gate * up_pre).astype(BF16)
    grad_hidden = nn(flat(cotangent_ref[...]), w_down[...])
    slope = sigmoid_gate + silu_gate * (1.0 - sigmoid_gate)
    gate_out[...] = (grad_hidden * up_pre * slope).astype(BF16)
    up_out[...] = (grad_hidden * silu_gate).astype(BF16)
    part = nt(gate_out[...], gate_ref[...]) + nt(up_out[...], up_ref[...])
    part_out[:, :, pl.ds(0, width)] = part.astype(BF16).reshape(members, own, width)
    part_out[:, :, pl.ds(width, wide - width)] = jnp.zeros((members, own, wide - width), BF16)
    layer = nt(hidden_out[...], w_down[...])
    layer_out[:, :, pl.ds(0, width)] = layer.astype(BF16).reshape(members, own, width)
    layer_out[:, :, pl.ds(width, wide - width)] = jnp.zeros((members, own, wide - width), BF16)


def feed_forward(place, main, side, tokens, parts, gain, gate_turned, up_turned, cotangent):
    members, lanes = main.shape[0], main.shape[2]
    own, width = cotangent.shape[1:]
    rows, units, wide = members * own, gate_turned.shape[1], members * lanes
    whole = pl.BlockSpec(memory_space=pltpu.VMEM)
    return pl.pallas_call(
        feed_forward_kernel,
        in_specs=[pl.BlockSpec(memory_space=pltpu.SMEM)] + [whole] * (7 + len(parts)),
        out_specs=[whole] * 9,
        out_shape=[
            jax.ShapeDtypeStruct((own, width), F32),
            jax.ShapeDtypeStruct((rows, wide), BF16),
            jax.ShapeDtypeStruct((width, lanes), BF16),
            jax.ShapeDtypeStruct((rows, width), BF16),
            jax.ShapeDtypeStruct((rows, units), BF16),
            jax.ShapeDtypeStruct((rows, units), BF16),
            jax.ShapeDtypeStruct((rows, units), BF16),
            jax.ShapeDtypeStruct((members, own, wide), BF16),
            jax.ShapeDtypeStruct((members, own, wide), BF16),
        ],
        scratch_shapes=[
            pltpu.VMEM((width, wide), BF16),
            pltpu.VMEM((width, units), BF16),
            pltpu.VMEM((rows, width), F32),
        ],
        compiler_params=pltpu.CompilerParams(vmem_limit_bytes=VMEM_LIMIT),
        cost_estimate=SHORT,
        name="feed_forward",
    )(place, main, side, tokens, gain, gate_turned, up_turned, cotangent, *parts)


def feed_forward_grads_kernel(place_ref, mlp_ref, gate_ref, up_ref, cotangent_ref, hidden_ref, keep_out, give_out):
    parity = place_ref[1]
    count = mlp_ref.shape[1] // 2
    rest = keep_out.shape[1] - count
    for i, (x, g) in enumerate(((mlp_ref, gate_ref), (mlp_ref, up_ref), (cotangent_ref, hidden_ref))):
        made = tn(x[...], g[...]).astype(BF16)
        low, high = made[:count], made[count:]
        keep_out[i, pl.ds(0, count), :] = jnp.where(parity == 0, low, high)
        give_out[i, pl.ds(0, count), :] = jnp.where(parity == 0, high, low)
        for out in (keep_out, give_out):
            out[i, pl.ds(count, rest), :] = jnp.zeros((rest, made.shape[1]), BF16)


def feed_forward_grads(place, mlp_in, grad_gate_pre, grad_up_pre, cotangent, hidden, half_rows):
    rows, width = mlp_in.shape
    units = hidden.shape[1]
    whole = pl.BlockSpec(memory_space=pltpu.VMEM)
    return pl.pallas_call(
        feed_forward_grads_kernel,
        in_specs=[pl.BlockSpec(memory_space=pltpu.SMEM)] + [whole] * 5,
        out_specs=[whole] * 2,
        out_shape=[jax.ShapeDtypeStruct((3, half_rows, units), BF16)] * 2,
        compiler_params=pltpu.CompilerParams(vmem_limit_bytes=VMEM_LIMIT),
        cost_estimate=pl.CostEstimate(flops=6 * rows * width * units, bytes_accessed=8000000, transcendentals=0),
        name="feed_forward_grads",
    )(place, mlp_in, grad_gate_pre, grad_up_pre, cotangent, hidden)


def finish_kernel(place_ref, *refs):
    chips = (len(refs) - 3) // 2
    parts, outs = refs[:-3], refs[-3:]
    parity, chip = place_ref[1], place_ref[2]
    part = parts[0].shape[1]
    count = outs[2].shape[0]
    tail = count % part
    for who in range(2):
        first = (parity ^ who) * count
        for q in range(chips):
            at = (chip ^ q) * part
            for i in range(3 - who):
                block = parts[who * chips + q][i].astype(outs[i].dtype)
                base = at if i == 2 else first + at

                @pl.when(at + part <= count)
                def _():
                    outs[i][pl.ds(pl.multiple_of(base, 16), part), :] = block

                if tail:

                    @pl.when(at + tail == count)
                    def _():
                        outs[i][pl.ds(pl.multiple_of(base, 16), tail), :] = block[:tail]


def finish(place, found, found_mate, width):
    units = found[0].shape[2]
    whole = pl.BlockSpec(memory_space=pltpu.VMEM)
    parts = [*found, *found_mate]
    return pl.pallas_call(
        finish_kernel,
        in_specs=[pl.BlockSpec(memory_space=pltpu.SMEM)] + [whole] * len(parts),
        out_specs=[whole] * 3,
        out_shape=[jax.ShapeDtypeStruct((width, units), F32)] * 2 + [jax.ShapeDtypeStruct((width // 2, units), BF16)],
        compiler_params=pltpu.CompilerParams(vmem_limit_bytes=VMEM_LIMIT),
        cost_estimate=pl.CostEstimate(flops=0, bytes_accessed=9000000, transcendentals=0),
        name="finish",
    )(place, *parts)


def down_kernel(place_ref, *refs):
    parts, out = refs[:-1], refs[-1]
    members = len(parts) // 2
    z, parity = place_ref[0], place_ref[1]
    units = parts[0].shape[1]
    mine = z // (members // 2) == parity
    for shift in range(members):
        source = lax.rem(z - shift + members, members)
        block = jnp.where(mine, parts[shift][...], parts[members + shift][...])
        out[:, pl.ds(pl.multiple_of(source * units, 128), units)] = block.astype(F32)


def finish_down(place, found, found_mate):
    rows, units = found[0].shape
    whole = pl.BlockSpec(memory_space=pltpu.VMEM)
    return pl.pallas_call(
        down_kernel,
        in_specs=[pl.BlockSpec(memory_space=pltpu.SMEM)] + [whole] * 2 * len(found),
        out_specs=whole,
        out_shape=jax.ShapeDtypeStruct((rows, len(found) * units), F32),
        compiler_params=pltpu.CompilerParams(vmem_limit_bytes=VMEM_LIMIT),
        cost_estimate=pl.CostEstimate(flops=0, bytes_accessed=6000000, transcendentals=0),
        name="finish_down",
    )(place, *found, *found_mate)


def output_kernel(
    place_ref, dq_ref, pair_ref, cos_ref, sin_ref, attn_ref, weight_ref, tokens_ref, grad_out_ref, mlp_gain_ref, *refs
):
    others, (keep_out, give_out, part_out, pre, sent) = refs[:-5], refs[-5:]
    members, piece, width = attn_ref.shape
    q_width = dq_ref.shape[2]
    gain = jnp.zeros((1, width), F32)
    for j in range(members):
        total = pair_ref[j]
        for other in others:
            total = total + other[j].astype(F32)
        keys = total[:, :128]
        pre[j, :, pl.ds(0, q_width)] = dq_ref[j]
        pre[j, :, pl.ds(q_width, 128)] = (keys * cos_ref[j] - swap_lanes(keys) * sin_ref[j]).astype(BF16)
        pre[j, :, pl.ds(q_width + 128, 128)] = total[:, 128:].astype(BF16)
        part = nn(pre[j], weight_ref[...])
        part_out[j, :, pl.ds(0, width)] = part.astype(BF16)
        part_out[j, :, pl.ds(width, part_out.shape[2] - width)] = jnp.zeros((piece, part_out.shape[2] - width), BF16)
        x = tokens_ref[j, pl.ds(0, piece), :].astype(F32)
        inverse = lax.rsqrt(jnp.mean(x * x, axis=1, keepdims=True) + EPSILON)
        gain = gain + jnp.sum(part * (x * inverse), axis=0, keepdims=True)
    half_rows = keep_out.shape[0]
    low = q_width + 128
    out_rows = grad_out_ref.shape[0]
    lanes = pl.ds(0, width)
    sent[...] = jnp.zeros_like(sent)
    made = tn(flat(pre[...]), flat(attn_ref[...])).astype(BF16)
    sent[pl.ds(0, low), lanes] = made[:low]
    sent[pl.ds(half_rows, 128), lanes] = made[low:]
    sent[pl.ds(half_rows + 128, out_rows), lanes] = grad_out_ref[...]
    row = lax.broadcasted_iota(jnp.int32, (16, width), 0)
    gains = jnp.where(row == 0, gain, jnp.where(row == 1, mlp_gain_ref[...], 0.0))
    sent[pl.ds(half_rows + 128 + out_rows, 16), lanes] = gains.astype(BF16)
    parity = place_ref[1]
    keep_out[...] = sent[pl.ds(pl.multiple_of(parity * half_rows, 16), half_rows), :]
    give_out[...] = sent[pl.ds(pl.multiple_of((1 - parity) * half_rows, 16), half_rows), :]


def project_outputs(place, dq, pair, others, cosine, sine, attn_in, w_in, tokens, grad_out, gain_mlp, half_rows):
    members, piece, width = attn_in.shape
    wide = -(-width // 128) * 128
    whole = pl.BlockSpec(memory_space=pltpu.VMEM)
    return pl.pallas_call(
        output_kernel,
        in_specs=[pl.BlockSpec(memory_space=pltpu.SMEM)] + [whole] * (9 + len(others)),
        out_specs=[whole] * 3,
        out_shape=[
            jax.ShapeDtypeStruct((half_rows, wide), BF16),
            jax.ShapeDtypeStruct((half_rows, wide), BF16),
            jax.ShapeDtypeStruct((members, piece, wide), BF16),
        ],
        scratch_shapes=[
            pltpu.VMEM((members, piece, w_in.shape[0]), BF16),
            pltpu.VMEM((2 * half_rows, wide), BF16),
        ],
        compiler_params=pltpu.CompilerParams(vmem_limit_bytes=VMEM_LIMIT),
        cost_estimate=SHORT,
        name="project_outputs",
    )(place, dq, pair, cosine, sine, attn_in, w_in, tokens, grad_out, gain_mlp, *others)


def shard_kernel(
    place_ref, mine_ref, other_ref, up_ref, up_mate_ref, down_ref, down_mate_ref, *refs
):
    gains, (q_out, k_out, v_out, o_out, gains_out, q_rows, early, late) = refs[:-8], refs[-8:]
    total = gains[0][...]
    for one in gains[1:]:
        total = total + one[...]
    gains_out[...] = total
    z, parity = place_ref[0], place_ref[1]
    width = q_out.shape[1]
    k_edge = down_ref.shape[0]
    q_edge = up_ref.shape[0] - k_edge
    q_width = q_rows.shape[0] - q_edge
    k_own, q_own = k_out.shape[0], q_out.shape[0]
    k_shift, q_shift = k_own - HEAD_SIZE, q_width - q_own

    def ordered(mine, other, rows):
        a, b = mine[rows, pl.ds(0, width)], other[rows, pl.ds(0, width)]
        return jnp.where(parity == 0, a, b), jnp.where(parity == 0, b, a)

    q_rows[pl.ds(0, q_edge), :] = ordered(up_ref, up_mate_ref, pl.ds(0, q_edge))[0]
    q_rows[pl.ds(q_edge, q_width), :] = ordered(mine_ref, other_ref, pl.ds(0, q_width))[0]
    start = pl.multiple_of(q_edge - z * q_shift, 16)
    q_out[...] = q_rows[pl.ds(start, q_own), :].astype(F32)
    o_out[...] = ordered(mine_ref, other_ref, pl.ds(128, o_out.shape[0]))[1].astype(F32)
    early[...] = jnp.zeros_like(early)
    late[...] = jnp.zeros_like(late)
    start = pl.multiple_of(z * k_shift, 16)
    for which, first, edge_at, out in ((0, q_width, q_edge, k_out), (1, 0, 0, v_out)):
        early[pl.ds(k_shift, k_edge), :] = ordered(up_ref, up_mate_ref, pl.ds(edge_at, k_edge))[which]
        late[pl.ds(HEAD_SIZE, k_edge), :] = ordered(down_ref, down_mate_ref, pl.ds(0, k_edge))[which]
        rows = pl.ds(pl.multiple_of(first + start, 16), k_own)
        total = ordered(mine_ref, other_ref, rows)[which].astype(F32)
        out[...] = total + early[pl.ds(start, k_own), :].astype(F32) + late[pl.ds(start, k_own), :].astype(F32)


def shard_rows(place, mine, other, up, up_mate, down, down_mate, gains, q_width, q_rows, k_rows, out_rows, width):
    k_edge = down.shape[0]
    q_edge = up.shape[0] - k_edge
    whole = pl.BlockSpec(memory_space=pltpu.VMEM)
    return pl.pallas_call(
        shard_kernel,
        in_specs=[pl.BlockSpec(memory_space=pltpu.SMEM)] + [whole] * (6 + len(gains)),
        out_specs=[whole] * 5,
        out_shape=[jax.ShapeDtypeStruct((rows, width), F32) for rows in (q_rows, k_rows, k_rows, out_rows)]
        + [jax.ShapeDtypeStruct(gains[0].shape, F32)],
        scratch_shapes=[
            pltpu.VMEM((q_width + q_edge, width), BF16),
            pltpu.VMEM((2 * k_rows, width), BF16),
            pltpu.VMEM((HEAD_SIZE + 2 * k_rows, width), BF16),
        ],
        compiler_params=pltpu.CompilerParams(vmem_limit_bytes=VMEM_LIMIT),
        cost_estimate=SHORT,
        name="shard_rows",
    )(place, mine, other, up, up_mate, down, down_mate, *gains)


def mate(x):
    return lax.ppermute(x, "core", [(0, 1), (1, 0)])


def across(x, by):
    return lax.ppermute(x, "pair", [(i, i ^ by) for i in range(lax.axis_size("pair"))])


def everywhere(x):
    return [x] + [across(x, by) for by in range(1, lax.axis_size("pair"))]


def pick(x, index, axis=0):
    return lax.dynamic_index_in_dim(x, index, axis, keepdims=False)


def pair_sum(x, parity):
    return (pick(x, parity).astype(F32) + mate(pick(x, 1 - parity)).astype(F32)).astype(BF16)


def add_up(pieces):
    total = pieces[0].astype(F32)
    for one in pieces[1:]:
        total = total + one.astype(F32)
    return total


def rotate(x, shift):
    nf = lax.axis_size("fsdp")
    return lax.ppermute(x, "fsdp", [(i, (i + shift) % nf) for i in range(nf)])


def after(x, *others):
    return lax.optimization_barrier((x, *others))[0]


def local(
    tokens,
    doc_lengths,
    block_table,
    attn_gain,
    w_query,
    key_weight,
    value_weight,
    w_out,
    mlp_gain,
    w_gate,
    w_up,
    w_down,
    out_cotangent,
):
    nf, chips, nc = lax.axis_size("fsdp"), lax.axis_size("pair"), lax.axis_size(CTX)
    z, parity, chip = lax.axis_index("fsdp"), lax.axis_index("core"), lax.axis_index("pair")
    c = 2 * chip + parity
    seqs, piece, width = tokens.shape
    rows = nf * piece
    half_len = HEAD_SIZE // 2
    up = [(i, i + 1) for i in range(nf - 1)]
    down = [(i + 1, i) for i in range(nf - 1)]

    heads = -(-QUERY_HEADS // nf)
    q_rows, k_rows = w_query.shape[0], key_weight.shape[0]
    q_width, k_width = heads * HEAD_SIZE, 2 * HEAD_SIZE
    q_shift = q_width - q_rows
    k_shift = k_rows - HEAD_SIZE
    q_edge, k_edge = q_shift * (nf - 1), k_shift * (nf - 1)
    head_index = jnp.arange(heads, dtype=jnp.int32)
    half = jnp.minimum((z * heads + head_index) // GROUP - z, 1).astype(jnp.int32)

    block = piece // 2
    pairs = block_table.shape[0]
    within = jnp.arange(block, dtype=jnp.int32)

    def positions_of(table):
        paired = jnp.stack([table, 2 * pairs - 1 - table], axis=1)
        return (paired[:, :, None] * block + within).reshape(-1)

    group_pos = positions_of(lax.dynamic_slice_in_dim(block_table.astype(jnp.int32), c * nf, nf, 0))
    frequency = ROPE_BASE ** (-(2.0 * jnp.arange(half_len, dtype=F32)) / HEAD_SIZE)
    angles = group_pos.astype(F32)[:, None] * frequency[None, :]
    cos, sin = jnp.cos(angles), jnp.sin(angles)
    cosine = jnp.concatenate([cos, cos, cos, cos], axis=1).reshape(nf, piece, 128)
    sine = jnp.concatenate([-sin, sin, -sin, sin], axis=1).reshape(nf, piece, 128)
    cosine_all, sine_all = jnp.concatenate([cosine] * seqs, axis=1), jnp.concatenate([sine] * seqs, axis=1)

    own_tokens = seqs * piece
    group_tokens = nf * own_tokens
    own_cotangent = out_cotangent.reshape(own_tokens, width)
    from_next = lax.ppermute(
        jnp.concatenate([w_query[:q_edge], key_weight[:k_edge], value_weight[:k_edge]], axis=0),
        "fsdp",
        down,
    )
    from_prev = lax.ppermute(
        jnp.concatenate([key_weight[k_rows - k_edge :], value_weight[k_rows - k_edge :]], axis=0),
        "fsdp",
        up,
    )

    gain_rows = jnp.pad(jnp.stack([attn_gain, mlp_gain]), ((0, 6), (0, width - attn_gain.shape[0])))
    own_payload = jnp.concatenate([tokens.reshape(own_tokens, width), gain_rows], axis=0)
    own_payload, from_next, from_prev = lax.optimization_barrier((own_payload, from_next, from_prev))
    gathered = lax.all_gather(own_payload, "fsdp", axis=0)
    gains_all = gathered[:, own_tokens : own_tokens + 2, : attn_gain.shape[0]]
    gains_all = jnp.transpose(gains_all, (1, 0, 2)).reshape(2, width).astype(F32)

    attn_in, queries, own_kv, w_in = project_inputs(
        z, gathered, gains_all[:1], w_query, key_weight, value_weight, from_next, from_prev,
        cosine_all, sine_all, heads,
    )
    positions = positions_of(block_table.astype(jnp.int32)).reshape(nc, rows)
    even = 2 * jnp.arange(chips, dtype=jnp.int32)
    key_pos = [jnp.take(positions, c ^ (even + i), axis=0).reshape(-1) for i in range(2)]
    own_pos = key_pos[0][:rows]
    bounds = jnp.cumsum(doc_lengths, axis=1)
    reached = own_pos[None, :, None] >= bounds[:, None, :-1]
    own_start = jnp.max(jnp.where(reached, bounds[:, None, :-1], 0), axis=-1)
    place = jnp.stack([z, parity, chip]).astype(jnp.int32)
    tables = (own_pos[:, None], own_start[:, :, None], key_pos[0][None, :], key_pos[1][None, :], place, gains_all[1:])

    out_rows, units = w_out.shape[0], w_gate.shape[0]
    some = -(-out_rows // (16 * nc)) * 16
    from_row = jnp.minimum(c * some, out_rows - some)
    wide = nf * q_width
    some_out = jnp.pad(lax.dynamic_slice_in_dim(w_out, from_row, some, 0), ((0, 0), (0, wide - width)))
    some_down = lax.dynamic_slice_in_dim(w_down, from_row, some, 0)
    some_out, some_down = lax.optimization_barrier((some_out, some_down, gathered))[:2]
    pieces = []
    for shift in range(nf):
        columns = lax.dynamic_slice_in_dim(some_down, lax.rem(z + shift, nf) * units, units, 1)
        piece_out = jnp.concatenate([some_out, columns], axis=1)
        pieces.append(rotate(piece_out, shift) if shift else piece_out)
    late_cotangent, _, _, tables = lax.optimization_barrier((own_cotangent, own_kv, pieces, tables))
    cotangent = lax.all_gather(late_cotangent, "fsdp", axis=0)
    parts = everywhere(jnp.stack(pieces))
    same_core, cotangent, parts = lax.optimization_barrier((everywhere(own_kv), cotangent, parts))
    same_core = jnp.concatenate(same_core, axis=0)
    kv = [half_kv.reshape(-1, seqs, piece, 2 * k_width) for half_kv in (same_core, mate(same_core))]
    queries = queries.reshape(nf, seqs, piece, q_width)

    gate_turned, up_turned = w_gate.T, w_up.T

    mixed_own, lse = attention_forward(half, queries, kv, *tables[:4])
    parts = after(parts, mixed_own)
    parts = parts + [mate(part) for part in parts]
    mixed_rows = after(mixed_own.reshape(group_tokens, q_width), parts[:chips])
    main_rows = group_tokens - 16
    side = jnp.stack([mixed_rows[main_rows:]] + [rotate(mixed_rows[main_rows:], shift) for shift in range(1, nf)])
    main = lax.all_gather(mixed_rows[:main_rows], "fsdp", axis=0)

    place, mlp_gain_row = tables[4:]
    (
        residual, mixed, w_out_heads, mlp_in, hidden, grad_gate_pre, grad_up_pre, grad_mlp_part, layer_part,
    ) = feed_forward(
        place, main, side, gathered, parts, mlp_gain_row, gate_turned, up_turned, cotangent
    )
    mixed = mixed[:, : QUERY_HEADS * HEAD_SIZE]

    def exchange(part):
        swapped = lax.all_to_all(part, "fsdp", 0, 0, tiled=True)
        return jnp.sum(swapped.astype(F32), axis=0)[:, :width]

    grad_mlp_in = exchange(grad_mlp_part)
    inv_mlp = lax.rsqrt(jnp.mean(residual * residual, axis=-1, keepdims=True) + EPSILON)
    normed_mlp = residual * inv_mlp
    scaled = grad_mlp_in * gains_all[1]
    grad_gain_mlp = jnp.sum(grad_mlp_in * normed_mlp, axis=0)
    grad_residual = own_cotangent.astype(F32) + inv_mlp * (
        scaled - normed_mlp * jnp.mean(scaled * normed_mlp, axis=-1, keepdims=True)
    )
    part_rows = -(-(width // 2) // (16 * chips)) * 16
    keep, give = feed_forward_grads(
        place, mlp_in, grad_gate_pre, grad_up_pre, cotangent.reshape(group_tokens, width), hidden, part_rows * chips
    )
    made_pair = (keep.astype(F32) + mate(give).astype(F32)).astype(BF16).reshape(3, chips, part_rows, units)
    made_pieces = [pick(made_pair, chip, 1)] + [across(pick(made_pair, chip ^ by, 1), by) for by in range(1, chips)]
    branch_own, _ = lax.optimization_barrier((grad_residual.astype(BF16), made_pair))
    grad_attn_branch = lax.all_gather(branch_own, "fsdp", axis=0, tiled=True)

    made_total = add_up(made_pieces).astype(BF16)
    grad_attn_branch, made_total = lax.optimization_barrier((grad_attn_branch, made_total))
    made_found = everywhere(made_total)
    branch = grad_attn_branch.reshape(nf, seqs, piece, width)
    grad_query_pre, *grad_kv = attention_backward(
        half, queries, mixed_own, branch, w_out_heads, lse, kv, tables[2:4], own_pos, own_start, cosine_all, sine_all
    )
    layer_part = lax.all_to_all(after(layer_part, grad_attn_branch), "fsdp", 0, 0, tiled=True)

    grad_kv, made_found, layer_part = lax.optimization_barrier((grad_kv, made_found, layer_part))
    taken = [own.reshape(chips, nf, own_tokens, 2 * k_width) for own in (grad_kv[0], mate(grad_kv[1]))]
    pair = taken[0][0].astype(F32) + taken[1][0].astype(F32)
    pair_low = [(taken[0][by].astype(F32) + taken[1][by].astype(F32)).astype(BF16) for by in range(1, chips)]
    made_found = after(made_found, pair_low)
    others = [across(pair_low[by - 1], by) for by in range(1, chips)]
    grad_attn_own = lax.dynamic_slice_in_dim(grad_attn_branch, z * out_rows, out_rows, 1)
    grad_out_w = tn(grad_attn_own, mixed).astype(BF16)
    grad_gate_w, grad_up_w, down_own = finish(place, made_found, [mate(found) for found in made_found], width)
    others, grad_gate_w, grad_up_w, down_own = lax.optimization_barrier((others, grad_gate_w, grad_up_w, down_own))
    half_rows = max(q_width + k_width, k_width + out_rows + 16)
    half_rows = -(-half_rows // (16 * chips)) * 16 * chips
    keep, give, grad_attn_part = project_outputs(
        place, grad_query_pre.reshape(nf, own_tokens, q_width), pair, others, cosine_all, sine_all, attn_in, w_in, gathered,
        grad_out_w, grad_gain_mlp[None], half_rows,
    )

    sent_pair = (keep.astype(F32) + mate(give).astype(F32)).astype(BF16)
    sent_pair = sent_pair.reshape(chips, half_rows // chips, -1)
    sent_pieces = [pick(sent_pair, chip)] + [across(pick(sent_pair, chip ^ by), by) for by in range(1, chips)]
    swapped = lax.all_to_all(grad_attn_part, "fsdp", 0, 0, tiled=True)

    blocks = nf // 2
    down_own = after(down_own, sent_pair).reshape(blocks, out_rows, units)
    down_found = [pick(down_own, lax.rem(z, blocks))]
    for shift in range(1, nf):
        sent_block = pick(down_own, lax.rem(z + shift, nf) - blocks * parity)
        links = [
            (p * nf + i, p * nf + (i + shift) % nf) for p in range(2) for i in range(nf) if (i + shift) % nf // blocks == p
        ]
        down_found.append(lax.ppermute(sent_block, ("core", "fsdp"), links))
    sent_total = add_up(sent_pieces).astype(BF16)
    mine = lax.all_gather(sent_total, "pair", axis=0, tiled=True)
    other = mate(mine)

    edge_rows = jnp.zeros((q_edge, mine.shape[1]), BF16)
    upward = jnp.where(
        parity == 0,
        jnp.concatenate([mine[q_width - q_edge : q_width], mine[q_width + k_width - k_edge : q_width + k_width]]),
        jnp.concatenate([mine[k_width - k_edge : k_width], edge_rows]),
    )
    downward = jnp.where(parity == 0, mine[q_width : q_width + k_edge], mine[:k_edge])
    upward, downward = lax.ppermute(upward, "fsdp", up), lax.ppermute(downward, "fsdp", down)
    gain_width = attn_gain.shape[0]
    gain_row = k_width + out_rows
    gains = jnp.where(parity == 0, other[gain_row : gain_row + 2, :width], mine[gain_row : gain_row + 2, :width])
    gains = gains.astype(F32).reshape(2, nf, gain_width)
    grad_gains = [pick(gains, z, 1)] + [rotate(pick(gains, lax.rem(z + shift, nf), 1), shift) for shift in range(1, nf)]
    grad_query_w, grad_key_w, grad_value_w, grad_out_w, gains = shard_rows(
        place, mine, other, upward, mate(upward), downward, mate(downward), grad_gains, q_width, q_rows, k_rows, out_rows, width
    )

    swapped = after(swapped, sent_total)
    grad_attn_in = add_up([pick(swapped, i) for i in range(nf)])[:, :width]
    own_x = tokens.reshape(own_tokens, width).astype(F32)
    inv_attn = lax.rsqrt(jnp.mean(own_x * own_x, axis=-1, keepdims=True) + EPSILON)
    normed_attn = own_x * inv_attn
    scaled = grad_attn_in * gains_all[0]
    grad_tokens = (
        grad_residual
        + inv_attn * (scaled - normed_attn * jnp.mean(scaled * normed_attn, axis=-1, keepdims=True))
    ).astype(BF16)

    layer_part = after(layer_part, sent_pair)
    layer_out = (residual + jnp.sum(layer_part.astype(F32), axis=0)[:, :width]).astype(BF16)
    down_found = after(down_found, mine)
    down_mate = after([mate(found) for found in down_found], grad_gains)
    grad_down_w = finish_down(place, down_found, down_mate)
    return (
        layer_out.reshape(tokens.shape),
        grad_tokens.reshape(tokens.shape),
        gains[0],
        grad_query_w,
        grad_key_w,
        grad_value_w,
        grad_out_w,
        gains[1],
        grad_gate_w.T,
        grad_up_w.T,
        grad_down_w,
    )


def solution(mesh):
    count, members = mesh.shape["ctx"], mesh.shape["fsdp"]
    paired = jax.sharding.Mesh(mesh.devices.reshape(count // 2, 2, members), ("pair", "core", "fsdp"))
    rows = P(None, ("pair", "core", "fsdp"), None)
    gain, weight = P("fsdp"), P("fsdp", None)
    return jax.shard_map(
        local,
        mesh=paired,
        in_specs=(rows, P(), P(), gain, weight, weight, weight, weight, gain, weight, weight, weight, rows),
        out_specs=(rows, rows, gain, weight, weight, weight, weight, gain, weight, weight, weight),
        check_vma=False,
    )
```

```python
import functools

import jax
import jax.numpy as jnp
from jax import lax
from jax.experimental import pallas as pl
from jax.experimental.pallas import tpu as pltpu
from jax.sharding import PartitionSpec as P

QUERY_HEADS = 15
KEY_VALUE_HEADS = 5
HEAD_SIZE = 64
GROUP = QUERY_HEADS // KEY_VALUE_HEADS
NEGATIVE = -1e30
EPSILON = 1e-05
ROPE_BASE = 10000.0
SCALE = HEAD_SIZE ** (-0.5)
BF16 = jnp.bfloat16
F32 = jnp.float32
VMEM_LIMIT = 56 * 1024 * 1024
SHORT = pl.CostEstimate(flops=1000000, bytes_accessed=1000000, transcendentals=0)
CTX = ("pair", "core")
FORWARD_ROWS, FORWARD_UNROLL = 512, 2
BACKWARD_BLOCKS, BACKWARD_UNROLL = 8, 2


def nt(a, b):
    return lax.dot_general(a, b, (((1,), (1,)), ((), ())), preferred_element_type=F32)


def nn(a, b):
    return lax.dot_general(a, b, (((1,), (0,)), ((), ())), preferred_element_type=F32)


def tn(a, b):
    return lax.dot_general(a, b, (((0,), (0,)), ((), ())), preferred_element_type=F32)


def spread(pair, head, half):
    lane = lax.broadcasted_iota(jnp.int32, pair.shape, 1)
    here = (lane // HEAD_SIZE) == (head % 2)
    alone = jnp.where(here, pair, jnp.zeros_like(pair))
    return jnp.where(half == head % 2, alone, pltpu.roll(alone, HEAD_SIZE, 1))


def collect(first, second, half_first, half_second):
    lane = lax.broadcasted_iota(jnp.int32, first.shape, 1)
    low = jnp.where(half_first == 0, first, pltpu.roll(first, HEAD_SIZE, 1))
    high = jnp.where(half_second == 1, second, pltpu.roll(second, HEAD_SIZE, 1))
    return jnp.where(lane < HEAD_SIZE, low, high)


def swap_lanes(x):
    lane = lax.broadcasted_iota(jnp.int32, x.shape, 1)
    half_len = HEAD_SIZE // 2
    first = (lane % HEAD_SIZE) < half_len
    return jnp.where(first, pltpu.roll(x, x.shape[1] - half_len, 1), pltpu.roll(x, half_len, 1))


def input_kernel(
    place_ref,
    gathered_ref,
    gain_ref,
    q_ref,
    k_ref,
    v_ref,
    next_ref,
    prev_ref,
    cos_ref,
    sin_ref,
    attn_out,
    turned_out,
    kv_out,
    weight_out,
    q_rows,
    k_rows,
):
    z = place_ref[0]
    members, piece = attn_out.shape[0], attn_out.shape[1]
    q_width, k_width = turned_out.shape[2], kv_out.shape[2] // 2
    q_own, k_own = q_ref.shape[0], k_ref.shape[0]
    k_edge = prev_ref.shape[0] // 2
    q_edge = next_ref.shape[0] - 2 * k_edge
    q_shift, k_shift = q_edge // (members - 1), k_edge // (members - 1)

    q_rows[pl.ds(0, q_own), :] = q_ref[...]
    q_rows[pl.ds(q_own, q_edge), :] = next_ref[pl.ds(0, q_edge), :]
    rest = q_rows.shape[0] - q_own - q_edge
    q_rows[pl.ds(q_own + q_edge, rest), :] = jnp.zeros((rest, q_rows.shape[1]), BF16)
    start = pl.multiple_of(z * q_shift, 16)
    weight_out[pl.ds(0, q_width), :] = q_rows[pl.ds(start, q_width), :]
    for i, own in enumerate((k_ref, v_ref)):
        k_rows[pl.ds(0, k_edge), :] = prev_ref[pl.ds(i * k_edge, k_edge), :]
        k_rows[pl.ds(k_edge, k_own), :] = own[...]
        k_rows[pl.ds(k_edge + k_own, k_edge), :] = next_ref[pl.ds(q_edge + i * k_edge, k_edge), :]
        start = pl.multiple_of(k_edge - z * k_shift, 16)
        weight_out[pl.ds(q_width + i * k_width, k_width), :] = k_rows[pl.ds(start, k_width), :]

    gain = gain_ref[...]

    def one(j, _):
        x = gathered_ref[j, pl.ds(0, piece), :].astype(F32)
        inverse = lax.rsqrt(jnp.mean(x * x, axis=1, keepdims=True) + EPSILON)
        attn_out[j] = (x * inverse * gain).astype(BF16)
        made = nt(attn_out[j], weight_out[...])
        for i in range((q_width + k_width) // 128):
            part = made[:, i * 128 : (i + 1) * 128]
            part = (part * cos_ref[j] + swap_lanes(part) * sin_ref[j]).astype(BF16)
            if i < q_width // 128:
                turned_out[j, :, pl.ds(i * 128, 128)] = part
            else:
                kv_out[j, :, pl.ds(i * 128 - q_width, 128)] = part
        kv_out[j, :, pl.ds(k_width, k_width)] = made[:, q_width + k_width :].astype(BF16)
        return 0

    lax.fori_loop(0, members, one, 0)


def project_inputs(z, gathered, gain, w_query, key_weight, value_weight, from_next, from_prev, cosine, sine, heads):
    members, width = gathered.shape[0], gathered.shape[2]
    piece = cosine.shape[1]
    q_width, k_width = heads * HEAD_SIZE, 2 * HEAD_SIZE
    k_edge = from_prev.shape[0] // 2
    whole = pl.BlockSpec(memory_space=pltpu.VMEM)
    return pl.pallas_call(
        input_kernel,
        in_specs=[pl.BlockSpec(memory_space=pltpu.SMEM)] + [whole] * 9,
        out_specs=[whole] * 4,
        out_shape=[
            jax.ShapeDtypeStruct((members, piece, width), BF16),
            jax.ShapeDtypeStruct((members, piece, q_width), BF16),
            jax.ShapeDtypeStruct((members, piece, 2 * k_width), BF16),
            jax.ShapeDtypeStruct((q_width + 2 * k_width, width), BF16),
        ],
        scratch_shapes=[
            pltpu.VMEM((q_width + from_next.shape[0] - 2 * k_edge, width), BF16),
            pltpu.VMEM((key_weight.shape[0] + 2 * k_edge, width), BF16),
        ],
        compiler_params=pltpu.CompilerParams(vmem_limit_bytes=VMEM_LIMIT),
        cost_estimate=pl.CostEstimate(
            flops=2 * members * piece * width * (q_width + 2 * k_width), bytes_accessed=6000000, transcendentals=0
        ),
        name="project_inputs",
    )(
        jnp.reshape(z, (1,)).astype(jnp.int32),
        gathered,
        gain,
        w_query,
        key_weight,
        value_weight,
        from_next,
        from_prev,
        cosine,
        sine,
    )


def flat(x):
    return x.reshape(-1, x.shape[-1])


def forward_kernel(
    half_ref, q_ref, k_ref, v_ref, k2_ref, v2_ref, kpos_ref, kpos2_ref, qpos_ref, qstart_ref,
    o_ref, lse_ref, q4, bias, m, l, acc,
):
    step, steps = pl.program_id(1), pl.num_programs(1)
    rows = q_ref.shape[0] * q_ref.shape[2]
    heads = q4.shape[0] // rows
    chunk = max(rows, min(FORWARD_ROWS, heads * rows))

    @pl.when(step == 0)
    def _():
        for h in range(heads):
            pair = flat(q_ref[:, 0, :, pl.ds((h // 2) * 128, 128)]).astype(F32) * SCALE
            q4[pl.ds(h * rows, rows), :] = spread(pair, h, half_ref[h]).astype(BF16)
        m[...] = jnp.full_like(m, NEGATIVE)
        l[...] = jnp.zeros_like(l)
        acc[...] = jnp.zeros_like(acc)

    kpos = jnp.concatenate([kpos_ref[...], kpos2_ref[...]], axis=1)
    seen = (kpos <= qpos_ref[...]) & (kpos >= qstart_ref[0])
    bias[...] = jnp.where(seen, 0.0, NEGATIVE)
    keys = jnp.concatenate([flat(k_ref[:, 0]), flat(k2_ref[:, 0])], axis=0)
    values = jnp.concatenate([flat(v_ref[:, 0]), flat(v2_ref[:, 0])], axis=0)

    def one(i, _):
        at = pl.multiple_of(i * chunk, chunk)
        s = nt(q4[pl.ds(at, chunk), :], keys) + jnp.concatenate([bias[...]] * (chunk // rows), axis=0)
        old = m[pl.ds(at, chunk), :]
        new = jnp.maximum(old, jnp.max(s, axis=1, keepdims=True))
        p = jnp.exp(s - new)
        factor = jnp.exp(old - new)
        m[pl.ds(at, chunk), :] = new
        l[pl.ds(at, chunk), :] = l[pl.ds(at, chunk), :] * factor + jnp.sum(p, axis=1, keepdims=True)
        acc[pl.ds(at, chunk), :] = acc[pl.ds(at, chunk), :] * factor + nn(p.astype(BF16), values)
        return 0

    lax.fori_loop(0, heads * rows // chunk, one, 0, unroll=FORWARD_UNROLL)

    @pl.when(step == steps - 1)
    def _():
        total = l[...]
        lse = m[...] + jnp.log(total)
        for i in range(heads * rows // 128):
            part = jnp.broadcast_to(lse[i * 128 : (i + 1) * 128], (128, 128))
            lse_ref[0, :, pl.ds(i * 128, 128)] = part.T[0:1, :]
        out = acc[...] / total
        for h in range(0, heads, 2):
            both = collect(
                out[h * rows : (h + 1) * rows],
                out[(h + 1) * rows : (h + 2) * rows],
                half_ref[h],
                half_ref[h + 1],
            )
            both = both.astype(BF16).reshape(o_ref.shape[0], o_ref.shape[2], 128)
            o_ref[:, 0, :, pl.ds((h // 2) * 128, 128)] = both


def backward_kernel(
    half_ref,
    q_ref,
    o_ref,
    branch_ref,
    w_ref,
    lse_ref,
    k_ref,
    v_ref,
    k2_ref,
    v2_ref,
    kpos_ref,
    kpos2_ref,
    qpos_ref,
    qstart_ref,
    cos_ref,
    sin_ref,
    dq_ref,
    dkv_ref,
    dkv2_ref,
    q4,
    do4,
    delta,
    dq,
):
    step, steps = pl.program_id(1), pl.num_programs(1)
    rows = q_ref.shape[0] * q_ref.shape[2]
    piece = k_ref.shape[2]
    heads = q4.shape[0] // rows
    blocks = min(BACKWARD_BLOCKS, k_ref.shape[0])
    chunk = blocks * piece

    @pl.when(step == 0)
    def _():
        grad_mixed = nn(flat(branch_ref[:, 0]), w_ref[...]).astype(BF16).astype(F32)
        for h in range(heads):
            lanes = pl.ds((h // 2) * 128, 128)
            pair = flat(q_ref[:, 0, :, lanes]).astype(F32) * SCALE
            q4[pl.ds(h * rows, rows), :] = spread(pair, h, half_ref[h]).astype(BF16)
            grad = grad_mixed[:, (h // 2) * 128 : (h // 2 + 1) * 128]
            wide = spread(grad, h, half_ref[h])
            do4[pl.ds(h * rows, rows), :] = wide.astype(BF16)
            lane = lax.broadcasted_iota(jnp.int32, grad.shape, 1)
            mine = (lane // HEAD_SIZE) == (h % 2)
            both = jnp.where(mine, grad * flat(o_ref[:, 0, :, lanes]).astype(F32), 0.0)
            total = jnp.sum(both, axis=1, keepdims=True)
            for i in range(rows // 128):
                part = jnp.broadcast_to(total[i * 128 : (i + 1) * 128], (128, 128))
                delta[:, pl.ds(h * rows + i * 128, 128)] = part.T[0:1, :]
        dq[...] = jnp.zeros_like(dq)

    lse = lse_ref[0]
    row_delta = delta[...]
    qpos, qstart = qpos_ref[...], qstart_ref[0]

    def one(k, v, positions, out, i):
        at = pl.multiple_of(i * chunk, chunk)
        keys = flat(k[pl.ds(i * blocks, blocks), 0])
        values = flat(v[pl.ds(i * blocks, blocks), 0])
        kpos = jnp.broadcast_to(positions[:, pl.ds(at, chunk)].astype(F32), (128, chunk)).T[:, :1].astype(jnp.int32)
        seen = (kpos <= qpos) & (kpos >= qstart)
        bias = jnp.where(seen, 0.0, NEGATIVE)
        bias = jnp.concatenate([bias] * heads, axis=1)
        p = jnp.exp(nt(keys, q4[...]) + bias - lse)
        dv = nn(p.astype(BF16), do4[...]).astype(BF16)
        ds = (p * (nt(values, do4[...]) - row_delta)).astype(BF16)
        dk = nn(ds, q4[...]).astype(BF16)
        out[pl.ds(i * blocks, blocks), 0, :, pl.ds(0, 128)] = dk.reshape(blocks, piece, 128)
        out[pl.ds(i * blocks, blocks), 0, :, pl.ds(128, 128)] = dv.reshape(blocks, piece, 128)
        dq[...] += tn(ds, keys)

    def both(i, _):
        one(k_ref, v_ref, kpos_ref, dkv_ref, i)
        one(k2_ref, v2_ref, kpos2_ref, dkv2_ref, i)
        return 0

    lax.fori_loop(0, k_ref.shape[0] // blocks, both, 0, unroll=BACKWARD_UNROLL)

    @pl.when(step == steps - 1)
    def _():
        cosine, sine = flat(cos_ref[...]), flat(sin_ref[...])
        for h in range(0, heads, 2):
            both = collect(
                dq[pl.ds(h * rows, rows), :],
                dq[pl.ds((h + 1) * rows, rows), :],
                half_ref[h],
                half_ref[h + 1],
            )
            both = both * SCALE
            back = (both * cosine - swap_lanes(both) * sine).astype(BF16)
            dq_ref[:, 0, :, pl.ds((h // 2) * 128, 128)] = back.reshape(dq_ref.shape[0], dq_ref.shape[2], 128)


def key_step(owners, piece):
    most = max(1, 1024 // piece)
    return most if owners % most == 0 else owners


def attention_forward(half, queries, kv, own_pos, own_start, key_pos, key_pos2):
    members, seqs, piece, width = queries.shape
    owners = kv[0].shape[0]
    rows, count = members * piece, 2 * owners * piece
    step = key_step(owners, piece)
    heads = width // HEAD_SIZE
    own = pl.BlockSpec((members, 1, piece, width), lambda s, b: (0, s, 0, 0))
    keys = pl.BlockSpec((step, 1, piece, 128), lambda s, b: (b, s, 0, 0))
    values = pl.BlockSpec((step, 1, piece, 128), lambda s, b: (b, s, 0, 1))
    places = pl.BlockSpec((1, step * piece), lambda s, b: (0, b))
    return pl.pallas_call(
        forward_kernel,
        grid=(seqs, owners // step),
        in_specs=[
            pl.BlockSpec(memory_space=pltpu.SMEM),
            own,
            keys,
            values,
            keys,
            values,
            places,
            places,
            pl.BlockSpec((rows, 1), lambda s, b: (0, 0)),
            pl.BlockSpec((1, rows, 1), lambda s, b: (s, 0, 0)),
        ],
        out_specs=[own, pl.BlockSpec((1, 1, heads * rows), lambda s, b: (s, 0, 0))],
        out_shape=[
            jax.ShapeDtypeStruct(queries.shape, BF16),
            jax.ShapeDtypeStruct((seqs, 1, heads * rows), F32),
        ],
        scratch_shapes=[
            pltpu.VMEM((heads * rows, 128), BF16),
            pltpu.VMEM((rows, 2 * step * piece), F32),
            pltpu.VMEM((heads * rows, 1), F32),
            pltpu.VMEM((heads * rows, 1), F32),
            pltpu.VMEM((heads * rows, 128), F32),
        ],
        compiler_params=pltpu.CompilerParams(
            dimension_semantics=("arbitrary", "arbitrary"), vmem_limit_bytes=VMEM_LIMIT
        ),
        cost_estimate=SHORT,
        name="attention_forward",
    )(
        half,
        queries,
        kv[0],
        kv[0],
        kv[1],
        kv[1],
        key_pos,
        key_pos2,
        own_pos,
        own_start,
    )


def attention_backward(half, queries, mixed, branch, w_heads, lse, kv, key_pos, own_pos, own_start, cosine, sine):
    members, seqs, piece, width = queries.shape
    owners = kv[0].shape[0]
    rows, count = members * piece, 2 * owners * piece
    step = key_step(owners, piece)
    heads = width // HEAD_SIZE
    own = pl.BlockSpec((members, 1, piece, width), lambda s, b: (0, s, 0, 0))
    table = pl.BlockSpec((members, piece, 128), lambda s, b: (0, 0, 0))
    keys = pl.BlockSpec((step, 1, piece, 128), lambda s, b: (b, s, 0, 0))
    values = pl.BlockSpec((step, 1, piece, 128), lambda s, b: (b, s, 0, 1))
    places = pl.BlockSpec((1, step * piece), lambda s, b: (0, b))
    made = pl.BlockSpec((step, 1, piece, 256), lambda s, b: (b, s, 0, 0))
    return pl.pallas_call(
        backward_kernel,
        grid=(seqs, owners // step),
        in_specs=[
            pl.BlockSpec(memory_space=pltpu.SMEM),
            own,
            own,
            pl.BlockSpec((members, 1, piece, branch.shape[3]), lambda s, b: (0, s, 0, 0)),
            pl.BlockSpec(w_heads.shape, lambda s, b: (0, 0)),
            pl.BlockSpec((1, 1, heads * rows), lambda s, b: (s, 0, 0)),
            keys,
            values,
            keys,
            values,
            places,
            places,
            pl.BlockSpec((1, rows), lambda s, b: (0, 0)),
            pl.BlockSpec((1, 1, rows), lambda s, b: (s, 0, 0)),
            table,
            table,
        ],
        out_specs=[own, made, made],
        out_shape=[
            jax.ShapeDtypeStruct(queries.shape, BF16),
            jax.ShapeDtypeStruct(kv[0].shape, BF16),
            jax.ShapeDtypeStruct(kv[1].shape, BF16),
        ],
        scratch_shapes=[
            pltpu.VMEM((heads * rows, 128), BF16),
            pltpu.VMEM((heads * rows, 128), BF16),
            pltpu.VMEM((1, heads * rows), F32),
            pltpu.VMEM((heads * rows, 128), F32),
        ],
        compiler_params=pltpu.CompilerParams(
            dimension_semantics=("arbitrary", "arbitrary"), vmem_limit_bytes=VMEM_LIMIT
        ),
        cost_estimate=SHORT,
        name="attention_backward",
    )(
        half,
        queries,
        mixed,
        branch,
        w_heads,
        lse,
        kv[0],
        kv[0],
        kv[1],
        kv[1],
        *key_pos,
        own_pos[None, :],
        own_start[:, None, :],
        cosine,
        sine,
    )


def feed_forward_kernel(
    place_ref,
    main_ref,
    side_ref,
    tokens_ref,
    gain_ref,
    gate_ref,
    up_ref,
    cotangent_ref,
    *refs,
):
    parts, refs = refs[:-12], refs[-12:]
    residual_out, mixed_out, heads_out, mlp_out, hidden_out, gate_out, up_out, part_out, layer_out = refs[:9]
    w_out, w_down, residual = refs[9:]
    members, chips = main_ref.shape[0], len(parts) // 2
    z, parity, chip = place_ref[0], place_ref[1], place_ref[2]
    own, width, units = residual_out.shape[0], w_out.shape[0], w_down.shape[1]
    out_rows, wide = width // members, w_out.shape[1]
    lanes = wide // members
    some = parts[0].shape[1]
    for shift in range(members):
        source = lax.rem(z - shift + members, members)
        first = source * out_rows
        for q in range(chips):
            for who in range(2):
                part = parts[who * chips + q]
                index = 2 * (chip ^ q) + (parity ^ who)
                at = pl.multiple_of(first + jnp.minimum(index * some, out_rows - some), 16)
                w_out[pl.ds(at, some), :] = part[shift, :, pl.ds(0, wide)]
                w_down[pl.ds(at, some), :] = part[shift, :, pl.ds(wide, units)]
    count = main_ref.shape[1]
    for j in range(members):
        mixed_out[pl.ds(0, count), pl.ds(j * lanes, lanes)] = main_ref[j]
        shift = lax.rem(z - j + members, members)
        mixed_out[pl.ds(count, side_ref.shape[1]), pl.ds(j * lanes, lanes)] = side_ref[shift]
    heads_out[...] = w_out[:, pl.ds(pl.multiple_of(z * lanes, lanes), lanes)]


    def one(i, _):
        rows, blocks = pl.ds(pl.multiple_of(i * 2 * own, 16), 2 * own), pl.ds(2 * i, 2)
        here = flat(tokens_ref[blocks, pl.ds(0, own), :]).astype(F32) + nt(mixed_out[rows, :], w_out[...])
        residual[rows, :] = here
        inverse = lax.rsqrt(jnp.mean(here * here, axis=1, keepdims=True) + EPSILON)
        mlp_in = (here * inverse * gain_ref[...]).astype(BF16)
        mlp_out[rows, :] = mlp_in
        gate_pre = nn(mlp_in, gate_ref[...])
        up_pre = nn(mlp_in, up_ref[...])
        sigmoid_gate = jax.nn.sigmoid(gate_pre)
        silu_gate = gate_pre * sigmoid_gate
        hidden = (silu_gate * up_pre).astype(BF16)
        hidden_out[rows, :] = hidden
        grad_hidden = nn(flat(cotangent_ref[blocks]), w_down[...])
        slope = sigmoid_gate + silu_gate * (1.0 - sigmoid_gate)
        grad_gate = (grad_hidden * up_pre * slope).astype(BF16)
        grad_up = (grad_hidden * silu_gate).astype(BF16)
        gate_out[rows, :] = grad_gate
        up_out[rows, :] = grad_up
        part = nt(grad_gate, gate_ref[...]) + nt(grad_up, up_ref[...])
        part_out[blocks, :, pl.ds(0, width)] = part.astype(BF16).reshape(2, own, width)
        part_out[blocks, :, pl.ds(width, wide - width)] = jnp.zeros((2, own, wide - width), BF16)
        layer = nt(hidden, w_down[...])
        layer_out[blocks, :, pl.ds(0, width)] = layer.astype(BF16).reshape(2, own, width)
        layer_out[blocks, :, pl.ds(width, wide - width)] = jnp.zeros((2, own, wide - width), BF16)
        return 0

    lax.fori_loop(0, members // 2, one, 0)
    residual_out[...] = residual[pl.ds(pl.multiple_of(z * own, own), own), :]


def feed_forward(place, main, side, tokens, parts, gain, gate_turned, up_turned, cotangent):
    members, lanes = main.shape[0], main.shape[2]
    own, width = cotangent.shape[1:]
    rows, units, wide = members * own, gate_turned.shape[1], members * lanes
    whole = pl.BlockSpec(memory_space=pltpu.VMEM)
    return pl.pallas_call(
        feed_forward_kernel,
        in_specs=[pl.BlockSpec(memory_space=pltpu.SMEM)] + [whole] * (7 + len(parts)),
        out_specs=[whole] * 9,
        out_shape=[
            jax.ShapeDtypeStruct((own, width), F32),
            jax.ShapeDtypeStruct((rows, wide), BF16),
            jax.ShapeDtypeStruct((width, lanes), BF16),
            jax.ShapeDtypeStruct((rows, width), BF16),
            jax.ShapeDtypeStruct((rows, units), BF16),
            jax.ShapeDtypeStruct((rows, units), BF16),
            jax.ShapeDtypeStruct((rows, units), BF16),
            jax.ShapeDtypeStruct((members, own, wide), BF16),
            jax.ShapeDtypeStruct((members, own, wide), BF16),
        ],
        scratch_shapes=[
            pltpu.VMEM((width, wide), BF16),
            pltpu.VMEM((width, units), BF16),
            pltpu.VMEM((rows, width), F32),
        ],
        compiler_params=pltpu.CompilerParams(vmem_limit_bytes=VMEM_LIMIT),
        cost_estimate=SHORT,
        name="feed_forward",
    )(place, main, side, tokens, gain, gate_turned, up_turned, cotangent, *parts)


def feed_forward_grads_kernel(place_ref, mlp_ref, gate_ref, up_ref, cotangent_ref, hidden_ref, keep_out, give_out):
    parity = place_ref[1]
    count = mlp_ref.shape[1] // 2
    rest = keep_out.shape[1] - count
    for i, (x, g) in enumerate(((mlp_ref, gate_ref), (mlp_ref, up_ref), (cotangent_ref, hidden_ref))):
        made = tn(x[...], g[...]).astype(BF16)
        low, high = made[:count], made[count:]
        keep_out[i, pl.ds(0, count), :] = jnp.where(parity == 0, low, high)
        give_out[i, pl.ds(0, count), :] = jnp.where(parity == 0, high, low)
        for out in (keep_out, give_out):
            out[i, pl.ds(count, rest), :] = jnp.zeros((rest, made.shape[1]), BF16)


def feed_forward_grads(place, mlp_in, grad_gate_pre, grad_up_pre, cotangent, hidden, half_rows):
    rows, width = mlp_in.shape
    units = hidden.shape[1]
    whole = pl.BlockSpec(memory_space=pltpu.VMEM)
    return pl.pallas_call(
        feed_forward_grads_kernel,
        in_specs=[pl.BlockSpec(memory_space=pltpu.SMEM)] + [whole] * 5,
        out_specs=[whole] * 2,
        out_shape=[jax.ShapeDtypeStruct((3, half_rows, units), BF16)] * 2,
        compiler_params=pltpu.CompilerParams(vmem_limit_bytes=VMEM_LIMIT),
        cost_estimate=pl.CostEstimate(flops=6 * rows * width * units, bytes_accessed=8000000, transcendentals=0),
        name="feed_forward_grads",
    )(place, mlp_in, grad_gate_pre, grad_up_pre, cotangent, hidden)


def finish_kernel(place_ref, *refs):
    chips = (len(refs) - 3) // 2
    parts, outs = refs[:-3], refs[-3:]
    parity, chip = place_ref[1], place_ref[2]
    part = parts[0].shape[1]
    count = outs[2].shape[0]
    tail = count % part
    for who in range(2):
        first = (parity ^ who) * count
        for q in range(chips):
            at = (chip ^ q) * part
            for i in range(3 - who):
                block = parts[who * chips + q][i].astype(outs[i].dtype)
                base = at if i == 2 else first + at

                @pl.when(at + part <= count)
                def _():
                    outs[i][pl.ds(pl.multiple_of(base, 16), part), :] = block

                if tail:

                    @pl.when(at + tail == count)
                    def _():
                        outs[i][pl.ds(pl.multiple_of(base, 16), tail), :] = block[:tail]


def finish(place, found, found_mate, width):
    units = found[0].shape[2]
    whole = pl.BlockSpec(memory_space=pltpu.VMEM)
    parts = [*found, *found_mate]
    return pl.pallas_call(
        finish_kernel,
        in_specs=[pl.BlockSpec(memory_space=pltpu.SMEM)] + [whole] * len(parts),
        out_specs=[whole] * 3,
        out_shape=[jax.ShapeDtypeStruct((width, units), F32)] * 2 + [jax.ShapeDtypeStruct((width // 2, units), BF16)],
        compiler_params=pltpu.CompilerParams(vmem_limit_bytes=VMEM_LIMIT),
        cost_estimate=pl.CostEstimate(flops=0, bytes_accessed=9000000, transcendentals=0),
        name="finish",
    )(place, *parts)


def down_kernel(place_ref, *refs):
    parts, out = refs[:-1], refs[-1]
    members = len(parts) // 2
    z, parity = place_ref[0], place_ref[1]
    units = parts[0].shape[1]
    mine = z // (members // 2) == parity
    for shift in range(members):
        source = lax.rem(z - shift + members, members)
        block = jnp.where(mine, parts[shift][...], parts[members + shift][...])
        out[:, pl.ds(pl.multiple_of(source * units, 128), units)] = block.astype(F32)


def finish_down(place, found, found_mate):
    rows, units = found[0].shape
    whole = pl.BlockSpec(memory_space=pltpu.VMEM)
    return pl.pallas_call(
        down_kernel,
        in_specs=[pl.BlockSpec(memory_space=pltpu.SMEM)] + [whole] * 2 * len(found),
        out_specs=whole,
        out_shape=jax.ShapeDtypeStruct((rows, len(found) * units), F32),
        compiler_params=pltpu.CompilerParams(vmem_limit_bytes=VMEM_LIMIT),
        cost_estimate=pl.CostEstimate(flops=0, bytes_accessed=6000000, transcendentals=0),
        name="finish_down",
    )(place, *found, *found_mate)


def output_kernel(
    place_ref, dq_ref, pair_ref, cos_ref, sin_ref, attn_ref, weight_ref, tokens_ref, grad_out_ref, mlp_gain_ref, *refs
):
    others, (keep_out, give_out, part_out, pre, sent) = refs[:-5], refs[-5:]
    members, piece, width = attn_ref.shape
    q_width = dq_ref.shape[2]

    def one(j, gain):
        total = pair_ref[j]
        for other in others:
            total = total + other[j].astype(F32)
        keys = total[:, :128]
        pre[j, :, pl.ds(0, q_width)] = dq_ref[j]
        pre[j, :, pl.ds(q_width, 128)] = (keys * cos_ref[j] - swap_lanes(keys) * sin_ref[j]).astype(BF16)
        pre[j, :, pl.ds(q_width + 128, 128)] = total[:, 128:].astype(BF16)
        part = nn(pre[j], weight_ref[...])
        part_out[j, :, pl.ds(0, width)] = part.astype(BF16)
        part_out[j, :, pl.ds(width, part_out.shape[2] - width)] = jnp.zeros((piece, part_out.shape[2] - width), BF16)
        x = tokens_ref[j, pl.ds(0, piece), :].astype(F32)
        inverse = lax.rsqrt(jnp.mean(x * x, axis=1, keepdims=True) + EPSILON)
        return gain + jnp.sum(part * (x * inverse), axis=0, keepdims=True)

    gain = lax.fori_loop(0, members, one, jnp.zeros((1, width), F32))
    half_rows = keep_out.shape[0]
    low = q_width + 128
    out_rows = grad_out_ref.shape[0]
    lanes = pl.ds(0, width)
    sent[...] = jnp.zeros_like(sent)
    made = tn(flat(pre[...]), flat(attn_ref[...])).astype(BF16)
    sent[pl.ds(0, low), lanes] = made[:low]
    sent[pl.ds(half_rows, 128), lanes] = made[low:]
    sent[pl.ds(half_rows + 128, out_rows), lanes] = grad_out_ref[...]
    row = lax.broadcasted_iota(jnp.int32, (16, width), 0)
    gains = jnp.where(row == 0, gain, jnp.where(row == 1, mlp_gain_ref[...], 0.0))
    sent[pl.ds(half_rows + 128 + out_rows, 16), lanes] = gains.astype(BF16)
    parity = place_ref[1]
    keep_out[...] = sent[pl.ds(pl.multiple_of(parity * half_rows, 16), half_rows), :]
    give_out[...] = sent[pl.ds(pl.multiple_of((1 - parity) * half_rows, 16), half_rows), :]


def project_outputs(place, dq, pair, others, cosine, sine, attn_in, w_in, tokens, grad_out, gain_mlp, half_rows):
    members, piece, width = attn_in.shape
    wide = -(-width // 128) * 128
    whole = pl.BlockSpec(memory_space=pltpu.VMEM)
    return pl.pallas_call(
        output_kernel,
        in_specs=[pl.BlockSpec(memory_space=pltpu.SMEM)] + [whole] * (9 + len(others)),
        out_specs=[whole] * 3,
        out_shape=[
            jax.ShapeDtypeStruct((half_rows, wide), BF16),
            jax.ShapeDtypeStruct((half_rows, wide), BF16),
            jax.ShapeDtypeStruct((members, piece, wide), BF16),
        ],
        scratch_shapes=[
            pltpu.VMEM((members, piece, w_in.shape[0]), BF16),
            pltpu.VMEM((2 * half_rows, wide), BF16),
        ],
        compiler_params=pltpu.CompilerParams(vmem_limit_bytes=VMEM_LIMIT),
        cost_estimate=SHORT,
        name="project_outputs",
    )(place, dq, pair, cosine, sine, attn_in, w_in, tokens, grad_out, gain_mlp, *others)


def shard_kernel(
    place_ref, mine_ref, other_ref, up_ref, up_mate_ref, down_ref, down_mate_ref, *refs
):
    gains, (q_out, k_out, v_out, o_out, gains_out, q_rows, early, late) = refs[:-8], refs[-8:]
    total = gains[0][...]
    for one in gains[1:]:
        total = total + one[...]
    gains_out[...] = total
    z, parity = place_ref[0], place_ref[1]
    width = q_out.shape[1]
    k_edge = down_ref.shape[0]
    q_edge = up_ref.shape[0] - k_edge
    q_width = q_rows.shape[0] - q_edge
    k_own, q_own = k_out.shape[0], q_out.shape[0]
    k_shift, q_shift = k_own - HEAD_SIZE, q_width - q_own

    def ordered(mine, other, rows):
        a, b = mine[rows, pl.ds(0, width)], other[rows, pl.ds(0, width)]
        return jnp.where(parity == 0, a, b), jnp.where(parity == 0, b, a)

    q_rows[pl.ds(0, q_edge), :] = ordered(up_ref, up_mate_ref, pl.ds(0, q_edge))[0]
    q_rows[pl.ds(q_edge, q_width), :] = ordered(mine_ref, other_ref, pl.ds(0, q_width))[0]
    start = pl.multiple_of(q_edge - z * q_shift, 16)
    q_out[...] = q_rows[pl.ds(start, q_own), :].astype(F32)
    o_out[...] = ordered(mine_ref, other_ref, pl.ds(128, o_out.shape[0]))[1].astype(F32)
    early[...] = jnp.zeros_like(early)
    late[...] = jnp.zeros_like(late)
    start = pl.multiple_of(z * k_shift, 16)
    for which, first, edge_at, out in ((0, q_width, q_edge, k_out), (1, 0, 0, v_out)):
        early[pl.ds(k_shift, k_edge), :] = ordered(up_ref, up_mate_ref, pl.ds(edge_at, k_edge))[which]
        late[pl.ds(HEAD_SIZE, k_edge), :] = ordered(down_ref, down_mate_ref, pl.ds(0, k_edge))[which]
        rows = pl.ds(pl.multiple_of(first + start, 16), k_own)
        total = ordered(mine_ref, other_ref, rows)[which].astype(F32)
        out[...] = total + early[pl.ds(start, k_own), :].astype(F32) + late[pl.ds(start, k_own), :].astype(F32)


def shard_rows(place, mine, other, up, up_mate, down, down_mate, gains, q_width, q_rows, k_rows, out_rows, width):
    k_edge = down.shape[0]
    q_edge = up.shape[0] - k_edge
    whole = pl.BlockSpec(memory_space=pltpu.VMEM)
    return pl.pallas_call(
        shard_kernel,
        in_specs=[pl.BlockSpec(memory_space=pltpu.SMEM)] + [whole] * (6 + len(gains)),
        out_specs=[whole] * 5,
        out_shape=[jax.ShapeDtypeStruct((rows, width), F32) for rows in (q_rows, k_rows, k_rows, out_rows)]
        + [jax.ShapeDtypeStruct(gains[0].shape, F32)],
        scratch_shapes=[
            pltpu.VMEM((q_width + q_edge, width), BF16),
            pltpu.VMEM((2 * k_rows, width), BF16),
            pltpu.VMEM((HEAD_SIZE + 2 * k_rows, width), BF16),
        ],
        compiler_params=pltpu.CompilerParams(vmem_limit_bytes=VMEM_LIMIT),
        cost_estimate=SHORT,
        name="shard_rows",
    )(place, mine, other, up, up_mate, down, down_mate, *gains)


def mate(x):
    return lax.ppermute(x, "core", [(0, 1), (1, 0)])


def across(x, by):
    return lax.ppermute(x, "pair", [(i, i ^ by) for i in range(lax.axis_size("pair"))])


def everywhere(x):
    return [x] + [across(x, by) for by in range(1, lax.axis_size("pair"))]


def pick(x, index, axis=0):
    return lax.dynamic_index_in_dim(x, index, axis, keepdims=False)


def pair_sum(x, parity):
    return (pick(x, parity).astype(F32) + mate(pick(x, 1 - parity)).astype(F32)).astype(BF16)


def add_up(pieces):
    total = pieces[0].astype(F32)
    for one in pieces[1:]:
        total = total + one.astype(F32)
    return total


def rotate(x, shift):
    nf = lax.axis_size("fsdp")
    return lax.ppermute(x, "fsdp", [(i, (i + shift) % nf) for i in range(nf)])


def after(x, *others):
    return lax.optimization_barrier((x, *others))[0]


def local(
    tokens,
    doc_lengths,
    block_table,
    attn_gain,
    w_query,
    key_weight,
    value_weight,
    w_out,
    mlp_gain,
    w_gate,
    w_up,
    w_down,
    out_cotangent,
):
    nf, chips, nc = lax.axis_size("fsdp"), lax.axis_size("pair"), lax.axis_size(CTX)
    z, parity, chip = lax.axis_index("fsdp"), lax.axis_index("core"), lax.axis_index("pair")
    c = 2 * chip + parity
    seqs, piece, width = tokens.shape
    rows = nf * piece
    half_len = HEAD_SIZE // 2
    up = [(i, i + 1) for i in range(nf - 1)]
    down = [(i + 1, i) for i in range(nf - 1)]

    heads = -(-QUERY_HEADS // nf)
    q_rows, k_rows = w_query.shape[0], key_weight.shape[0]
    q_width, k_width = heads * HEAD_SIZE, 2 * HEAD_SIZE
    q_shift = q_width - q_rows
    k_shift = k_rows - HEAD_SIZE
    q_edge, k_edge = q_shift * (nf - 1), k_shift * (nf - 1)
    head_index = jnp.arange(heads, dtype=jnp.int32)
    half = jnp.minimum((z * heads + head_index) // GROUP - z, 1).astype(jnp.int32)

    block = piece // 2
    pairs = block_table.shape[0]
    within = jnp.arange(block, dtype=jnp.int32)

    def positions_of(table):
        paired = jnp.stack([table, 2 * pairs - 1 - table], axis=1)
        return (paired[:, :, None] * block + within).reshape(-1)

    group_pos = positions_of(lax.dynamic_slice_in_dim(block_table.astype(jnp.int32), c * nf, nf, 0))
    frequency = ROPE_BASE ** (-(2.0 * jnp.arange(half_len, dtype=F32)) / HEAD_SIZE)
    angles = group_pos.astype(F32)[:, None] * frequency[None, :]
    cos, sin = jnp.cos(angles), jnp.sin(angles)
    cosine = jnp.concatenate([cos, cos, cos, cos], axis=1).reshape(nf, piece, 128)
    sine = jnp.concatenate([-sin, sin, -sin, sin], axis=1).reshape(nf, piece, 128)
    cosine_all, sine_all = jnp.concatenate([cosine] * seqs, axis=1), jnp.concatenate([sine] * seqs, axis=1)

    own_tokens = seqs * piece
    group_tokens = nf * own_tokens
    own_cotangent = out_cotangent.reshape(own_tokens, width)
    from_next = lax.ppermute(
        jnp.concatenate([w_query[:q_edge], key_weight[:k_edge], value_weight[:k_edge]], axis=0),
        "fsdp",
        down,
    )
    from_prev = lax.ppermute(
        jnp.concatenate([key_weight[k_rows - k_edge :], value_weight[k_rows - k_edge :]], axis=0),
        "fsdp",
        up,
    )

    gain_rows = jnp.pad(jnp.stack([attn_gain, mlp_gain]), ((0, 6), (0, width - attn_gain.shape[0])))
    own_payload = jnp.concatenate([tokens.reshape(own_tokens, width), gain_rows], axis=0)
    own_payload, from_next, from_prev = lax.optimization_barrier((own_payload, from_next, from_prev))
    gathered = lax.all_gather(own_payload, "fsdp", axis=0)
    gains_all = gathered[:, own_tokens : own_tokens + 2, : attn_gain.shape[0]]
    gains_all = jnp.transpose(gains_all, (1, 0, 2)).reshape(2, width).astype(F32)

    attn_in, queries, own_kv, w_in = project_inputs(
        z, gathered, gains_all[:1], w_query, key_weight, value_weight, from_next, from_prev,
        cosine_all, sine_all, heads,
    )
    positions = positions_of(block_table.astype(jnp.int32)).reshape(nc, rows)
    even = 2 * jnp.arange(chips, dtype=jnp.int32)
    key_pos = [jnp.take(positions, c ^ (even + i), axis=0).reshape(-1) for i in range(2)]
    own_pos = key_pos[0][:rows]
    bounds = jnp.cumsum(doc_lengths, axis=1)
    reached = own_pos[None, :, None] >= bounds[:, None, :-1]
    own_start = jnp.max(jnp.where(reached, bounds[:, None, :-1], 0), axis=-1)
    place = jnp.stack([z, parity, chip]).astype(jnp.int32)
    tables = (own_pos[:, None], own_start[:, :, None], key_pos[0][None, :], key_pos[1][None, :], place, gains_all[1:])

    out_rows, units = w_out.shape[0], w_gate.shape[0]
    some = -(-out_rows // (16 * nc)) * 16
    from_row = jnp.minimum(c * some, out_rows - some)
    wide = nf * q_width
    some_out = jnp.pad(lax.dynamic_slice_in_dim(w_out, from_row, some, 0), ((0, 0), (0, wide - width)))
    some_down = lax.dynamic_slice_in_dim(w_down, from_row, some, 0)
    some_out, some_down = lax.optimization_barrier((some_out, some_down, gathered))[:2]
    pieces = []
    for shift in range(nf):
        columns = lax.dynamic_slice_in_dim(some_down, lax.rem(z + shift, nf) * units, units, 1)
        piece_out = jnp.concatenate([some_out, columns], axis=1)
        pieces.append(rotate(piece_out, shift) if shift else piece_out)
    late_cotangent, _, _, tables = lax.optimization_barrier((own_cotangent, own_kv, pieces, tables))
    cotangent = lax.all_gather(late_cotangent, "fsdp", axis=0)
    parts = everywhere(jnp.stack(pieces))
    same_core, cotangent, parts = lax.optimization_barrier((everywhere(own_kv), cotangent, parts))
    same_core = jnp.concatenate(same_core, axis=0)
    kv = [half_kv.reshape(-1, seqs, piece, 2 * k_width) for half_kv in (same_core, mate(same_core))]
    queries = queries.reshape(nf, seqs, piece, q_width)

    gate_turned, up_turned = w_gate.T, w_up.T

    mixed_own, lse = attention_forward(half, queries, kv, *tables[:4])
    parts = after(parts, mixed_own)
    parts = parts + [mate(part) for part in parts]
    mixed_rows = after(mixed_own.reshape(group_tokens, q_width), parts[:chips])
    main_rows = group_tokens - 16
    side = jnp.stack([mixed_rows[main_rows:]] + [rotate(mixed_rows[main_rows:], shift) for shift in range(1, nf)])
    main = lax.all_gather(mixed_rows[:main_rows], "fsdp", axis=0)

    place, mlp_gain_row = tables[4:]
    (
        residual, mixed, w_out_heads, mlp_in, hidden, grad_gate_pre, grad_up_pre, grad_mlp_part, layer_part,
    ) = feed_forward(
        place, main, side, gathered, parts, mlp_gain_row, gate_turned, up_turned, cotangent
    )
    mixed = mixed[:, : QUERY_HEADS * HEAD_SIZE]

    def exchange(part):
        swapped = lax.all_to_all(part, "fsdp", 0, 0, tiled=True)
        return jnp.sum(swapped.astype(F32), axis=0)[:, :width]

    grad_mlp_in = exchange(grad_mlp_part)
    inv_mlp = lax.rsqrt(jnp.mean(residual * residual, axis=-1, keepdims=True) + EPSILON)
    normed_mlp = residual * inv_mlp
    scaled = grad_mlp_in * gains_all[1]
    grad_gain_mlp = jnp.sum(grad_mlp_in * normed_mlp, axis=0)
    grad_residual = own_cotangent.astype(F32) + inv_mlp * (
        scaled - normed_mlp * jnp.mean(scaled * normed_mlp, axis=-1, keepdims=True)
    )
    part_rows = -(-(width // 2) // (16 * chips)) * 16
    keep, give = feed_forward_grads(
        place, mlp_in, grad_gate_pre, grad_up_pre, cotangent.reshape(group_tokens, width), hidden, part_rows * chips
    )
    made_pair = (keep.astype(F32) + mate(give).astype(F32)).astype(BF16).reshape(3, chips, part_rows, units)
    made_pieces = [pick(made_pair, chip, 1)] + [across(pick(made_pair, chip ^ by, 1), by) for by in range(1, chips)]
    branch_own, _ = lax.optimization_barrier((grad_residual.astype(BF16), made_pair))
    grad_attn_branch = lax.all_gather(branch_own, "fsdp", axis=0, tiled=True)

    made_total = add_up(made_pieces).astype(BF16)
    grad_attn_branch, made_total = lax.optimization_barrier((grad_attn_branch, made_total))
    made_found = everywhere(made_total)
    branch = grad_attn_branch.reshape(nf, seqs, piece, width)
    grad_query_pre, *grad_kv = attention_backward(
        half, queries, mixed_own, branch, w_out_heads, lse, kv, tables[2:4], own_pos, own_start, cosine_all, sine_all
    )
    layer_part = lax.all_to_all(after(layer_part, grad_attn_branch), "fsdp", 0, 0, tiled=True)

    grad_kv, made_found, layer_part = lax.optimization_barrier((grad_kv, made_found, layer_part))
    taken = [own.reshape(chips, nf, own_tokens, 2 * k_width) for own in (grad_kv[0], mate(grad_kv[1]))]
    pair = taken[0][0].astype(F32) + taken[1][0].astype(F32)
    pair_low = [(taken[0][by].astype(F32) + taken[1][by].astype(F32)).astype(BF16) for by in range(1, chips)]
    made_found = after(made_found, pair_low)
    others = [across(pair_low[by - 1], by) for by in range(1, chips)]
    grad_attn_own = lax.dynamic_slice_in_dim(grad_attn_branch, z * out_rows, out_rows, 1)
    grad_out_w = tn(grad_attn_own, mixed).astype(BF16)
    grad_gate_w, grad_up_w, down_own = finish(place, made_found, [mate(found) for found in made_found], width)
    others, grad_gate_w, grad_up_w, down_own = lax.optimization_barrier((others, grad_gate_w, grad_up_w, down_own))
    half_rows = max(q_width + k_width, k_width + out_rows + 16)
    half_rows = -(-half_rows // (16 * chips)) * 16 * chips
    keep, give, grad_attn_part = project_outputs(
        place, grad_query_pre.reshape(nf, own_tokens, q_width), pair, others, cosine_all, sine_all, attn_in, w_in, gathered,
        grad_out_w, grad_gain_mlp[None], half_rows,
    )

    sent_pair = (keep.astype(F32) + mate(give).astype(F32)).astype(BF16)
    sent_pair = sent_pair.reshape(chips, half_rows // chips, -1)
    sent_pieces = [pick(sent_pair, chip)] + [across(pick(sent_pair, chip ^ by), by) for by in range(1, chips)]
    swapped = lax.all_to_all(grad_attn_part, "fsdp", 0, 0, tiled=True)

    blocks = nf // 2
    down_own = after(down_own, sent_pair).reshape(blocks, out_rows, units)
    down_found = [pick(down_own, lax.rem(z, blocks))]
    for shift in range(1, nf):
        sent_block = pick(down_own, lax.rem(z + shift, nf) - blocks * parity)
        links = [
            (p * nf + i, p * nf + (i + shift) % nf) for p in range(2) for i in range(nf) if (i + shift) % nf // blocks == p
        ]
        down_found.append(lax.ppermute(sent_block, ("core", "fsdp"), links))
    sent_total = add_up(sent_pieces).astype(BF16)
    mine = lax.all_gather(sent_total, "pair", axis=0, tiled=True)
    other = mate(mine)

    edge_rows = jnp.zeros((q_edge, mine.shape[1]), BF16)
    upward = jnp.where(
        parity == 0,
        jnp.concatenate([mine[q_width - q_edge : q_width], mine[q_width + k_width - k_edge : q_width + k_width]]),
        jnp.concatenate([mine[k_width - k_edge : k_width], edge_rows]),
    )
    downward = jnp.where(parity == 0, mine[q_width : q_width + k_edge], mine[:k_edge])
    upward, downward = lax.ppermute(upward, "fsdp", up), lax.ppermute(downward, "fsdp", down)
    gain_width = attn_gain.shape[0]
    gain_row = k_width + out_rows
    gains = jnp.where(parity == 0, other[gain_row : gain_row + 2, :width], mine[gain_row : gain_row + 2, :width])
    gains = gains.astype(F32).reshape(2, nf, gain_width)
    grad_gains = [pick(gains, z, 1)] + [rotate(pick(gains, lax.rem(z + shift, nf), 1), shift) for shift in range(1, nf)]
    grad_query_w, grad_key_w, grad_value_w, grad_out_w, gains = shard_rows(
        place, mine, other, upward, mate(upward), downward, mate(downward), grad_gains, q_width, q_rows, k_rows, out_rows, width
    )

    swapped = after(swapped, sent_total)
    grad_attn_in = add_up([pick(swapped, i) for i in range(nf)])[:, :width]
    own_x = tokens.reshape(own_tokens, width).astype(F32)
    inv_attn = lax.rsqrt(jnp.mean(own_x * own_x, axis=-1, keepdims=True) + EPSILON)
    normed_attn = own_x * inv_attn
    scaled = grad_attn_in * gains_all[0]
    grad_tokens = (
        grad_residual
        + inv_attn * (scaled - normed_attn * jnp.mean(scaled * normed_attn, axis=-1, keepdims=True))
    ).astype(BF16)

    layer_part = after(layer_part, sent_pair)
    layer_out = (residual + jnp.sum(layer_part.astype(F32), axis=0)[:, :width]).astype(BF16)
    down_found = after(down_found, mine)
    down_mate = after([mate(found) for found in down_found], grad_gains)
    grad_down_w = finish_down(place, down_found, down_mate)
    return (
        layer_out.reshape(tokens.shape),
        grad_tokens.reshape(tokens.shape),
        gains[0],
        grad_query_w,
        grad_key_w,
        grad_value_w,
        grad_out_w,
        gains[1],
        grad_gate_w.T,
        grad_up_w.T,
        grad_down_w,
    )


def solution(mesh):
    count, members = mesh.shape["ctx"], mesh.shape["fsdp"]
    paired = jax.sharding.Mesh(mesh.devices.reshape(count // 2, 2, members), ("pair", "core", "fsdp"))
    rows = P(None, ("pair", "core", "fsdp"), None)
    gain, weight = P("fsdp"), P("fsdp", None)
    return jax.shard_map(
        local,
        mesh=paired,
        in_specs=(rows, P(), P(), gain, weight, weight, weight, weight, gain, weight, weight, weight, rows),
        out_specs=(rows, rows, gain, weight, weight, weight, weight, gain, weight, weight, weight),
        check_vma=False,
    )
```

```python
import functools

import jax
import jax.numpy as jnp
from jax import lax
from jax.experimental import pallas as pl
from jax.experimental.pallas import tpu as pltpu
from jax.sharding import PartitionSpec as P

QUERY_HEADS = 15
KEY_VALUE_HEADS = 5
HEAD_SIZE = 64
GROUP = QUERY_HEADS // KEY_VALUE_HEADS
NEGATIVE = -1e30
EPSILON = 1e-05
ROPE_BASE = 10000.0
SCALE = HEAD_SIZE ** (-0.5)
BF16 = jnp.bfloat16
F32 = jnp.float32
VMEM_LIMIT = 56 * 1024 * 1024
SHORT = pl.CostEstimate(flops=1000000, bytes_accessed=1000000, transcendentals=0)
CTX = ("pair", "core")
FORWARD_ROWS, FORWARD_UNROLL = 512, 2
BACKWARD_BLOCKS, BACKWARD_UNROLL = 8, 2


def nt(a, b):
    return lax.dot_general(a, b, (((1,), (1,)), ((), ())), preferred_element_type=F32)


def nn(a, b):
    return lax.dot_general(a, b, (((1,), (0,)), ((), ())), preferred_element_type=F32)


def tn(a, b):
    return lax.dot_general(a, b, (((0,), (0,)), ((), ())), preferred_element_type=F32)


def spread(pair, head, half):
    lane = lax.broadcasted_iota(jnp.int32, pair.shape, 1)
    here = (lane // HEAD_SIZE) == (head % 2)
    alone = jnp.where(here, pair, jnp.zeros_like(pair))
    return jnp.where(half == head % 2, alone, pltpu.roll(alone, HEAD_SIZE, 1))


def collect(first, second, half_first, half_second):
    lane = lax.broadcasted_iota(jnp.int32, first.shape, 1)
    low = jnp.where(half_first == 0, first, pltpu.roll(first, HEAD_SIZE, 1))
    high = jnp.where(half_second == 1, second, pltpu.roll(second, HEAD_SIZE, 1))
    return jnp.where(lane < HEAD_SIZE, low, high)


def swap_lanes(x):
    lane = lax.broadcasted_iota(jnp.int32, x.shape, 1)
    half_len = HEAD_SIZE // 2
    first = (lane % HEAD_SIZE) < half_len
    return jnp.where(first, pltpu.roll(x, x.shape[1] - half_len, 1), pltpu.roll(x, half_len, 1))


def input_kernel(
    place_ref,
    gathered_ref,
    gain_ref,
    q_ref,
    k_ref,
    v_ref,
    next_ref,
    prev_ref,
    cos_ref,
    sin_ref,
    attn_out,
    turned_out,
    kv_out,
    weight_out,
    q_rows,
    k_rows,
):
    z = place_ref[0]
    members, piece = attn_out.shape[0], attn_out.shape[1]
    q_width, k_width = turned_out.shape[2], kv_out.shape[2] // 2
    q_own, k_own = q_ref.shape[0], k_ref.shape[0]
    k_edge = prev_ref.shape[0] // 2
    q_edge = next_ref.shape[0] - 2 * k_edge
    q_shift, k_shift = q_edge // (members - 1), k_edge // (members - 1)

    q_rows[pl.ds(0, q_own), :] = q_ref[...]
    q_rows[pl.ds(q_own, q_edge), :] = next_ref[pl.ds(0, q_edge), :]
    rest = q_rows.shape[0] - q_own - q_edge
    q_rows[pl.ds(q_own + q_edge, rest), :] = jnp.zeros((rest, q_rows.shape[1]), BF16)
    start = pl.multiple_of(z * q_shift, 16)
    weight_out[pl.ds(0, q_width), :] = q_rows[pl.ds(start, q_width), :]
    for i, own in enumerate((k_ref, v_ref)):
        k_rows[pl.ds(0, k_edge), :] = prev_ref[pl.ds(i * k_edge, k_edge), :]
        k_rows[pl.ds(k_edge, k_own), :] = own[...]
        k_rows[pl.ds(k_edge + k_own, k_edge), :] = next_ref[pl.ds(q_edge + i * k_edge, k_edge), :]
        start = pl.multiple_of(k_edge - z * k_shift, 16)
        weight_out[pl.ds(q_width + i * k_width, k_width), :] = k_rows[pl.ds(start, k_width), :]

    gain = gain_ref[...]

    def one(j, _):
        x = gathered_ref[j, pl.ds(0, piece), :].astype(F32)
        inverse = lax.rsqrt(jnp.mean(x * x, axis=1, keepdims=True) + EPSILON)
        attn_out[j] = (x * inverse * gain).astype(BF16)
        made = nt(attn_out[j], weight_out[...])
        for i in range((q_width + k_width) // 128):
            part = made[:, i * 128 : (i + 1) * 128]
            part = (part * cos_ref[j] + swap_lanes(part) * sin_ref[j]).astype(BF16)
            if i < q_width // 128:
                turned_out[j, :, pl.ds(i * 128, 128)] = part
            else:
                kv_out[j, :, pl.ds(i * 128 - q_width, 128)] = part
        kv_out[j, :, pl.ds(k_width, k_width)] = made[:, q_width + k_width :].astype(BF16)
        return 0

    for j in range(members):
        one(j, 0)


def project_inputs(z, gathered, gain, w_query, key_weight, value_weight, from_next, from_prev, cosine, sine, heads):
    members, width = gathered.shape[0], gathered.shape[2]
    piece = cosine.shape[1]
    q_width, k_width = heads * HEAD_SIZE, 2 * HEAD_SIZE
    k_edge = from_prev.shape[0] // 2
    whole = pl.BlockSpec(memory_space=pltpu.VMEM)
    return pl.pallas_call(
        input_kernel,
        in_specs=[pl.BlockSpec(memory_space=pltpu.SMEM)] + [whole] * 9,
        out_specs=[whole] * 4,
        out_shape=[
            jax.ShapeDtypeStruct((members, piece, width), BF16),
            jax.ShapeDtypeStruct((members, piece, q_width), BF16),
            jax.ShapeDtypeStruct((members, piece, 2 * k_width), BF16),
            jax.ShapeDtypeStruct((q_width + 2 * k_width, width), BF16),
        ],
        scratch_shapes=[
            pltpu.VMEM((q_width + from_next.shape[0] - 2 * k_edge, width), BF16),
            pltpu.VMEM((key_weight.shape[0] + 2 * k_edge, width), BF16),
        ],
        compiler_params=pltpu.CompilerParams(vmem_limit_bytes=VMEM_LIMIT),
        cost_estimate=pl.CostEstimate(
            flops=2 * members * piece * width * (q_width + 2 * k_width), bytes_accessed=6000000, transcendentals=0
        ),
        name="project_inputs",
    )(
        jnp.reshape(z, (1,)).astype(jnp.int32),
        gathered,
        gain,
        w_query,
        key_weight,
        value_weight,
        from_next,
        from_prev,
        cosine,
        sine,
    )


def flat(x):
    return x.reshape(-1, x.shape[-1])


def forward_kernel(
    half_ref, q_ref, k_ref, v_ref, k2_ref, v2_ref, kpos_ref, kpos2_ref, qpos_ref, qstart_ref,
    o_ref, lse_ref, q4, bias, m, l, acc,
):
    step, steps = pl.program_id(1), pl.num_programs(1)
    rows = q_ref.shape[0] * q_ref.shape[2]
    heads = q4.shape[0] // rows
    chunk = max(rows, min(FORWARD_ROWS, heads * rows))

    @pl.when(step == 0)
    def _():
        for h in range(heads):
            pair = flat(q_ref[:, 0, :, pl.ds((h // 2) * 128, 128)]).astype(F32) * SCALE
            q4[pl.ds(h * rows, rows), :] = spread(pair, h, half_ref[h]).astype(BF16)
        m[...] = jnp.full_like(m, NEGATIVE)
        l[...] = jnp.zeros_like(l)
        acc[...] = jnp.zeros_like(acc)

    kpos = jnp.concatenate([kpos_ref[...], kpos2_ref[...]], axis=1)
    seen = (kpos <= qpos_ref[...]) & (kpos >= qstart_ref[0])
    bias[...] = jnp.where(seen, 0.0, NEGATIVE)
    keys = jnp.concatenate([flat(k_ref[:, 0]), flat(k2_ref[:, 0])], axis=0)
    values = jnp.concatenate([flat(v_ref[:, 0]), flat(v2_ref[:, 0])], axis=0)

    def one(i, _):
        at = pl.multiple_of(i * chunk, chunk)
        s = nt(q4[pl.ds(at, chunk), :], keys) + jnp.concatenate([bias[...]] * (chunk // rows), axis=0)
        old = m[pl.ds(at, chunk), :]
        new = jnp.maximum(old, jnp.max(s, axis=1, keepdims=True))
        p = jnp.exp(s - new)
        factor = jnp.exp(old - new)
        m[pl.ds(at, chunk), :] = new
        l[pl.ds(at, chunk), :] = l[pl.ds(at, chunk), :] * factor + jnp.sum(p, axis=1, keepdims=True)
        acc[pl.ds(at, chunk), :] = acc[pl.ds(at, chunk), :] * factor + nn(p.astype(BF16), values)
        return 0

    lax.fori_loop(0, heads * rows // chunk, one, 0, unroll=FORWARD_UNROLL)

    @pl.when(step == steps - 1)
    def _():
        total = l[...]
        lse = m[...] + jnp.log(total)
        for i in range(heads * rows // 128):
            part = jnp.broadcast_to(lse[i * 128 : (i + 1) * 128], (128, 128))
            lse_ref[0, :, pl.ds(i * 128, 128)] = part.T[0:1, :]
        out = acc[...] / total
        for h in range(0, heads, 2):
            both = collect(
                out[h * rows : (h + 1) * rows],
                out[(h + 1) * rows : (h + 2) * rows],
                half_ref[h],
                half_ref[h + 1],
            )
            both = both.astype(BF16).reshape(o_ref.shape[0], o_ref.shape[2], 128)
            o_ref[:, 0, :, pl.ds((h // 2) * 128, 128)] = both


def backward_kernel(
    half_ref,
    q_ref,
    o_ref,
    branch_ref,
    w_ref,
    lse_ref,
    k_ref,
    v_ref,
    k2_ref,
    v2_ref,
    kpos_ref,
    kpos2_ref,
    qpos_ref,
    qstart_ref,
    cos_ref,
    sin_ref,
    dq_ref,
    dkv_ref,
    dkv2_ref,
    q4,
    do4,
    delta,
    dq,
):
    step, steps = pl.program_id(1), pl.num_programs(1)
    rows = q_ref.shape[0] * q_ref.shape[2]
    piece = k_ref.shape[2]
    heads = q4.shape[0] // rows
    blocks = min(BACKWARD_BLOCKS, k_ref.shape[0])
    chunk = blocks * piece

    @pl.when(step == 0)
    def _():
        grad_mixed = nn(flat(branch_ref[:, 0]), w_ref[...]).astype(BF16).astype(F32)
        for h in range(heads):
            lanes = pl.ds((h // 2) * 128, 128)
            pair = flat(q_ref[:, 0, :, lanes]).astype(F32) * SCALE
            q4[pl.ds(h * rows, rows), :] = spread(pair, h, half_ref[h]).astype(BF16)
            grad = grad_mixed[:, (h // 2) * 128 : (h // 2 + 1) * 128]
            wide = spread(grad, h, half_ref[h])
            do4[pl.ds(h * rows, rows), :] = wide.astype(BF16)
            lane = lax.broadcasted_iota(jnp.int32, grad.shape, 1)
            mine = (lane // HEAD_SIZE) == (h % 2)
            both = jnp.where(mine, grad * flat(o_ref[:, 0, :, lanes]).astype(F32), 0.0)
            total = jnp.sum(both, axis=1, keepdims=True)
            for i in range(rows // 128):
                part = jnp.broadcast_to(total[i * 128 : (i + 1) * 128], (128, 128))
                delta[:, pl.ds(h * rows + i * 128, 128)] = part.T[0:1, :]
        dq[...] = jnp.zeros_like(dq)

    lse = lse_ref[0]
    row_delta = delta[...]
    qpos, qstart = qpos_ref[...], qstart_ref[0]

    def one(k, v, positions, out, i):
        at = pl.multiple_of(i * chunk, chunk)
        keys = flat(k[pl.ds(i * blocks, blocks), 0])
        values = flat(v[pl.ds(i * blocks, blocks), 0])
        kpos = jnp.broadcast_to(positions[:, pl.ds(at, chunk)].astype(F32), (128, chunk)).T[:, :1].astype(jnp.int32)
        seen = (kpos <= qpos) & (kpos >= qstart)
        bias = jnp.where(seen, 0.0, NEGATIVE)
        bias = jnp.concatenate([bias] * heads, axis=1)
        p = jnp.exp(nt(keys, q4[...]) + bias - lse)
        dv = nn(p.astype(BF16), do4[...]).astype(BF16)
        ds = (p * (nt(values, do4[...]) - row_delta)).astype(BF16)
        dk = nn(ds, q4[...]).astype(BF16)
        out[pl.ds(i * blocks, blocks), 0, :, pl.ds(0, 128)] = dk.reshape(blocks, piece, 128)
        out[pl.ds(i * blocks, blocks), 0, :, pl.ds(128, 128)] = dv.reshape(blocks, piece, 128)
        dq[...] += tn(ds, keys)

    def both(i, _):
        one(k_ref, v_ref, kpos_ref, dkv_ref, i)
        one(k2_ref, v2_ref, kpos2_ref, dkv2_ref, i)
        return 0

    lax.fori_loop(0, k_ref.shape[0] // blocks, both, 0, unroll=BACKWARD_UNROLL)

    @pl.when(step == steps - 1)
    def _():
        cosine, sine = flat(cos_ref[...]), flat(sin_ref[...])
        for h in range(0, heads, 2):
            both = collect(
                dq[pl.ds(h * rows, rows), :],
                dq[pl.ds((h + 1) * rows, rows), :],
                half_ref[h],
                half_ref[h + 1],
            )
            both = both * SCALE
            back = (both * cosine - swap_lanes(both) * sine).astype(BF16)
            dq_ref[:, 0, :, pl.ds((h // 2) * 128, 128)] = back.reshape(dq_ref.shape[0], dq_ref.shape[2], 128)


def key_step(owners, piece):
    most = max(1, 1024 // piece)
    return most if owners % most == 0 else owners


def attention_forward(half, queries, kv, own_pos, own_start, key_pos, key_pos2):
    members, seqs, piece, width = queries.shape
    owners = kv[0].shape[0]
    rows, count = members * piece, 2 * owners * piece
    step = key_step(owners, piece)
    heads = width // HEAD_SIZE
    own = pl.BlockSpec((members, 1, piece, width), lambda s, b: (0, s, 0, 0))
    keys = pl.BlockSpec((step, 1, piece, 128), lambda s, b: (b, s, 0, 0))
    values = pl.BlockSpec((step, 1, piece, 128), lambda s, b: (b, s, 0, 1))
    places = pl.BlockSpec((1, step * piece), lambda s, b: (0, b))
    return pl.pallas_call(
        forward_kernel,
        grid=(seqs, owners // step),
        in_specs=[
            pl.BlockSpec(memory_space=pltpu.SMEM),
            own,
            keys,
            values,
            keys,
            values,
            places,
            places,
            pl.BlockSpec((rows, 1), lambda s, b: (0, 0)),
            pl.BlockSpec((1, rows, 1), lambda s, b: (s, 0, 0)),
        ],
        out_specs=[own, pl.BlockSpec((1, 1, heads * rows), lambda s, b: (s, 0, 0))],
        out_shape=[
            jax.ShapeDtypeStruct(queries.shape, BF16),
            jax.ShapeDtypeStruct((seqs, 1, heads * rows), F32),
        ],
        scratch_shapes=[
            pltpu.VMEM((heads * rows, 128), BF16),
            pltpu.VMEM((rows, 2 * step * piece), F32),
            pltpu.VMEM((heads * rows, 1), F32),
            pltpu.VMEM((heads * rows, 1), F32),
            pltpu.VMEM((heads * rows, 128), F32),
        ],
        compiler_params=pltpu.CompilerParams(
            dimension_semantics=("arbitrary", "arbitrary"), vmem_limit_bytes=VMEM_LIMIT
        ),
        cost_estimate=SHORT,
        name="attention_forward",
    )(
        half,
        queries,
        kv[0],
        kv[0],
        kv[1],
        kv[1],
        key_pos,
        key_pos2,
        own_pos,
        own_start,
    )


def attention_backward(half, queries, mixed, branch, w_heads, lse, kv, key_pos, own_pos, own_start, cosine, sine):
    members, seqs, piece, width = queries.shape
    owners = kv[0].shape[0]
    rows, count = members * piece, 2 * owners * piece
    step = key_step(owners, piece)
    heads = width // HEAD_SIZE
    own = pl.BlockSpec((members, 1, piece, width), lambda s, b: (0, s, 0, 0))
    table = pl.BlockSpec((members, piece, 128), lambda s, b: (0, 0, 0))
    keys = pl.BlockSpec((step, 1, piece, 128), lambda s, b: (b, s, 0, 0))
    values = pl.BlockSpec((step, 1, piece, 128), lambda s, b: (b, s, 0, 1))
    places = pl.BlockSpec((1, step * piece), lambda s, b: (0, b))
    made = pl.BlockSpec((step, 1, piece, 256), lambda s, b: (b, s, 0, 0))
    return pl.pallas_call(
        backward_kernel,
        grid=(seqs, owners // step),
        in_specs=[
            pl.BlockSpec(memory_space=pltpu.SMEM),
            own,
            own,
            pl.BlockSpec((members, 1, piece, branch.shape[3]), lambda s, b: (0, s, 0, 0)),
            pl.BlockSpec(w_heads.shape, lambda s, b: (0, 0)),
            pl.BlockSpec((1, 1, heads * rows), lambda s, b: (s, 0, 0)),
            keys,
            values,
            keys,
            values,
            places,
            places,
            pl.BlockSpec((1, rows), lambda s, b: (0, 0)),
            pl.BlockSpec((1, 1, rows), lambda s, b: (s, 0, 0)),
            table,
            table,
        ],
        out_specs=[own, made, made],
        out_shape=[
            jax.ShapeDtypeStruct(queries.shape, BF16),
            jax.ShapeDtypeStruct(kv[0].shape, BF16),
            jax.ShapeDtypeStruct(kv[1].shape, BF16),
        ],
        scratch_shapes=[
            pltpu.VMEM((heads * rows, 128), BF16),
            pltpu.VMEM((heads * rows, 128), BF16),
            pltpu.VMEM((1, heads * rows), F32),
            pltpu.VMEM((heads * rows, 128), F32),
        ],
        compiler_params=pltpu.CompilerParams(
            dimension_semantics=("arbitrary", "arbitrary"), vmem_limit_bytes=VMEM_LIMIT
        ),
        cost_estimate=SHORT,
        name="attention_backward",
    )(
        half,
        queries,
        mixed,
        branch,
        w_heads,
        lse,
        kv[0],
        kv[0],
        kv[1],
        kv[1],
        *key_pos,
        own_pos[None, :],
        own_start[:, None, :],
        cosine,
        sine,
    )


def feed_forward_kernel(
    place_ref,
    main_ref,
    side_ref,
    tokens_ref,
    gain_ref,
    gate_ref,
    up_ref,
    cotangent_ref,
    *refs,
):
    parts, refs = refs[:-12], refs[-12:]
    residual_out, mixed_out, heads_out, mlp_out, hidden_out, gate_out, up_out, part_out, layer_out = refs[:9]
    w_out, w_down, residual = refs[9:]
    members, chips = main_ref.shape[0], len(parts) // 2
    z, parity, chip = place_ref[0], place_ref[1], place_ref[2]
    own, width, units = residual_out.shape[0], w_out.shape[0], w_down.shape[1]
    out_rows, wide = width // members, w_out.shape[1]
    lanes = wide // members
    some = parts[0].shape[1]
    for shift in range(members):
        source = lax.rem(z - shift + members, members)
        first = source * out_rows
        for q in range(chips):
            for who in range(2):
                part = parts[who * chips + q]
                index = 2 * (chip ^ q) + (parity ^ who)
                at = pl.multiple_of(first + jnp.minimum(index * some, out_rows - some), 16)
                w_out[pl.ds(at, some), :] = part[shift, :, pl.ds(0, wide)]
                w_down[pl.ds(at, some), :] = part[shift, :, pl.ds(wide, units)]
    count = main_ref.shape[1]
    for j in range(members):
        mixed_out[pl.ds(0, count), pl.ds(j * lanes, lanes)] = main_ref[j]
        shift = lax.rem(z - j + members, members)
        mixed_out[pl.ds(count, side_ref.shape[1]), pl.ds(j * lanes, lanes)] = side_ref[shift]
    heads_out[...] = w_out[:, pl.ds(pl.multiple_of(z * lanes, lanes), lanes)]


    def one(i, _):
        rows, blocks = pl.ds(pl.multiple_of(i * 2 * own, 16), 2 * own), pl.ds(2 * i, 2)
        here = flat(tokens_ref[blocks, pl.ds(0, own), :]).astype(F32) + nt(mixed_out[rows, :], w_out[...])
        residual[rows, :] = here
        inverse = lax.rsqrt(jnp.mean(here * here, axis=1, keepdims=True) + EPSILON)
        mlp_in = (here * inverse * gain_ref[...]).astype(BF16)
        mlp_out[rows, :] = mlp_in
        gate_pre = nn(mlp_in, gate_ref[...])
        up_pre = nn(mlp_in, up_ref[...])
        sigmoid_gate = jax.nn.sigmoid(gate_pre)
        silu_gate = gate_pre * sigmoid_gate
        hidden = (silu_gate * up_pre).astype(BF16)
        hidden_out[rows, :] = hidden
        grad_hidden = nn(flat(cotangent_ref[blocks]), w_down[...])
        slope = sigmoid_gate + silu_gate * (1.0 - sigmoid_gate)
        grad_gate = (grad_hidden * up_pre * slope).astype(BF16)
        grad_up = (grad_hidden * silu_gate).astype(BF16)
        gate_out[rows, :] = grad_gate
        up_out[rows, :] = grad_up
        part = nt(grad_gate, gate_ref[...]) + nt(grad_up, up_ref[...])
        part_out[blocks, :, pl.ds(0, width)] = part.astype(BF16).reshape(2, own, width)
        part_out[blocks, :, pl.ds(width, wide - width)] = jnp.zeros((2, own, wide - width), BF16)
        layer = nt(hidden, w_down[...])
        layer_out[blocks, :, pl.ds(0, width)] = layer.astype(BF16).reshape(2, own, width)
        layer_out[blocks, :, pl.ds(width, wide - width)] = jnp.zeros((2, own, wide - width), BF16)
        return 0

    lax.fori_loop(0, members // 2, one, 0)
    residual_out[...] = residual[pl.ds(pl.multiple_of(z * own, own), own), :]


def feed_forward(place, main, side, tokens, parts, gain, gate_turned, up_turned, cotangent):
    members, lanes = main.shape[0], main.shape[2]
    own, width = cotangent.shape[1:]
    rows, units, wide = members * own, gate_turned.shape[1], members * lanes
    whole = pl.BlockSpec(memory_space=pltpu.VMEM)
    return pl.pallas_call(
        feed_forward_kernel,
        in_specs=[pl.BlockSpec(memory_space=pltpu.SMEM)] + [whole] * (7 + len(parts)),
        out_specs=[whole] * 9,
        out_shape=[
            jax.ShapeDtypeStruct((own, width), F32),
            jax.ShapeDtypeStruct((rows, wide), BF16),
            jax.ShapeDtypeStruct((width, lanes), BF16),
            jax.ShapeDtypeStruct((rows, width), BF16),
            jax.ShapeDtypeStruct((rows, units), BF16),
            jax.ShapeDtypeStruct((rows, units), BF16),
            jax.ShapeDtypeStruct((rows, units), BF16),
            jax.ShapeDtypeStruct((members, own, wide), BF16),
            jax.ShapeDtypeStruct((members, own, wide), BF16),
        ],
        scratch_shapes=[
            pltpu.VMEM((width, wide), BF16),
            pltpu.VMEM((width, units), BF16),
            pltpu.VMEM((rows, width), F32),
        ],
        compiler_params=pltpu.CompilerParams(vmem_limit_bytes=VMEM_LIMIT),
        cost_estimate=SHORT,
        name="feed_forward",
    )(place, main, side, tokens, gain, gate_turned, up_turned, cotangent, *parts)


def feed_forward_grads_kernel(place_ref, mlp_ref, gate_ref, up_ref, cotangent_ref, hidden_ref, keep_out, give_out):
    parity = place_ref[1]
    count = mlp_ref.shape[1] // 2
    rest = keep_out.shape[1] - count
    for i, (x, g) in enumerate(((mlp_ref, gate_ref), (mlp_ref, up_ref), (cotangent_ref, hidden_ref))):
        made = tn(x[...], g[...]).astype(BF16)
        low, high = made[:count], made[count:]
        keep_out[i, pl.ds(0, count), :] = jnp.where(parity == 0, low, high)
        give_out[i, pl.ds(0, count), :] = jnp.where(parity == 0, high, low)
        for out in (keep_out, give_out):
            out[i, pl.ds(count, rest), :] = jnp.zeros((rest, made.shape[1]), BF16)


def feed_forward_grads(place, mlp_in, grad_gate_pre, grad_up_pre, cotangent, hidden, half_rows):
    rows, width = mlp_in.shape
    units = hidden.shape[1]
    whole = pl.BlockSpec(memory_space=pltpu.VMEM)
    return pl.pallas_call(
        feed_forward_grads_kernel,
        in_specs=[pl.BlockSpec(memory_space=pltpu.SMEM)] + [whole] * 5,
        out_specs=[whole] * 2,
        out_shape=[jax.ShapeDtypeStruct((3, half_rows, units), BF16)] * 2,
        compiler_params=pltpu.CompilerParams(vmem_limit_bytes=VMEM_LIMIT),
        cost_estimate=pl.CostEstimate(flops=6 * rows * width * units, bytes_accessed=8000000, transcendentals=0),
        name="feed_forward_grads",
    )(place, mlp_in, grad_gate_pre, grad_up_pre, cotangent, hidden)


def finish_kernel(place_ref, *refs):
    chips = (len(refs) - 3) // 2
    parts, outs = refs[:-3], refs[-3:]
    parity, chip = place_ref[1], place_ref[2]
    part = parts[0].shape[1]
    count = outs[2].shape[0]
    tail = count % part
    for who in range(2):
        first = (parity ^ who) * count
        for q in range(chips):
            at = (chip ^ q) * part
            for i in range(3 - who):
                block = parts[who * chips + q][i].astype(outs[i].dtype)
                base = at if i == 2 else first + at

                @pl.when(at + part <= count)
                def _():
                    outs[i][pl.ds(pl.multiple_of(base, 16), part), :] = block

                if tail:

                    @pl.when(at + tail == count)
                    def _():
                        outs[i][pl.ds(pl.multiple_of(base, 16), tail), :] = block[:tail]


def finish(place, found, found_mate, width):
    units = found[0].shape[2]
    whole = pl.BlockSpec(memory_space=pltpu.VMEM)
    parts = [*found, *found_mate]
    return pl.pallas_call(
        finish_kernel,
        in_specs=[pl.BlockSpec(memory_space=pltpu.SMEM)] + [whole] * len(parts),
        out_specs=[whole] * 3,
        out_shape=[jax.ShapeDtypeStruct((width, units), F32)] * 2 + [jax.ShapeDtypeStruct((width // 2, units), BF16)],
        compiler_params=pltpu.CompilerParams(vmem_limit_bytes=VMEM_LIMIT),
        cost_estimate=pl.CostEstimate(flops=0, bytes_accessed=9000000, transcendentals=0),
        name="finish",
    )(place, *parts)


def down_kernel(place_ref, *refs):
    parts, out = refs[:-1], refs[-1]
    members = len(parts) // 2
    z, parity = place_ref[0], place_ref[1]
    units = parts[0].shape[1]
    mine = z // (members // 2) == parity
    for shift in range(members):
        source = lax.rem(z - shift + members, members)
        block = jnp.where(mine, parts[shift][...], parts[members + shift][...])
        out[:, pl.ds(pl.multiple_of(source * units, 128), units)] = block.astype(F32)


def finish_down(place, found, found_mate):
    rows, units = found[0].shape
    whole = pl.BlockSpec(memory_space=pltpu.VMEM)
    return pl.pallas_call(
        down_kernel,
        in_specs=[pl.BlockSpec(memory_space=pltpu.SMEM)] + [whole] * 2 * len(found),
        out_specs=whole,
        out_shape=jax.ShapeDtypeStruct((rows, len(found) * units), F32),
        compiler_params=pltpu.CompilerParams(vmem_limit_bytes=VMEM_LIMIT),
        cost_estimate=pl.CostEstimate(flops=0, bytes_accessed=6000000, transcendentals=0),
        name="finish_down",
    )(place, *found, *found_mate)


def output_kernel(
    place_ref, dq_ref, pair_ref, cos_ref, sin_ref, attn_ref, weight_ref, tokens_ref, grad_out_ref, mlp_gain_ref, *refs
):
    others, (keep_out, give_out, part_out, pre, sent) = refs[:-5], refs[-5:]
    members, piece, width = attn_ref.shape
    q_width = dq_ref.shape[2]

    def one(j, gain):
        total = pair_ref[j]
        for other in others:
            total = total + other[j].astype(F32)
        keys = total[:, :128]
        pre[j, :, pl.ds(0, q_width)] = dq_ref[j]
        pre[j, :, pl.ds(q_width, 128)] = (keys * cos_ref[j] - swap_lanes(keys) * sin_ref[j]).astype(BF16)
        pre[j, :, pl.ds(q_width + 128, 128)] = total[:, 128:].astype(BF16)
        part = nn(pre[j], weight_ref[...])
        part_out[j, :, pl.ds(0, width)] = part.astype(BF16)
        part_out[j, :, pl.ds(width, part_out.shape[2] - width)] = jnp.zeros((piece, part_out.shape[2] - width), BF16)
        x = tokens_ref[j, pl.ds(0, piece), :].astype(F32)
        inverse = lax.rsqrt(jnp.mean(x * x, axis=1, keepdims=True) + EPSILON)
        return gain + jnp.sum(part * (x * inverse), axis=0, keepdims=True)

    gain = lax.fori_loop(0, members, one, jnp.zeros((1, width), F32))
    half_rows = keep_out.shape[0]
    low = q_width + 128
    out_rows = grad_out_ref.shape[0]
    lanes = pl.ds(0, width)
    sent[...] = jnp.zeros_like(sent)
    made = tn(flat(pre[...]), flat(attn_ref[...])).astype(BF16)
    sent[pl.ds(0, low), lanes] = made[:low]
    sent[pl.ds(half_rows, 128), lanes] = made[low:]
    sent[pl.ds(half_rows + 128, out_rows), lanes] = grad_out_ref[...]
    row = lax.broadcasted_iota(jnp.int32, (16, width), 0)
    gains = jnp.where(row == 0, gain, jnp.where(row == 1, mlp_gain_ref[...], 0.0))
    sent[pl.ds(half_rows + 128 + out_rows, 16), lanes] = gains.astype(BF16)
    parity = place_ref[1]
    keep_out[...] = sent[pl.ds(pl.multiple_of(parity * half_rows, 16), half_rows), :]
    give_out[...] = sent[pl.ds(pl.multiple_of((1 - parity) * half_rows, 16), half_rows), :]


def project_outputs(place, dq, pair, others, cosine, sine, attn_in, w_in, tokens, grad_out, gain_mlp, half_rows):
    members, piece, width = attn_in.shape
    wide = -(-width // 128) * 128
    whole = pl.BlockSpec(memory_space=pltpu.VMEM)
    return pl.pallas_call(
        output_kernel,
        in_specs=[pl.BlockSpec(memory_space=pltpu.SMEM)] + [whole] * (9 + len(others)),
        out_specs=[whole] * 3,
        out_shape=[
            jax.ShapeDtypeStruct((half_rows, wide), BF16),
            jax.ShapeDtypeStruct((half_rows, wide), BF16),
            jax.ShapeDtypeStruct((members, piece, wide), BF16),
        ],
        scratch_shapes=[
            pltpu.VMEM((members, piece, w_in.shape[0]), BF16),
            pltpu.VMEM((2 * half_rows, wide), BF16),
        ],
        compiler_params=pltpu.CompilerParams(vmem_limit_bytes=VMEM_LIMIT),
        cost_estimate=SHORT,
        name="project_outputs",
    )(place, dq, pair, cosine, sine, attn_in, w_in, tokens, grad_out, gain_mlp, *others)


def shard_kernel(
    place_ref, mine_ref, other_ref, up_ref, up_mate_ref, down_ref, down_mate_ref, *refs
):
    gains, (q_out, k_out, v_out, o_out, gains_out, q_rows, early, late) = refs[:-8], refs[-8:]
    total = gains[0][...]
    for one in gains[1:]:
        total = total + one[...]
    gains_out[...] = total
    z, parity = place_ref[0], place_ref[1]
    width = q_out.shape[1]
    k_edge = down_ref.shape[0]
    q_edge = up_ref.shape[0] - k_edge
    q_width = q_rows.shape[0] - q_edge
    k_own, q_own = k_out.shape[0], q_out.shape[0]
    k_shift, q_shift = k_own - HEAD_SIZE, q_width - q_own

    def ordered(mine, other, rows):
        a, b = mine[rows, pl.ds(0, width)], other[rows, pl.ds(0, width)]
        return jnp.where(parity == 0, a, b), jnp.where(parity == 0, b, a)

    q_rows[pl.ds(0, q_edge), :] = ordered(up_ref, up_mate_ref, pl.ds(0, q_edge))[0]
    q_rows[pl.ds(q_edge, q_width), :] = ordered(mine_ref, other_ref, pl.ds(0, q_width))[0]
    start = pl.multiple_of(q_edge - z * q_shift, 16)
    q_out[...] = q_rows[pl.ds(start, q_own), :].astype(F32)
    o_out[...] = ordered(mine_ref, other_ref, pl.ds(128, o_out.shape[0]))[1].astype(F32)
    early[...] = jnp.zeros_like(early)
    late[...] = jnp.zeros_like(late)
    start = pl.multiple_of(z * k_shift, 16)
    for which, first, edge_at, out in ((0, q_width, q_edge, k_out), (1, 0, 0, v_out)):
        early[pl.ds(k_shift, k_edge), :] = ordered(up_ref, up_mate_ref, pl.ds(edge_at, k_edge))[which]
        late[pl.ds(HEAD_SIZE, k_edge), :] = ordered(down_ref, down_mate_ref, pl.ds(0, k_edge))[which]
        rows = pl.ds(pl.multiple_of(first + start, 16), k_own)
        total = ordered(mine_ref, other_ref, rows)[which].astype(F32)
        out[...] = total + early[pl.ds(start, k_own), :].astype(F32) + late[pl.ds(start, k_own), :].astype(F32)


def shard_rows(place, mine, other, up, up_mate, down, down_mate, gains, q_width, q_rows, k_rows, out_rows, width):
    k_edge = down.shape[0]
    q_edge = up.shape[0] - k_edge
    whole = pl.BlockSpec(memory_space=pltpu.VMEM)
    return pl.pallas_call(
        shard_kernel,
        in_specs=[pl.BlockSpec(memory_space=pltpu.SMEM)] + [whole] * (6 + len(gains)),
        out_specs=[whole] * 5,
        out_shape=[jax.ShapeDtypeStruct((rows, width), F32) for rows in (q_rows, k_rows, k_rows, out_rows)]
        + [jax.ShapeDtypeStruct(gains[0].shape, F32)],
        scratch_shapes=[
            pltpu.VMEM((q_width + q_edge, width), BF16),
            pltpu.VMEM((2 * k_rows, width), BF16),
            pltpu.VMEM((HEAD_SIZE + 2 * k_rows, width), BF16),
        ],
        compiler_params=pltpu.CompilerParams(vmem_limit_bytes=VMEM_LIMIT),
        cost_estimate=SHORT,
        name="shard_rows",
    )(place, mine, other, up, up_mate, down, down_mate, *gains)


def mate(x):
    return lax.ppermute(x, "core", [(0, 1), (1, 0)])


def across(x, by):
    return lax.ppermute(x, "pair", [(i, i ^ by) for i in range(lax.axis_size("pair"))])


def everywhere(x):
    return [x] + [across(x, by) for by in range(1, lax.axis_size("pair"))]


def pick(x, index, axis=0):
    return lax.dynamic_index_in_dim(x, index, axis, keepdims=False)


def pair_sum(x, parity):
    return (pick(x, parity).astype(F32) + mate(pick(x, 1 - parity)).astype(F32)).astype(BF16)


def add_up(pieces):
    total = pieces[0].astype(F32)
    for one in pieces[1:]:
        total = total + one.astype(F32)
    return total


def rotate(x, shift):
    nf = lax.axis_size("fsdp")
    return lax.ppermute(x, "fsdp", [(i, (i + shift) % nf) for i in range(nf)])


def after(x, *others):
    return lax.optimization_barrier((x, *others))[0]


def local(
    tokens,
    doc_lengths,
    block_table,
    attn_gain,
    w_query,
    key_weight,
    value_weight,
    w_out,
    mlp_gain,
    w_gate,
    w_up,
    w_down,
    out_cotangent,
):
    nf, chips, nc = lax.axis_size("fsdp"), lax.axis_size("pair"), lax.axis_size(CTX)
    z, parity, chip = lax.axis_index("fsdp"), lax.axis_index("core"), lax.axis_index("pair")
    c = 2 * chip + parity
    seqs, piece, width = tokens.shape
    rows = nf * piece
    half_len = HEAD_SIZE // 2
    up = [(i, i + 1) for i in range(nf - 1)]
    down = [(i + 1, i) for i in range(nf - 1)]

    heads = -(-QUERY_HEADS // nf)
    q_rows, k_rows = w_query.shape[0], key_weight.shape[0]
    q_width, k_width = heads * HEAD_SIZE, 2 * HEAD_SIZE
    q_shift = q_width - q_rows
    k_shift = k_rows - HEAD_SIZE
    q_edge, k_edge = q_shift * (nf - 1), k_shift * (nf - 1)
    head_index = jnp.arange(heads, dtype=jnp.int32)
    half = jnp.minimum((z * heads + head_index) // GROUP - z, 1).astype(jnp.int32)

    block = piece // 2
    pairs = block_table.shape[0]
    within = jnp.arange(block, dtype=jnp.int32)

    def positions_of(table):
        paired = jnp.stack([table, 2 * pairs - 1 - table], axis=1)
        return (paired[:, :, None] * block + within).reshape(-1)

    group_pos = positions_of(lax.dynamic_slice_in_dim(block_table.astype(jnp.int32), c * nf, nf, 0))
    frequency = ROPE_BASE ** (-(2.0 * jnp.arange(half_len, dtype=F32)) / HEAD_SIZE)
    angles = group_pos.astype(F32)[:, None] * frequency[None, :]
    cos, sin = jnp.cos(angles), jnp.sin(angles)
    cosine = jnp.concatenate([cos, cos, cos, cos], axis=1).reshape(nf, piece, 128)
    sine = jnp.concatenate([-sin, sin, -sin, sin], axis=1).reshape(nf, piece, 128)
    cosine_all, sine_all = jnp.concatenate([cosine] * seqs, axis=1), jnp.concatenate([sine] * seqs, axis=1)

    own_tokens = seqs * piece
    group_tokens = nf * own_tokens
    own_cotangent = out_cotangent.reshape(own_tokens, width)
    from_next = lax.ppermute(
        jnp.concatenate([w_query[:q_edge], key_weight[:k_edge], value_weight[:k_edge]], axis=0),
        "fsdp",
        down,
    )
    from_prev = lax.ppermute(
        jnp.concatenate([key_weight[k_rows - k_edge :], value_weight[k_rows - k_edge :]], axis=0),
        "fsdp",
        up,
    )

    gain_rows = jnp.pad(jnp.stack([attn_gain, mlp_gain]), ((0, 6), (0, width - attn_gain.shape[0])))
    own_payload = jnp.concatenate([tokens.reshape(own_tokens, width), gain_rows], axis=0)
    own_payload, from_next, from_prev = lax.optimization_barrier((own_payload, from_next, from_prev))
    gathered = lax.all_gather(own_payload, "fsdp", axis=0)
    gains_all = gathered[:, own_tokens : own_tokens + 2, : attn_gain.shape[0]]
    gains_all = jnp.transpose(gains_all, (1, 0, 2)).reshape(2, width).astype(F32)

    attn_in, queries, own_kv, w_in = project_inputs(
        z, gathered, gains_all[:1], w_query, key_weight, value_weight, from_next, from_prev,
        cosine_all, sine_all, heads,
    )
    positions = positions_of(block_table.astype(jnp.int32)).reshape(nc, rows)
    even = 2 * jnp.arange(chips, dtype=jnp.int32)
    key_pos = [jnp.take(positions, c ^ (even + i), axis=0).reshape(-1) for i in range(2)]
    own_pos = key_pos[0][:rows]
    bounds = jnp.cumsum(doc_lengths, axis=1)
    reached = own_pos[None, :, None] >= bounds[:, None, :-1]
    own_start = jnp.max(jnp.where(reached, bounds[:, None, :-1], 0), axis=-1)
    place = jnp.stack([z, parity, chip]).astype(jnp.int32)
    tables = (own_pos[:, None], own_start[:, :, None], key_pos[0][None, :], key_pos[1][None, :], place, gains_all[1:])

    out_rows, units = w_out.shape[0], w_gate.shape[0]
    some = -(-out_rows // (16 * nc)) * 16
    from_row = jnp.minimum(c * some, out_rows - some)
    wide = nf * q_width
    some_out = jnp.pad(lax.dynamic_slice_in_dim(w_out, from_row, some, 0), ((0, 0), (0, wide - width)))
    some_down = lax.dynamic_slice_in_dim(w_down, from_row, some, 0)
    some_out, some_down = lax.optimization_barrier((some_out, some_down, gathered))[:2]
    pieces = []
    for shift in range(nf):
        columns = lax.dynamic_slice_in_dim(some_down, lax.rem(z + shift, nf) * units, units, 1)
        piece_out = jnp.concatenate([some_out, columns], axis=1)
        pieces.append(rotate(piece_out, shift) if shift else piece_out)
    late_cotangent, _, _, tables = lax.optimization_barrier((own_cotangent, own_kv, pieces, tables))
    cotangent = lax.all_gather(late_cotangent, "fsdp", axis=0)
    parts = everywhere(jnp.stack(pieces))
    same_core, cotangent, parts = lax.optimization_barrier((everywhere(own_kv), cotangent, parts))
    same_core = jnp.concatenate(same_core, axis=0)
    kv = [half_kv.reshape(-1, seqs, piece, 2 * k_width) for half_kv in (same_core, mate(same_core))]
    queries = queries.reshape(nf, seqs, piece, q_width)

    gate_turned, up_turned = w_gate.T, w_up.T

    mixed_own, lse = attention_forward(half, queries, kv, *tables[:4])
    parts = after(parts, mixed_own)
    parts = parts + [mate(part) for part in parts]
    mixed_rows = after(mixed_own.reshape(group_tokens, q_width), parts[:chips])
    main_rows = group_tokens - 16
    side = jnp.stack([mixed_rows[main_rows:]] + [rotate(mixed_rows[main_rows:], shift) for shift in range(1, nf)])
    main = lax.all_gather(mixed_rows[:main_rows], "fsdp", axis=0)

    place, mlp_gain_row = tables[4:]
    (
        residual, mixed, w_out_heads, mlp_in, hidden, grad_gate_pre, grad_up_pre, grad_mlp_part, layer_part,
    ) = feed_forward(
        place, main, side, gathered, parts, mlp_gain_row, gate_turned, up_turned, cotangent
    )
    mixed = mixed[:, : QUERY_HEADS * HEAD_SIZE]

    def exchange(part):
        swapped = lax.all_to_all(part, "fsdp", 0, 0, tiled=True)
        return jnp.sum(swapped.astype(F32), axis=0)[:, :width]

    grad_mlp_in = exchange(grad_mlp_part)
    inv_mlp = lax.rsqrt(jnp.mean(residual * residual, axis=-1, keepdims=True) + EPSILON)
    normed_mlp = residual * inv_mlp
    scaled = grad_mlp_in * gains_all[1]
    grad_gain_mlp = jnp.sum(grad_mlp_in * normed_mlp, axis=0)
    grad_residual = own_cotangent.astype(F32) + inv_mlp * (
        scaled - normed_mlp * jnp.mean(scaled * normed_mlp, axis=-1, keepdims=True)
    )
    part_rows = -(-(width // 2) // (16 * chips)) * 16
    keep, give = feed_forward_grads(
        place, mlp_in, grad_gate_pre, grad_up_pre, cotangent.reshape(group_tokens, width), hidden, part_rows * chips
    )
    made_pair = (keep.astype(F32) + mate(give).astype(F32)).astype(BF16).reshape(3, chips, part_rows, units)
    made_pieces = [pick(made_pair, chip, 1)] + [across(pick(made_pair, chip ^ by, 1), by) for by in range(1, chips)]
    branch_own, _ = lax.optimization_barrier((grad_residual.astype(BF16), made_pair))
    grad_attn_branch = lax.all_gather(branch_own, "fsdp", axis=0, tiled=True)

    made_total = add_up(made_pieces).astype(BF16)
    grad_attn_branch, made_total = lax.optimization_barrier((grad_attn_branch, made_total))
    made_found = everywhere(made_total)
    branch = grad_attn_branch.reshape(nf, seqs, piece, width)
    grad_query_pre, *grad_kv = attention_backward(
        half, queries, mixed_own, branch, w_out_heads, lse, kv, tables[2:4], own_pos, own_start, cosine_all, sine_all
    )
    layer_part = lax.all_to_all(after(layer_part, grad_attn_branch), "fsdp", 0, 0, tiled=True)

    grad_kv, made_found, layer_part = lax.optimization_barrier((grad_kv, made_found, layer_part))
    taken = [own.reshape(chips, nf, own_tokens, 2 * k_width) for own in (grad_kv[0], mate(grad_kv[1]))]
    pair = taken[0][0].astype(F32) + taken[1][0].astype(F32)
    pair_low = [(taken[0][by].astype(F32) + taken[1][by].astype(F32)).astype(BF16) for by in range(1, chips)]
    made_found = after(made_found, pair_low)
    others = [across(pair_low[by - 1], by) for by in range(1, chips)]
    grad_attn_own = lax.dynamic_slice_in_dim(grad_attn_branch, z * out_rows, out_rows, 1)
    grad_out_w = tn(grad_attn_own, mixed).astype(BF16)
    grad_gate_w, grad_up_w, down_own = finish(place, made_found, [mate(found) for found in made_found], width)
    others, grad_gate_w, grad_up_w, down_own = lax.optimization_barrier((others, grad_gate_w, grad_up_w, down_own))
    half_rows = max(q_width + k_width, k_width + out_rows + 16)
    half_rows = -(-half_rows // (16 * chips)) * 16 * chips
    keep, give, grad_attn_part = project_outputs(
        place, grad_query_pre.reshape(nf, own_tokens, q_width), pair, others, cosine_all, sine_all, attn_in, w_in, gathered,
        grad_out_w, grad_gain_mlp[None], half_rows,
    )

    sent_pair = (keep.astype(F32) + mate(give).astype(F32)).astype(BF16)
    sent_pair = sent_pair.reshape(chips, half_rows // chips, -1)
    sent_pieces = [pick(sent_pair, chip)] + [across(pick(sent_pair, chip ^ by), by) for by in range(1, chips)]
    swapped = lax.all_to_all(grad_attn_part, "fsdp", 0, 0, tiled=True)

    blocks = nf // 2
    down_own = after(down_own, sent_pair).reshape(blocks, out_rows, units)
    down_found = [pick(down_own, lax.rem(z, blocks))]
    for shift in range(1, nf):
        sent_block = pick(down_own, lax.rem(z + shift, nf) - blocks * parity)
        links = [
            (p * nf + i, p * nf + (i + shift) % nf) for p in range(2) for i in range(nf) if (i + shift) % nf // blocks == p
        ]
        down_found.append(lax.ppermute(sent_block, ("core", "fsdp"), links))
    sent_total = add_up(sent_pieces).astype(BF16)
    mine = lax.all_gather(sent_total, "pair", axis=0, tiled=True)
    other = mate(mine)

    edge_rows = jnp.zeros((q_edge, mine.shape[1]), BF16)
    upward = jnp.where(
        parity == 0,
        jnp.concatenate([mine[q_width - q_edge : q_width], mine[q_width + k_width - k_edge : q_width + k_width]]),
        jnp.concatenate([mine[k_width - k_edge : k_width], edge_rows]),
    )
    downward = jnp.where(parity == 0, mine[q_width : q_width + k_edge], mine[:k_edge])
    upward, downward = lax.ppermute(upward, "fsdp", up), lax.ppermute(downward, "fsdp", down)
    gain_width = attn_gain.shape[0]
    gain_row = k_width + out_rows
    gains = jnp.where(parity == 0, other[gain_row : gain_row + 2, :width], mine[gain_row : gain_row + 2, :width])
    gains = gains.astype(F32).reshape(2, nf, gain_width)
    grad_gains = [pick(gains, z, 1)] + [rotate(pick(gains, lax.rem(z + shift, nf), 1), shift) for shift in range(1, nf)]
    grad_query_w, grad_key_w, grad_value_w, grad_out_w, gains = shard_rows(
        place, mine, other, upward, mate(upward), downward, mate(downward), grad_gains, q_width, q_rows, k_rows, out_rows, width
    )

    swapped = after(swapped, sent_total)
    grad_attn_in = add_up([pick(swapped, i) for i in range(nf)])[:, :width]
    own_x = tokens.reshape(own_tokens, width).astype(F32)
    inv_attn = lax.rsqrt(jnp.mean(own_x * own_x, axis=-1, keepdims=True) + EPSILON)
    normed_attn = own_x * inv_attn
    scaled = grad_attn_in * gains_all[0]
    grad_tokens = (
        grad_residual
        + inv_attn * (scaled - normed_attn * jnp.mean(scaled * normed_attn, axis=-1, keepdims=True))
    ).astype(BF16)

    layer_part = after(layer_part, sent_pair)
    layer_out = (residual + jnp.sum(layer_part.astype(F32), axis=0)[:, :width]).astype(BF16)
    down_found = after(down_found, mine)
    down_mate = after([mate(found) for found in down_found], grad_gains)
    grad_down_w = finish_down(place, down_found, down_mate)
    return (
        layer_out.reshape(tokens.shape),
        grad_tokens.reshape(tokens.shape),
        gains[0],
        grad_query_w,
        grad_key_w,
        grad_value_w,
        grad_out_w,
        gains[1],
        grad_gate_w.T,
        grad_up_w.T,
        grad_down_w,
    )


def solution(mesh):
    count, members = mesh.shape["ctx"], mesh.shape["fsdp"]
    paired = jax.sharding.Mesh(mesh.devices.reshape(count // 2, 2, members), ("pair", "core", "fsdp"))
    rows = P(None, ("pair", "core", "fsdp"), None)
    gain, weight = P("fsdp"), P("fsdp", None)
    return jax.shard_map(
        local,
        mesh=paired,
        in_specs=(rows, P(), P(), gain, weight, weight, weight, weight, gain, weight, weight, weight, rows),
        out_specs=(rows, rows, gain, weight, weight, weight, weight, gain, weight, weight, weight),
        check_vma=False,
    )
```
